32 devices in a mesh: dp: 16 (over z, x, core), chan: 2 (over y).
Axes of the slice: x: 2, y: 2, z: 4, core: 2. Of those that a mesh axis runs over, the one named last changes fastest.
Arguments:
- inputs: bfloat16 [16, 2048, 1152], P('dp', 'chan'), may hold values from -6 to 6
- weight: bfloat16 [2048, 9, 256], P('chan'), may hold values from -0.046875 to 0.046875
- cotangent: bfloat16 [16, 256, 1152], P('dp', 'chan'), may hold values from -6 to 6
Outputs:
- result: bfloat16 [16, 256, 1152], P('dp', 'chan')
- input_grad: bfloat16 [16, 2048, 1152], P('dp', 'chan')
- weight_grad: float32 [2048, 9, 256], P('chan')
The draws below stay inside these ranges and needn't reach their ends.
All inputs are finite; a program needn't handle non-finite values.
Results may differ from the reference program's by a relative error of at most 0.001.
Values may be sent and summed in bfloat16 or wider, within the bound.
No kernel may reach another device: no remote copies, remote signals or barrier semaphores. Data moves between devices by JAX's collectives and lax.ppermute only.
A program may use at most 64 MiB of HBM per device.

```python
import jax
import jax.numpy as jnp
from jax import lax

CIN = 2048
COUT = 256
DILATION_RATE = 12
KERNEL_TAPS = 9
MAP_HEIGHT = 16
MAP_WIDTH = 72
HW = 1152
BATCH = 16


def levels(own_key, shape, shards, low, largest):
    def one(dim, blocks):
        draws = jax.random.uniform(jax.random.fold_in(jax.random.fold_in(own_key, 6), dim), (blocks,), jnp.float32, low / len(shards), largest / len(shards))
        return jnp.repeat(jnp.exp(draws), shape[dim] // blocks).reshape((-1,) + (1,) * (len(shape) - dim - 1))

    gain = one(*shards[0])
    for cut in shards[1:]:
        gain = gain * one(*cut)
    return gain


def centred(stream_key, dims, scale, reach, pieces=(), dtype=jnp.bfloat16):
    entries = scale * jax.random.normal(stream_key, dims, jnp.float32)
    if pieces:
        entries = entries * levels(stream_key, dims, pieces, -0.22, 0.18)
    return jnp.clip(entries, -reach, reach).astype(dtype)


def setup_inputs(seed: int = 0) -> dict:
    key_list = jax.random.split(jax.random.key(seed), 4)
    inputs = centred(key_list[0], (BATCH, CIN, HW), 1.0, 6.0, ((0, 16), (1, 2)))
    weight = centred(key_list[1], (CIN, KERNEL_TAPS, COUT), (CIN * KERNEL_TAPS) ** -0.5, 0.046875, ((0, 2),))
    cotangent = centred(key_list[2], (BATCH, COUT, HW), 1.0, 6.0, ((0, 16), (1, 2)))
    return {"inputs": inputs, "weight": weight, "cotangent": cotangent}


def translated_input(receptive_field, row_shift, column_shift):
    bordered_input = jnp.pad(receptive_field, ((0, 0), (DILATION_RATE, DILATION_RATE), (DILATION_RATE, DILATION_RATE)))
    return bordered_input[:, DILATION_RATE + row_shift:DILATION_RATE + row_shift + MAP_HEIGHT, DILATION_RATE + column_shift:DILATION_RATE + column_shift + MAP_WIDTH]


def reference(inputs, weight, cotangent):
    tap_shifts = [(DILATION_RATE * (tap_index // 3 - 1), DILATION_RATE * (tap_index % 3 - 1)) for tap_index in range(KERNEL_TAPS)]

    def one_sample(carry, sample):
        feature_flat, grads_flat = sample
        feature_map = feature_flat.reshape(CIN, MAP_HEIGHT, MAP_WIDTH)
        grads = grads_flat.reshape(COUT, MAP_HEIGHT, MAP_WIDTH)
        out_sum = jnp.zeros((COUT, MAP_HEIGHT * MAP_WIDTH), jnp.float32)
        back_sum = jnp.zeros((CIN, MAP_HEIGHT * MAP_WIDTH), jnp.float32)
        tap_grads = []
        for tap_index in range(KERNEL_TAPS):
            row_shift, column_shift = tap_shifts[tap_index]
            displaced_input = translated_input(feature_map, row_shift, column_shift).reshape(CIN, MAP_HEIGHT * MAP_WIDTH)
            out_sum = out_sum + jnp.dot(weight[:, tap_index, :].T, displaced_input, preferred_element_type=jnp.float32)
            displaced_gradient = translated_input(grads, -row_shift, -column_shift).reshape(COUT, MAP_HEIGHT * MAP_WIDTH)
            back_sum = back_sum + jnp.dot(weight[:, tap_index, :], displaced_gradient, preferred_element_type=jnp.float32)
            tap_grads.append(jnp.dot(displaced_input, grads_flat.T, preferred_element_type=jnp.float32))
        carry = carry + jnp.stack(tap_grads, axis=1)
        return carry, (out_sum.astype(jnp.bfloat16), back_sum.astype(jnp.bfloat16))

    start = jnp.zeros((CIN, KERNEL_TAPS, COUT), jnp.float32)
    total, (outs, backs) = lax.scan(one_sample, start, (inputs, cotangent))
    return (outs, backs, total / jnp.float32(BATCH))
```

```python
import jax
import jax.numpy as jnp
from jax import lax
from jax.experimental import pallas as pl
from jax.experimental.pallas import tpu as pltpu
from jax.sharding import PartitionSpec as P

DILATION_RATE = 12
MAP_HEIGHT = 16
MAP_WIDTH = 72
HW = MAP_HEIGHT * MAP_WIDTH
REACH = (MAP_HEIGHT - DILATION_RATE) * MAP_WIDTH
WINDOW = 384
PAD = WINDOW - REACH
COLUMN_SHIFTS = (-DILATION_RATE, 0, DILATION_RATE)
VMEM_LIMIT = 48 * 1024 * 1024


def column_mask(start, width, shift):
    position = lax.broadcasted_iota(jnp.int32, (1, width), 1) + start
    column = lax.rem(position, MAP_WIDTH) + shift
    return position, (column >= 0) & (column < MAP_WIDTH)


def moved(values, amount):
    amount = amount % values.shape[1]
    return values if amount == 0 else pltpu.roll(values, amount, 1)


def moved_cotangent(cot, group, shift):
    if group == 1:
        _, inside = column_mask(0, HW, -shift)
        values = moved(cot, shift)
    elif group == 0:
        position, inside = column_mask(0, WINDOW, -shift)
        inside = inside & (position < REACH)
        values = moved(cot[:, HW - WINDOW :], shift - PAD)
    else:
        position, inside = column_mask(HW - WINDOW, WINDOW, -shift)
        inside = inside & (position >= HW - REACH)
        values = moved(cot[:, :WINDOW], PAD + shift)
    return jnp.where(inside, values, 0.0).astype(jnp.bfloat16)


def window(group):
    return (slice(0, WINDOW), slice(0, HW), slice(HW - WINDOW, HW))[group]


def kernel_grad_kernel(half_ref, own_x, other_x, own_cot, other_cot, out_ref):
    step = pl.program_id(0)
    for group in range(3):

        @pl.when(step == group)
        def _(group=group):
            where = window(group)
            for column, shift in enumerate(COLUMN_SHIFTS):
                total = None
                for x_ref, cot_ref in ((own_x, own_cot), (other_x, other_cot)):
                    cot = moved_cotangent(cot_ref[...].astype(jnp.float32), group, shift)
                    term = lax.dot_general(
                        x_ref[:, where],
                        cot,
                        (((1,), (1,)), ((), ())),
                        preferred_element_type=jnp.float32,
                    )
                    total = term if total is None else total + term
                out_ref[column] = total


def kernel_grad(half, x, other_x, own_cot, other_cot):
    rows, positions = other_x.shape
    outs = own_cot.shape[0]
    whole = lambda g, h: (0, 0)
    return pl.pallas_call(
        kernel_grad_kernel,
        out_shape=jax.ShapeDtypeStruct((9, rows, outs), jnp.float32),
        grid_spec=pltpu.PrefetchScalarGridSpec(
            num_scalar_prefetch=1,
            grid=(3,),
            in_specs=[
                pl.BlockSpec((rows, positions), lambda g, h: (h[0], 0)),
                pl.BlockSpec((rows, positions), whole),
                pl.BlockSpec((outs, positions), whole),
                pl.BlockSpec((outs, positions), whole),
            ],
            out_specs=pl.BlockSpec((3, rows, outs), lambda g, h: (g, 0, 0)),
        ),
        compiler_params=pltpu.CompilerParams(vmem_limit_bytes=VMEM_LIMIT),
        cost_estimate=pl.CostEstimate(
            flops=4 * rows * outs * 3 * (HW + 2 * WINDOW),
            bytes_accessed=4 * rows * positions + 4 * outs * positions + 36 * rows * outs,
            transcendentals=0,
        ),
        name="kernel_grad",
    )(half, x, other_x, own_cot, other_cot)


def forward_kernel(x_ref, w_ref, out_ref):
    step = pl.program_id(0)
    for group in range(3):

        @pl.when(step == group)
        def _(group=group):
            where = window(group)
            total = None
            for column, shift in enumerate(COLUMN_SHIFTS):
                term = lax.dot_general(
                    w_ref[column],
                    x_ref[:, where],
                    (((0,), (0,)), ((), ())),
                    preferred_element_type=jnp.float32,
                )
                if group == 1:
                    _, inside = column_mask(0, HW, shift)
                    term = moved(term, -shift)
                elif group == 0:
                    position, inside = column_mask(HW - WINDOW, WINDOW, shift)
                    inside = inside & (position >= HW - REACH)
                    term = moved(term, PAD - shift)
                else:
                    position, inside = column_mask(0, WINDOW, shift)
                    inside = inside & (position < REACH)
                    term = moved(term, -PAD - shift)
                term = jnp.where(inside, term, 0.0)
                total = term if total is None else total + term
            if group == 0:
                out_ref[:, : HW - WINDOW] = jnp.zeros((out_ref.shape[0], HW - WINDOW), jnp.float32)
                out_ref[:, HW - WINDOW :] = total
            elif group == 1:
                out_ref[...] += total
            else:
                out_ref[:, :WINDOW] += total


def forward(x, w):
    rows, positions = x.shape
    outs = w.shape[2]
    return pl.pallas_call(
        forward_kernel,
        out_shape=jax.ShapeDtypeStruct((outs, positions), jnp.float32),
        grid=(3,),
        in_specs=[
            pl.BlockSpec((rows, positions), lambda g: (0, 0)),
            pl.BlockSpec((3, rows, outs), lambda g: (g, 0, 0)),
        ],
        out_specs=pl.BlockSpec((outs, positions), lambda g: (0, 0)),
        compiler_params=pltpu.CompilerParams(vmem_limit_bytes=VMEM_LIMIT),
        cost_estimate=pl.CostEstimate(
            flops=2 * rows * outs * 3 * (HW + 2 * WINDOW),
            bytes_accessed=2 * rows * positions + 18 * rows * outs + 4 * outs * positions,
            transcendentals=0,
        ),
        name="forward",
    )(x, w)


def input_grad_kernel(cot_ref, w_ref, out_ref, middle, upper, lower):
    @pl.when(pl.program_id(0) == 0)
    def _():
        cot = cot_ref[...].astype(jnp.float32)
        for group, held in enumerate((upper, middle, lower)):
            for column, shift in enumerate(COLUMN_SHIFTS):
                held[column] = moved_cotangent(cot, group, shift)

    def products(group, held):
        total = None
        for column in range(3):
            term = jnp.dot(
                w_ref[3 * group + column], held[column], preferred_element_type=jnp.float32
            )
            total = term if total is None else total + term
        return total

    edge = HW - WINDOW
    centre = products(1, middle)
    out_ref[:, :WINDOW] = (centre[:, :WINDOW] + products(0, upper)).astype(jnp.bfloat16)
    out_ref[:, WINDOW:edge] = centre[:, WINDOW:edge].astype(jnp.bfloat16)
    out_ref[:, edge:] = (centre[:, edge:] + products(2, lower)).astype(jnp.bfloat16)


def input_gradient(cot, w):
    outs, positions = cot.shape
    rows = w.shape[1]
    block = min(rows, 256)
    return pl.pallas_call(
        input_grad_kernel,
        out_shape=jax.ShapeDtypeStruct((rows, positions), jnp.bfloat16),
        grid=(rows // block,),
        in_specs=[
            pl.BlockSpec((outs, positions), lambda g: (0, 0)),
            pl.BlockSpec((9, block, outs), lambda g: (0, g, 0)),
        ],
        out_specs=pl.BlockSpec((block, positions), lambda g: (g, 0)),
        scratch_shapes=[
            pltpu.VMEM((3, outs, HW), jnp.bfloat16),
            pltpu.VMEM((3, outs, WINDOW), jnp.bfloat16),
            pltpu.VMEM((3, outs, WINDOW), jnp.bfloat16),
        ],
        compiler_params=pltpu.CompilerParams(vmem_limit_bytes=VMEM_LIMIT),
        cost_estimate=pl.CostEstimate(
            flops=2 * rows * outs * 3 * (HW + 2 * WINDOW),
            bytes_accessed=2 * outs * positions + 18 * rows * outs + 2 * rows * positions,
            transcendentals=0,
        ),
        name="input_gradient",
    )(cot, w)


def on_device(inputs, weight, cotangent):
    x = inputs[0]
    own_cot = cotangent[0]
    w = jnp.transpose(weight, (1, 0, 2))
    taps, rows, outs = w.shape
    own_outs, positions = own_cot.shape
    samples = lax.axis_size("dp")
    chans = lax.axis_size("chan")
    depth = samples // 4
    place = lax.axis_index("dp")
    chan = lax.axis_index("chan")
    core, column, level = place % 2, (place // 2) % 2, place // 4
    core_rows = rows // 2
    chip_rows = core_rows // 2
    shard_rows = chip_rows // depth

    def to(value, target):
        return lax.ppermute(value, "dp", [(i, target(i)) for i in range(samples)])

    def to_core(value):
        return to(value, lambda i: i ^ 1)

    def to_column(value):
        return to(value, lambda i: i ^ 2)

    def to_level(value, step):
        return to(value, lambda i: ((i // 4 + step) % depth) * 4 + i % 4)

    other_x = to_core(lax.dynamic_slice_in_dim(x, (1 - core) * core_rows, core_rows, 0))
    if chans == 2:
        their_cot = lax.ppermute(own_cot, "chan", [(0, 1), (1, 0)])
        cot = jnp.where(
            chan == 0,
            jnp.concatenate([own_cot, their_cot], 0),
            jnp.concatenate([their_cot, own_cot], 0),
        )
    else:
        cot = lax.all_gather(own_cot, "chan", axis=0, tiled=True)
    other_cot = to_core(cot)

    largest = lax.pmax(
        jnp.stack([jnp.max(jnp.abs(x)), jnp.max(jnp.abs(own_cot))]).astype(jnp.float32),
        ("dp", "chan"),
    )
    bound = jnp.maximum(largest[0] * largest[1] * (positions * samples), 1e-30)
    scale = 30000.0 / bound
    unscale = bound * (1.0 / (30000.0 * samples))

    half = jnp.reshape(core, (1,)).astype(jnp.int32)
    partial = kernel_grad(half, x, other_x, cot, other_cot)

    def piece(row):
        return lax.dynamic_slice_in_dim(partial, row, shard_rows, 1) * scale

    summed = [None] * depth
    for step in list(range(1, depth)) + [0]:
        owner = (level + step) % depth
        sent = piece((1 - column) * chip_rows + owner * shard_rows).astype(jnp.float16)
        came = to_column(sent)
        summed[step] = piece(column * chip_rows + owner * shard_rows) + came.astype(jnp.float32)
    own = summed[0]
    for step in range(1, depth):
        own = own + to_level(summed[step].astype(jnp.float16), step).astype(jnp.float32)
    shard = own.astype(jnp.float16)

    pieces = []
    for step in range(depth):
        near = shard if step == 0 else to_level(shard, step)
        far = to_column(near)
        owner = (level - step) % depth
        for which, value in ((column, near), (1 - column, far)):
            row = which * chip_rows + owner * shard_rows
            pieces.append((core * core_rows + row, value))
            pieces.append(((1 - core) * core_rows + row, to_core(value)))
    grad = jnp.zeros((taps, rows, outs), jnp.float32)
    for row, value in pieces:
        grad = lax.dynamic_update_slice_in_dim(grad, value.astype(jnp.float32) * unscale, row, 1)
    weight_grad = jnp.transpose(grad, (1, 0, 2))

    total = forward(x, w)
    if chans == 2:
        mine = lax.dynamic_slice_in_dim(total, chan * own_outs, own_outs, 0)
        theirs = lax.dynamic_slice_in_dim(total, (1 - chan) * own_outs, own_outs, 0)
        result = mine + lax.ppermute(theirs, "chan", [(0, 1), (1, 0)])
    else:
        result = lax.psum_scatter(total, "chan", scatter_dimension=0, tiled=True)
    result = result.astype(jnp.bfloat16)[None]
    input_grad = input_gradient(cot, w)[None]
    return (result, input_grad, weight_grad)


def solution(mesh):
    placed = (P("dp", "chan", None), P("chan", None, None), P("dp", "chan", None))
    return jax.shard_map(
        on_device,
        mesh=mesh,
        in_specs=placed,
        out_specs=(P("dp", "chan", None), P("dp", "chan", None), P("chan", None, None)),
        check_vma=False,
    )
```

```python
import functools

import jax
import jax.numpy as jnp
from jax import lax
from jax.experimental import pallas as pl
from jax.experimental.pallas import tpu as pltpu
from jax.sharding import PartitionSpec as P

DILATION_RATE = 12
MAP_HEIGHT = 16
MAP_WIDTH = 72
HW = MAP_HEIGHT * MAP_WIDTH
REACH = (MAP_HEIGHT - DILATION_RATE) * MAP_WIDTH
WINDOW = 384
PAD = WINDOW - REACH
COLUMN_SHIFTS = (-DILATION_RATE, 0, DILATION_RATE)
VMEM_LIMIT = 48 * 1024 * 1024


def column_mask(start, width, shift):
    position = lax.broadcasted_iota(jnp.int32, (1, width), 1) + start
    column = lax.rem(position, MAP_WIDTH) + shift
    return position, (column >= 0) & (column < MAP_WIDTH)


def moved(values, amount):
    amount = amount % values.shape[1]
    return values if amount == 0 else pltpu.roll(values, amount, 1)


def moved_cotangent(cot, group, shift):
    if group == 1:
        _, inside = column_mask(0, HW, -shift)
        values = moved(cot, shift)
    elif group == 0:
        position, inside = column_mask(0, WINDOW, -shift)
        inside = inside & (position < REACH)
        values = moved(cot[:, HW - WINDOW :], shift - PAD)
    else:
        position, inside = column_mask(HW - WINDOW, WINDOW, -shift)
        inside = inside & (position >= HW - REACH)
        values = moved(cot[:, :WINDOW], PAD + shift)
    return jnp.where(inside, values, 0.0).astype(jnp.bfloat16)


def window(group):
    return (slice(0, WINDOW), slice(0, HW), slice(HW - WINDOW, HW))[group]


TILE = 8
LANES = 128
TOP = 30000.0


def kernel_grad_kernel(shards, place_ref, own_x, other_x, own_cot, other_cot, _, *refs):
    outs, sums, peak_ref = refs[:shards], refs[shards], refs[shards + 1]
    step = pl.program_id(0)
    rows, width = own_x.shape[0], own_cot.shape[0]
    shard_rows = rows // shards
    tiles = shard_rows // TILE

    @pl.when(step == 0)
    def _():
        peak_ref[...] = jnp.zeros(peak_ref.shape, jnp.float32)

    for group in range(3):

        @pl.when(step == group)
        def _(group=group):
            where = window(group)
            for column, shift in enumerate(COLUMN_SHIFTS):
                total = None
                for x_ref, cot_ref in ((own_x, own_cot), (other_x, other_cot)):
                    cot = moved_cotangent(cot_ref[...].astype(jnp.float32), group, shift)
                    term = lax.dot_general(
                        x_ref[:, where],
                        cot,
                        (((1,), (1,)), ((), ())),
                        preferred_element_type=jnp.float32,
                    )
                    total = term if total is None else total + term
                peak_ref[...] = jnp.maximum(
                    peak_ref[...], jnp.max(jnp.abs(total), axis=0, keepdims=True)
                )
                lanes = width // LANES
                for shard in range(shards):
                    for tile in range(tiles):
                        for lane in range(lanes):
                            row = shard * shard_rows + tile * TILE
                            slot = ((3 * group + column) * tiles + tile) * lanes + lane
                            sums[shard, slot] = total[
                                row : row + TILE, lane * LANES : (lane + 1) * LANES
                            ]

    @pl.when(step == 2)
    def _():
        peak = jnp.max(peak_ref[...], axis=1, keepdims=True)
        exponent = jnp.floor(jnp.log2(TOP / jnp.maximum(peak, 1e-30)))
        exponent = jnp.broadcast_to(exponent, (TILE, LANES))
        scale = jnp.exp2(exponent)
        for distance, out in enumerate(outs):
            count = sums.shape[1]
            out[:count] = sums[place_ref[1] ^ distance] * scale
            out[count] = exponent


def kernel_grad(place, shards, x, other_x, own_cot, other_cot, after):
    rows, positions = other_x.shape
    outs = own_cot.shape[0]
    tiles = 9 * rows * outs // (shards * TILE * LANES)
    whole = lambda g, h: (0, 0)
    return pl.pallas_call(
        functools.partial(kernel_grad_kernel, shards),
        out_shape=[jax.ShapeDtypeStruct((tiles + 1, TILE, LANES), jnp.float32)] * shards,
        grid_spec=pltpu.PrefetchScalarGridSpec(
            num_scalar_prefetch=1,
            grid=(3,),
            in_specs=[
                pl.BlockSpec((rows, positions), lambda g, h: (h[0], 0)),
                pl.BlockSpec((rows, positions), whole),
                pl.BlockSpec((outs, positions), whole),
                pl.BlockSpec((outs, positions), whole),
                pl.BlockSpec(memory_space=pl.ANY),
            ],
            out_specs=[pl.BlockSpec((tiles + 1, TILE, LANES), lambda g, h: (0, 0, 0))] * shards,
            scratch_shapes=[
                pltpu.VMEM((shards, tiles, TILE, LANES), jnp.float32),
                pltpu.VMEM((1, outs), jnp.float32),
            ],
        ),
        compiler_params=pltpu.CompilerParams(vmem_limit_bytes=VMEM_LIMIT),
        cost_estimate=pl.CostEstimate(
            flops=4 * rows * outs * 3 * (HW + 2 * WINDOW),
            bytes_accessed=4 * rows * positions + 4 * outs * positions + 36 * rows * outs,
            transcendentals=0,
        ),
        name="kernel_grad",
    )(place, x, other_x, own_cot, other_cot, after)


def forward_kernel(x_ref, w_ref, _, out_ref):
    step = pl.program_id(0)
    for group in range(3):

        @pl.when(step == group)
        def _(group=group):
            where = window(group)
            total = None
            for column, shift in enumerate(COLUMN_SHIFTS):
                term = lax.dot_general(
                    w_ref[column],
                    x_ref[:, where],
                    (((0,), (0,)), ((), ())),
                    preferred_element_type=jnp.float32,
                )
                if group == 1:
                    _, inside = column_mask(0, HW, shift)
                    term = moved(term, -shift)
                elif group == 0:
                    position, inside = column_mask(HW - WINDOW, WINDOW, shift)
                    inside = inside & (position >= HW - REACH)
                    term = moved(term, PAD - shift)
                else:
                    position, inside = column_mask(0, WINDOW, shift)
                    inside = inside & (position < REACH)
                    term = moved(term, -PAD - shift)
                term = jnp.where(inside, term, 0.0)
                total = term if total is None else total + term
            if group == 0:
                out_ref[:, : HW - WINDOW] = jnp.zeros((out_ref.shape[0], HW - WINDOW), jnp.float32)
                out_ref[:, HW - WINDOW :] = total
            elif group == 1:
                out_ref[...] += total
            else:
                out_ref[:, :WINDOW] += total


def forward(x, w, after):
    rows, positions = x.shape
    outs = w.shape[2]
    return pl.pallas_call(
        forward_kernel,
        out_shape=jax.ShapeDtypeStruct((outs, positions), jnp.float32),
        grid=(3,),
        in_specs=[
            pl.BlockSpec((rows, positions), lambda g: (0, 0)),
            pl.BlockSpec((3, rows, outs), lambda g: (g, 0, 0)),
            pl.BlockSpec(memory_space=pl.ANY),
        ],
        out_specs=pl.BlockSpec((outs, positions), lambda g: (0, 0)),
        compiler_params=pltpu.CompilerParams(vmem_limit_bytes=VMEM_LIMIT),
        cost_estimate=pl.CostEstimate(
            flops=2 * rows * outs * 3 * (HW + 2 * WINDOW),
            bytes_accessed=2 * rows * positions + 18 * rows * outs + 4 * outs * positions,
            transcendentals=0,
        ),
        name="forward",
    )(x, w, after)


def input_grad_kernel(cot_ref, w_ref, _, out_ref, middle, upper, lower):
    @pl.when(pl.program_id(0) == 0)
    def _():
        cot = cot_ref[...].astype(jnp.float32)
        for group, held in enumerate((upper, middle, lower)):
            for column, shift in enumerate(COLUMN_SHIFTS):
                held[column] = moved_cotangent(cot, group, shift)

    def products(group, held):
        total = None
        for column in range(3):
            term = jnp.dot(
                w_ref[3 * group + column], held[column], preferred_element_type=jnp.float32
            )
            total = term if total is None else total + term
        return total

    edge = HW - WINDOW
    centre = products(1, middle)
    out_ref[:, :WINDOW] = (centre[:, :WINDOW] + products(0, upper)).astype(jnp.bfloat16)
    out_ref[:, WINDOW:edge] = centre[:, WINDOW:edge].astype(jnp.bfloat16)
    out_ref[:, edge:] = (centre[:, edge:] + products(2, lower)).astype(jnp.bfloat16)


def input_gradient(cot, w, after):
    outs, positions = cot.shape
    rows = w.shape[1]
    block = min(rows, 256)
    return pl.pallas_call(
        input_grad_kernel,
        out_shape=jax.ShapeDtypeStruct((rows, positions), jnp.bfloat16),
        grid=(rows // block,),
        in_specs=[
            pl.BlockSpec((outs, positions), lambda g: (0, 0)),
            pl.BlockSpec((9, block, outs), lambda g: (0, g, 0)),
            pl.BlockSpec(memory_space=pl.ANY),
        ],
        out_specs=pl.BlockSpec((block, positions), lambda g: (g, 0)),
        scratch_shapes=[
            pltpu.VMEM((3, outs, HW), jnp.bfloat16),
            pltpu.VMEM((3, outs, WINDOW), jnp.bfloat16),
            pltpu.VMEM((3, outs, WINDOW), jnp.bfloat16),
        ],
        compiler_params=pltpu.CompilerParams(vmem_limit_bytes=VMEM_LIMIT),
        cost_estimate=pl.CostEstimate(
            flops=2 * rows * outs * 3 * (HW + 2 * WINDOW),
            bytes_accessed=2 * outs * positions + 18 * rows * outs + 2 * rows * positions,
            transcendentals=0,
        ),
        name="input_gradient",
    )(cot, w, after)


def summed(values):
    exponents = [value[-1:].astype(jnp.float32) for value in values]
    lowest = functools.reduce(jnp.minimum, exponents) - float((len(values) - 1).bit_length())
    total = sum(
        value.astype(jnp.float32) * jnp.exp2(lowest - exponent)
        for value, exponent in zip(values, exponents)
    )
    last = lax.broadcasted_iota(jnp.int32, total.shape, 0) == total.shape[0] - 1
    return jnp.where(last, jnp.broadcast_to(lowest, total.shape), total).astype(jnp.float16)


def token(value):
    return value[0].astype(jnp.float32)


def on_device(inputs, weight, cotangent):
    x = inputs[0]
    own_cot = cotangent[0]
    w = jnp.transpose(weight, (1, 0, 2))
    taps, rows, outs = w.shape
    own_outs, positions = own_cot.shape
    samples = lax.axis_size("dp")
    chans = lax.axis_size("chan")
    depth = samples // 4
    place = lax.axis_index("dp")
    chan = lax.axis_index("chan")
    core, column, level = place % 2, (place // 2) % 2, place // 4
    core_rows = rows // 2
    core_tiles = core_rows // TILE
    chip_tiles = core_tiles // 2
    shard_tiles = chip_tiles // depth

    def to(value, distance):
        return lax.ppermute(value, "dp", [(i, i ^ distance) for i in range(samples)])

    def to_core(value):
        return to(value, 1)

    def to_column(value):
        return to(value, 2)

    def to_level(value, step):
        return to(value, 4 * step)

    if chans == 2:
        their_cot = lax.ppermute(own_cot, "chan", [(0, 1), (1, 0)])
        cot = jnp.where(
            chan == 0,
            jnp.concatenate([own_cot, their_cot], 0),
            jnp.concatenate([their_cot, own_cot], 0),
        )
    else:
        cot = lax.all_gather(own_cot, "chan", axis=0, tiled=True)
    other_x = to_core(lax.dynamic_slice_in_dim(x, (1 - core) * core_rows, core_rows, 0))
    other_cot = to_core(cot)
    where = jnp.stack([core, column * depth + level]).astype(jnp.int32)

    shards = kernel_grad(where, 2 * depth, x, other_x, cot, other_cot, own_cot)
    near, far = shards[:depth], shards[depth:]

    total = forward(x, w, token(near[0]))

    order = list(range(depth - 1, -1, -1))
    kept = None
    line = []
    for step in order:
        came = to_column(far[step].astype(jnp.float16))
        pair = [near[step], came]
        if step:
            line.append(to_level(summed(pair), step))
        else:
            kept = summed(pair)
    shard = summed([kept] + line[::-1])
    input_grad = input_gradient(cot, w, token(line[0]))[None]

    grad = jnp.zeros((taps, rows // TILE, outs // LANES, TILE, LANES), jnp.float32)
    for step in range(depth):
        here = shard if step == 0 else to_level(shard, step)
        there = to_column(here)
        owner = level ^ step
        for chip, value in ((column, here), (1 - column, there)):
            row = chip * chip_tiles + owner * shard_tiles
            for base, part in ((core, value), (1 - core, to_core(value))):
                factor = jnp.exp2(-part[-1].astype(jnp.float32)) * (1.0 / samples)
                part = part[:-1].reshape(taps, shard_tiles, outs // LANES, TILE, LANES)
                part = part.astype(jnp.float32) * factor
                grad = lax.dynamic_update_slice_in_dim(grad, part, base * core_tiles + row, 1)
    weight_grad = jnp.transpose(grad, (1, 3, 0, 2, 4)).reshape(rows, taps, outs)

    if chans == 2:
        mine = lax.dynamic_slice_in_dim(total, chan * own_outs, own_outs, 0)
        theirs = lax.dynamic_slice_in_dim(total, (1 - chan) * own_outs, own_outs, 0)
        result = mine + lax.ppermute(theirs, "chan", [(0, 1), (1, 0)])
    else:
        result = lax.psum_scatter(total, "chan", scatter_dimension=0, tiled=True)
    result = result.astype(jnp.bfloat16)[None]
    return (result, input_grad, weight_grad)


def solution(mesh):
    placed = (P("dp", "chan", None), P("chan", None, None), P("dp", "chan", None))
    return jax.shard_map(
        on_device,
        mesh=mesh,
        in_specs=placed,
        out_specs=(P("dp", "chan", None), P("dp", "chan", None), P("chan", None, None)),
        check_vma=False,
    )
```

```python
import functools

import jax
import jax.numpy as jnp
from jax import lax
from jax.experimental import pallas as pl
from jax.experimental.pallas import tpu as pltpu
from jax.sharding import PartitionSpec as P

DILATION_RATE = 12
MAP_HEIGHT = 16
MAP_WIDTH = 72
HW = MAP_HEIGHT * MAP_WIDTH
REACH = (MAP_HEIGHT - DILATION_RATE) * MAP_WIDTH
WINDOW = 384
PAD = WINDOW - REACH
COLUMN_SHIFTS = (-DILATION_RATE, 0, DILATION_RATE)
VMEM_LIMIT = 24 * 1024 * 1024


def column_mask(start, width, shift):
    position = lax.broadcasted_iota(jnp.int32, (1, width), 1) + start
    column = lax.rem(position, MAP_WIDTH) + shift
    return position, (column >= 0) & (column < MAP_WIDTH)


def moved(values, amount):
    amount = amount % values.shape[1]
    return values if amount == 0 else pltpu.roll(values, amount, 1)


def moved_cotangent(cot, group, shift):
    if group == 1:
        _, inside = column_mask(0, HW, -shift)
        values = moved(cot, shift)
    elif group == 0:
        position, inside = column_mask(0, WINDOW, -shift)
        inside = inside & (position < REACH)
        values = moved(cot[:, HW - WINDOW :], shift - PAD)
    else:
        position, inside = column_mask(HW - WINDOW, WINDOW, -shift)
        inside = inside & (position >= HW - REACH)
        values = moved(cot[:, :WINDOW], PAD + shift)
    return jnp.where(inside, values, 0.0).astype(jnp.bfloat16)


def window(group):
    return (slice(0, WINDOW), slice(0, HW), slice(HW - WINDOW, HW))[group]


TILE = 8
LANES = 128
TOP = 30000.0


def kernel_grad_kernel(shards, place_ref, own_x, other_x, own_cot, other_cot, _, *refs):
    outs, sums, peak_ref = refs[:shards], refs[shards], refs[shards + 1]
    step = pl.program_id(0)
    rows, width = own_x.shape[0], own_cot.shape[0]
    shard_rows = rows // shards
    tiles = shard_rows // TILE

    @pl.when(step == 0)
    def _():
        peak_ref[...] = jnp.zeros(peak_ref.shape, jnp.float32)

    for group in range(3):

        @pl.when(step == group)
        def _(group=group):
            where = window(group)
            for column, shift in enumerate(COLUMN_SHIFTS):
                total = None
                for x_ref, cot_ref in ((own_x, own_cot), (other_x, other_cot)):
                    cot = moved_cotangent(cot_ref[...].astype(jnp.float32), group, shift)
                    term = lax.dot_general(
                        x_ref[:, where],
                        cot,
                        (((1,), (1,)), ((), ())),
                        preferred_element_type=jnp.float32,
                    )
                    total = term if total is None else total + term
                peak_ref[...] = jnp.maximum(
                    peak_ref[...], jnp.max(jnp.abs(total), axis=0, keepdims=True)
                )
                lanes = width // LANES
                for shard in range(shards):
                    for tile in range(tiles):
                        for lane in range(lanes):
                            row = shard * shard_rows + tile * TILE
                            slot = ((3 * group + column) * tiles + tile) * lanes + lane
                            sums[shard, slot] = total[
                                row : row + TILE, lane * LANES : (lane + 1) * LANES
                            ]

    @pl.when(step == 2)
    def _():
        peak = jnp.max(peak_ref[...], axis=1, keepdims=True)
        exponent = jnp.floor(jnp.log2(TOP / jnp.maximum(peak, 1e-30)))
        exponent = jnp.broadcast_to(exponent, (TILE, LANES))
        scale = jnp.exp2(exponent)
        for distance, out in enumerate(outs):
            count = sums.shape[1]
            out[:count] = sums[place_ref[1] ^ distance] * scale
            out[count] = exponent


def kernel_grad(place, shards, x, other_x, own_cot, other_cot, after):
    rows, positions = other_x.shape
    outs = own_cot.shape[0]
    tiles = 9 * rows * outs // (shards * TILE * LANES)
    whole = lambda g, h: (0, 0)
    return pl.pallas_call(
        functools.partial(kernel_grad_kernel, shards),
        out_shape=[jax.ShapeDtypeStruct((tiles + 1, TILE, LANES), jnp.float32)] * shards,
        grid_spec=pltpu.PrefetchScalarGridSpec(
            num_scalar_prefetch=1,
            grid=(3,),
            in_specs=[
                pl.BlockSpec((rows, positions), lambda g, h: (h[0], 0)),
                pl.BlockSpec((rows, positions), whole),
                pl.BlockSpec((outs, positions), whole),
                pl.BlockSpec((outs, positions), whole),
                pl.BlockSpec(memory_space=pl.ANY),
            ],
            out_specs=[pl.BlockSpec((tiles + 1, TILE, LANES), lambda g, h: (0, 0, 0))] * shards,
            scratch_shapes=[
                pltpu.VMEM((shards, tiles, TILE, LANES), jnp.float32),
                pltpu.VMEM((1, outs), jnp.float32),
            ],
        ),
        compiler_params=pltpu.CompilerParams(vmem_limit_bytes=VMEM_LIMIT),
        cost_estimate=pl.CostEstimate(
            flops=4 * rows * outs * 3 * (HW + 2 * WINDOW),
            bytes_accessed=4 * rows * positions + 4 * outs * positions + 36 * rows * outs,
            transcendentals=0,
        ),
        name="kernel_grad",
    )(place, x, other_x, own_cot, other_cot, after)


def forward_kernel(x_ref, w_ref, _, out_ref):
    step = pl.program_id(0)
    for group in range(3):

        @pl.when(step == group)
        def _(group=group):
            where = window(group)
            total = None
            for column, shift in enumerate(COLUMN_SHIFTS):
                term = lax.dot_general(
                    w_ref[column],
                    x_ref[:, where],
                    (((0,), (0,)), ((), ())),
                    preferred_element_type=jnp.float32,
                )
                if group == 1:
                    _, inside = column_mask(0, HW, shift)
                    term = moved(term, -shift)
                elif group == 0:
                    position, inside = column_mask(HW - WINDOW, WINDOW, shift)
                    inside = inside & (position >= HW - REACH)
                    term = moved(term, PAD - shift)
                else:
                    position, inside = column_mask(0, WINDOW, shift)
                    inside = inside & (position < REACH)
                    term = moved(term, -PAD - shift)
                term = jnp.where(inside, term, 0.0)
                total = term if total is None else total + term
            if group == 0:
                out_ref[:, : HW - WINDOW] = jnp.zeros((out_ref.shape[0], HW - WINDOW), jnp.float32)
                out_ref[:, HW - WINDOW :] = total
            elif group == 1:
                out_ref[...] += total
            else:
                out_ref[:, :WINDOW] += total


def forward(x, w, after):
    rows, positions = x.shape
    outs = w.shape[2]
    return pl.pallas_call(
        forward_kernel,
        out_shape=jax.ShapeDtypeStruct((outs, positions), jnp.float32),
        grid=(3,),
        in_specs=[
            pl.BlockSpec((rows, positions), lambda g: (0, 0)),
            pl.BlockSpec((3, rows, outs), lambda g: (g, 0, 0)),
            pl.BlockSpec(memory_space=pl.ANY),
        ],
        out_specs=pl.BlockSpec((outs, positions), lambda g: (0, 0)),
        compiler_params=pltpu.CompilerParams(vmem_limit_bytes=VMEM_LIMIT),
        cost_estimate=pl.CostEstimate(
            flops=2 * rows * outs * 3 * (HW + 2 * WINDOW),
            bytes_accessed=2 * rows * positions + 18 * rows * outs + 4 * outs * positions,
            transcendentals=0,
        ),
        name="forward",
    )(x, w, after)


def input_grad_kernel(cot_ref, w_ref, _, out_ref, middle, upper, lower):
    @pl.when(pl.program_id(0) == 0)
    def _():
        cot = cot_ref[...].astype(jnp.float32)
        for group, held in enumerate((upper, middle, lower)):
            for column, shift in enumerate(COLUMN_SHIFTS):
                held[column] = moved_cotangent(cot, group, shift)

    def products(group, held):
        total = None
        for column in range(3):
            term = jnp.dot(
                w_ref[3 * group + column], held[column], preferred_element_type=jnp.float32
            )
            total = term if total is None else total + term
        return total

    edge = HW - WINDOW
    centre = products(1, middle)
    out_ref[:, :WINDOW] = (centre[:, :WINDOW] + products(0, upper)).astype(jnp.bfloat16)
    out_ref[:, WINDOW:edge] = centre[:, WINDOW:edge].astype(jnp.bfloat16)
    out_ref[:, edge:] = (centre[:, edge:] + products(2, lower)).astype(jnp.bfloat16)


def input_gradient(cot, w, after):
    outs, positions = cot.shape
    rows = w.shape[1]
    block = min(rows, 256)
    return pl.pallas_call(
        input_grad_kernel,
        out_shape=jax.ShapeDtypeStruct((rows, positions), jnp.bfloat16),
        grid=(rows // block,),
        in_specs=[
            pl.BlockSpec((outs, positions), lambda g: (0, 0)),
            pl.BlockSpec((9, block, outs), lambda g: (0, g, 0)),
            pl.BlockSpec(memory_space=pl.ANY),
        ],
        out_specs=pl.BlockSpec((block, positions), lambda g: (g, 0)),
        scratch_shapes=[
            pltpu.VMEM((3, outs, HW), jnp.bfloat16),
            pltpu.VMEM((3, outs, WINDOW), jnp.bfloat16),
            pltpu.VMEM((3, outs, WINDOW), jnp.bfloat16),
        ],
        compiler_params=pltpu.CompilerParams(vmem_limit_bytes=VMEM_LIMIT),
        cost_estimate=pl.CostEstimate(
            flops=2 * rows * outs * 3 * (HW + 2 * WINDOW),
            bytes_accessed=2 * outs * positions + 18 * rows * outs + 2 * rows * positions,
            transcendentals=0,
        ),
        name="input_gradient",
    )(cot, w, after)


def common_exponent(values, bits):
    lowest = functools.reduce(
        jnp.minimum, [value[-1:].astype(jnp.float32) + bit for value, bit in values]
    )
    return lowest - bits


def scaled_sum(values, lowest):
    return sum(
        value.astype(jnp.float32) * jnp.exp2(lowest - value[-1:].astype(jnp.float32))
        for value, _ in values
    )


def summed(values, bits, key):
    lowest = common_exponent(values, bits)
    total = scaled_sum(values, lowest)
    tile = lax.broadcasted_iota(jnp.int32, total.shape, 0)
    marked = tile * key >= (total.shape[0] - 1) * key
    return jnp.where(marked, jnp.broadcast_to(lowest, total.shape), total).astype(jnp.float16)


def token(value):
    return value[0].astype(jnp.float32)


def on_device(inputs, weight, cotangent):
    x = inputs[0]
    own_cot = cotangent[0]
    w = jnp.transpose(weight, (1, 0, 2))
    taps, rows, outs = w.shape
    own_outs, positions = own_cot.shape
    samples = lax.axis_size("dp")
    chans = lax.axis_size("chan")
    depth = samples // 4
    place = lax.axis_index("dp")
    chan = lax.axis_index("chan")
    core, column, level = place % 2, (place // 2) % 2, place // 4
    core_rows = rows // 2
    core_tiles = core_rows // TILE
    chip_tiles = core_tiles // 2
    shard_tiles = chip_tiles // depth

    def to(value, distance):
        return lax.ppermute(value, "dp", [(i, i ^ distance) for i in range(samples)])

    def to_core(value):
        return to(value, 1)

    def to_column(value):
        return to(value, 2)

    def to_level(value, step):
        return to(value, 4 * step)

    if chans == 2:
        their_cot = lax.ppermute(own_cot, "chan", [(0, 1), (1, 0)])
        parts = (own_cot, their_cot)
        first = chan
    else:
        cot = lax.all_gather(own_cot, "chan", axis=0, tiled=True)
        parts = (cot[:LANES], cot[LANES:])
        first = 0
    other_cots = [to_core(part) for part in parts]
    other_x = to_core(lax.dynamic_slice_in_dim(x, (1 - core) * core_rows, core_rows, 0))
    where = jnp.stack([core, column * depth + level]).astype(jnp.int32)
    halves, exponents = [], []
    after = own_cot
    for side, (part, other) in enumerate(zip(parts, other_cots)):
        shards = kernel_grad(where, 2 * depth, x, other_x, part, other, after)
        held = [None] * depth
        for step in range(depth - 1, -1, -1):
            sent = shards[depth + step].astype(jnp.float16)
            held[step] = [(shards[step], 0.0), (to_column(sent), 0.0)]
        bits = 1.0
        for bit in [1 << shift for shift in range(depth.bit_length() - 1)]:
            for step in range(depth - bit, 0, -2 * bit):
                pair = summed(held[step], bits, 2 * step + side)
                held[step ^ bit].append((to_level(pair, bit), bits))
                after = token(pair) if step == depth - 1 else after
            bits += 1.0
        lowest = common_exponent(held[0], bits)
        halves.append(scaled_sum([(v, b) for v, b in held[0]], lowest)[:-1].astype(jnp.float16))
        exponents.append(lowest)
    halves = [jnp.where(first == side, halves[0], halves[1]) for side in range(2)]
    exponents = [jnp.where(first == side, exponents[0], exponents[1]) for side in range(2)]
    halves = [half.reshape(taps, shard_tiles, TILE, LANES) for half in halves]
    shard = jnp.stack(halves, 2)
    exponent = jnp.concatenate(exponents, 0)

    grad = jnp.zeros((taps, rows // TILE, 2, TILE, LANES), jnp.float16)
    near = [shard]
    for step in range(1, depth):
        low = step & -step
        near.append(to_level(near[step ^ low], low))
    far = [to_column(value) for value in near]
    for chip, values, group in ((column, near, depth), (1 - column, far, 2)):
        for start in range(0, depth, group):
            across = to_core(jnp.stack(values[start : start + group]))
            for step in range(start, start + group):
                row = chip * chip_tiles + (level ^ step) * shard_tiles
                for base, part in ((core, values[step]), (1 - core, across[step - start])):
                    grad = lax.dynamic_update_slice_in_dim(grad, part, base * core_tiles + row, 1)
    other = to_core(exponent + 0.0 * token(near[-1][0, 0])[0])
    by_core = [jnp.where(core == side, exponent, other) for side in range(2)]
    factor = jnp.exp2(-jnp.stack(by_core)) * (1.0 / samples)
    grad = grad.reshape(taps, 2, core_tiles, 2, TILE, LANES).astype(jnp.float32)
    grad = (grad * factor[None, :, None]).reshape(taps, rows // TILE, 2, TILE, LANES)
    weight_grad = jnp.transpose(grad, (1, 3, 0, 2, 4)).reshape(rows, taps, outs)

    total = forward(x, w, token(shard[0, 0]))
    if chans == 2:
        mine = lax.dynamic_slice_in_dim(total, chan * own_outs, own_outs, 0)
        theirs = lax.dynamic_slice_in_dim(total, (1 - chan) * own_outs, own_outs, 0)
        result = mine + lax.ppermute(theirs, "chan", [(0, 1), (1, 0)])
        cot = jnp.where(
            chan == 0,
            jnp.concatenate([own_cot, their_cot], 0),
            jnp.concatenate([their_cot, own_cot], 0),
        )
    else:
        result = lax.psum_scatter(total, "chan", scatter_dimension=0, tiled=True)
    result = result.astype(jnp.bfloat16)[None]
    input_grad = input_gradient(cot, w, token(near[depth // 2][0, 0]))[None]
    return (result, input_grad, weight_grad)


def solution(mesh):
    placed = (P("dp", "chan", None), P("chan", None, None), P("dp", "chan", None))
    return jax.shard_map(
        on_device,
        mesh=mesh,
        in_specs=placed,
        out_specs=(P("dp", "chan", None), P("dp", "chan", None), P("chan", None, None)),
        check_vma=False,
    )
```

```python
import functools

import jax
import jax.numpy as jnp
from jax import lax
from jax.experimental import pallas as pl
from jax.experimental.pallas import tpu as pltpu
from jax.sharding import PartitionSpec as P

DILATION_RATE = 12
MAP_HEIGHT = 16
MAP_WIDTH = 72
HW = MAP_HEIGHT * MAP_WIDTH
REACH = (MAP_HEIGHT - DILATION_RATE) * MAP_WIDTH
WINDOW = 384
PAD = WINDOW - REACH
COLUMN_SHIFTS = (-DILATION_RATE, 0, DILATION_RATE)
VMEM_LIMIT = 16 * 1024 * 1024


def column_mask(start, width, shift):
    position = lax.broadcasted_iota(jnp.int32, (1, width), 1) + start
    column = lax.rem(position, MAP_WIDTH) + shift
    return position, (column >= 0) & (column < MAP_WIDTH)


def moved(values, amount):
    amount = amount % values.shape[1]
    return values if amount == 0 else pltpu.roll(values, amount, 1)


def moved_cotangent(cot, group, shift):
    if group == 1:
        _, inside = column_mask(0, HW, -shift)
        values = moved(cot, shift)
    elif group == 0:
        position, inside = column_mask(0, WINDOW, -shift)
        inside = inside & (position < REACH)
        values = moved(cot[:, HW - WINDOW :], shift - PAD)
    else:
        position, inside = column_mask(HW - WINDOW, WINDOW, -shift)
        inside = inside & (position >= HW - REACH)
        values = moved(cot[:, :WINDOW], PAD + shift)
    return jnp.where(inside, values, 0.0).astype(jnp.bfloat16)


def window(group):
    return (slice(0, WINDOW), slice(0, HW), slice(HW - WINDOW, HW))[group]


TILE = 8
LANES = 128
TOP = 30000.0


def kernel_grad_kernel(depth, place_ref, own_x, other_x, own_cot, other_cot, _, *refs):
    near, far = refs[:depth], refs[depth : depth + 2]
    sums, peak_ref = refs[depth + 2 :]
    step = pl.program_id(0)
    rows, width = own_x.shape[0], own_cot.shape[0]
    shards = 2 * depth
    shard_rows = rows // shards
    tiles = shard_rows // TILE
    lanes = width // LANES

    @pl.when(step == 0)
    def _():
        peak_ref[...] = jnp.zeros(peak_ref.shape, jnp.float32)

    for group in range(3):

        @pl.when(step == group)
        def _(group=group):
            where = window(group)
            total = None
            for x_ref, cot_ref in ((own_x, own_cot), (other_x, other_cot)):
                cot = cot_ref[...].astype(jnp.float32)
                cots = [moved_cotangent(cot, group, shift) for shift in COLUMN_SHIFTS]
                term = lax.dot_general(
                    x_ref[:, where],
                    jnp.concatenate(cots, 0),
                    (((1,), (1,)), ((), ())),
                    preferred_element_type=jnp.float32,
                )
                total = term if total is None else total + term
            peak_ref[...] = jnp.maximum(
                peak_ref[...], jnp.max(jnp.abs(total), axis=0, keepdims=True)
            )
            for column in range(3):
                for shard in range(shards):
                    for tile in range(tiles):
                        for lane in range(lanes):
                            row = shard * shard_rows + tile * TILE
                            first = column * width + lane * LANES
                            slot = ((3 * group + column) * tiles + tile) * lanes + lane
                            sums[shard, slot] = total[row : row + TILE, first : first + LANES]

    @pl.when(step == 2)
    def _():
        peak = jnp.max(peak_ref[...], axis=1, keepdims=True)
        exponent = jnp.floor(jnp.log2(TOP / jnp.maximum(peak, 1e-30)))
        exponent = jnp.broadcast_to(exponent, (TILE, LANES))
        scale = jnp.exp2(exponent)
        count = sums.shape[1]
        for distance in range(shards):
            if distance < depth:
                out = near[distance]
            else:
                message, slot = divmod(distance - depth, depth // 2)
                out = far[message].at[slot]
            out[:count] = sums[place_ref[1] ^ distance] * scale
            out[count] = exponent


def kernel_grad(place, depth, x, other_x, own_cot, other_cot, after):
    rows, positions = other_x.shape
    outs = own_cot.shape[0]
    tiles = 9 * rows * outs // (2 * depth * TILE * LANES)
    whole = lambda g, h: (0, 0)
    once = pl.Buffered(1)
    shapes = [(tiles + 1, TILE, LANES)] * depth + [(depth // 2, tiles + 1, TILE, LANES)] * 2
    return pl.pallas_call(
        functools.partial(kernel_grad_kernel, depth),
        out_shape=[jax.ShapeDtypeStruct(shape, jnp.float32) for shape in shapes],
        grid_spec=pltpu.PrefetchScalarGridSpec(
            num_scalar_prefetch=1,
            grid=(3,),
            in_specs=[
                pl.BlockSpec((rows, positions), lambda g, h: (h[0], 0), pipeline_mode=once),
                pl.BlockSpec((rows, positions), whole, pipeline_mode=once),
                pl.BlockSpec((outs, positions), whole, pipeline_mode=once),
                pl.BlockSpec((outs, positions), whole, pipeline_mode=once),
                pl.BlockSpec(memory_space=pl.ANY),
            ],
            out_specs=[
                pl.BlockSpec(shape, functools.partial(lambda n, g, h: (0,) * n, len(shape)))
                for shape in shapes
            ],
            scratch_shapes=[
                pltpu.VMEM((2 * depth, tiles, TILE, LANES), jnp.float32),
                pltpu.VMEM((1, 3 * outs), jnp.float32),
            ],
        ),
        compiler_params=pltpu.CompilerParams(vmem_limit_bytes=VMEM_LIMIT),
        cost_estimate=pl.CostEstimate(
            flops=4 * rows * outs * 3 * (HW + 2 * WINDOW),
            bytes_accessed=4 * rows * positions + 4 * outs * positions + 36 * rows * outs,
            transcendentals=0,
        ),
        name="kernel_grad",
    )(place, x, other_x, own_cot, other_cot, after)


def forward_kernel(x_ref, w_ref, _, out_ref):
    step = pl.program_id(0)
    for group in range(3):

        @pl.when(step == group)
        def _(group=group):
            where = window(group)
            total = None
            for column, shift in enumerate(COLUMN_SHIFTS):
                term = lax.dot_general(
                    w_ref[column],
                    x_ref[:, where],
                    (((0,), (0,)), ((), ())),
                    preferred_element_type=jnp.float32,
                )
                if group == 1:
                    _, inside = column_mask(0, HW, shift)
                    term = moved(term, -shift)
                elif group == 0:
                    position, inside = column_mask(HW - WINDOW, WINDOW, shift)
                    inside = inside & (position >= HW - REACH)
                    term = moved(term, PAD - shift)
                else:
                    position, inside = column_mask(0, WINDOW, shift)
                    inside = inside & (position < REACH)
                    term = moved(term, -PAD - shift)
                term = jnp.where(inside, term, 0.0)
                total = term if total is None else total + term
            if group == 0:
                out_ref[:, : HW - WINDOW] = jnp.zeros((out_ref.shape[0], HW - WINDOW), jnp.float32)
                out_ref[:, HW - WINDOW :] = total
            elif group == 1:
                out_ref[...] += total
            else:
                out_ref[:, :WINDOW] += total


def forward(x, w, after):
    rows, positions = x.shape
    outs = w.shape[2]
    return pl.pallas_call(
        forward_kernel,
        out_shape=jax.ShapeDtypeStruct((outs, positions), jnp.float32),
        grid=(3,),
        in_specs=[
            pl.BlockSpec((rows, positions), lambda g: (0, 0), pipeline_mode=pl.Buffered(1)),
            pl.BlockSpec((3, rows, outs), lambda g: (g, 0, 0)),
            pl.BlockSpec(memory_space=pl.ANY),
        ],
        out_specs=pl.BlockSpec((outs, positions), lambda g: (0, 0)),
        compiler_params=pltpu.CompilerParams(vmem_limit_bytes=VMEM_LIMIT),
        cost_estimate=pl.CostEstimate(
            flops=2 * rows * outs * 3 * (HW + 2 * WINDOW),
            bytes_accessed=2 * rows * positions + 18 * rows * outs + 4 * outs * positions,
            transcendentals=0,
        ),
        name="forward",
    )(x, w, after)


def input_grad_kernel(cot_ref, w_ref, _, out_ref, middle, upper, lower):
    @pl.when(pl.program_id(0) == 0)
    def _():
        cot = cot_ref[...].astype(jnp.float32)
        for group, held in enumerate((upper, middle, lower)):
            for column, shift in enumerate(COLUMN_SHIFTS):
                held[column] = moved_cotangent(cot, group, shift)

    def products(group, held):
        total = None
        for column in range(3):
            term = jnp.dot(
                w_ref[3 * group + column], held[column], preferred_element_type=jnp.float32
            )
            total = term if total is None else total + term
        return total

    edge = HW - WINDOW
    centre = products(1, middle)
    out_ref[:, :WINDOW] = (centre[:, :WINDOW] + products(0, upper)).astype(jnp.bfloat16)
    out_ref[:, WINDOW:edge] = centre[:, WINDOW:edge].astype(jnp.bfloat16)
    out_ref[:, edge:] = (centre[:, edge:] + products(2, lower)).astype(jnp.bfloat16)


def input_gradient(cot, w, after):
    outs, positions = cot.shape
    rows = w.shape[1]
    block = min(rows, 256)
    return pl.pallas_call(
        input_grad_kernel,
        out_shape=jax.ShapeDtypeStruct((rows, positions), jnp.bfloat16),
        grid=(rows // block,),
        in_specs=[
            pl.BlockSpec((outs, positions), lambda g: (0, 0)),
            pl.BlockSpec((9, block, outs), lambda g: (0, g, 0)),
            pl.BlockSpec(memory_space=pl.ANY),
        ],
        out_specs=pl.BlockSpec((block, positions), lambda g: (g, 0)),
        scratch_shapes=[
            pltpu.VMEM((3, outs, HW), jnp.bfloat16),
            pltpu.VMEM((3, outs, WINDOW), jnp.bfloat16),
            pltpu.VMEM((3, outs, WINDOW), jnp.bfloat16),
        ],
        compiler_params=pltpu.CompilerParams(vmem_limit_bytes=VMEM_LIMIT),
        cost_estimate=pl.CostEstimate(
            flops=2 * rows * outs * 3 * (HW + 2 * WINDOW),
            bytes_accessed=2 * outs * positions + 18 * rows * outs + 2 * rows * positions,
            transcendentals=0,
        ),
        name="input_gradient",
    )(cot, w, after)


def common_exponent(values, bits):
    lowest = functools.reduce(
        jnp.minimum, [value[-1:].astype(jnp.float32) + bit for value, bit in values]
    )
    return lowest - bits


def scaled_sum(values, lowest):
    return sum(
        value.astype(jnp.float32) * jnp.exp2(lowest - value[-1:].astype(jnp.float32))
        for value, _ in values
    )


def summed(values, bits):
    lowest = common_exponent(values, bits)
    total = scaled_sum(values, lowest).astype(jnp.float16)
    return lax.dynamic_update_slice(
        total, lowest.astype(jnp.float16), (total.shape[0] - 1, 0, 0)
    )


def token(value):
    return value[0].astype(jnp.float32)


def on_device(inputs, weight, cotangent):
    x = inputs[0]
    own_cot = cotangent[0]
    w = jnp.transpose(weight, (1, 0, 2))
    taps, rows, outs = w.shape
    own_outs, positions = own_cot.shape
    samples = lax.axis_size("dp")
    chans = lax.axis_size("chan")
    depth = samples // 4
    place = lax.axis_index("dp")
    chan = lax.axis_index("chan")
    core, column, level = place % 2, (place // 2) % 2, place // 4
    core_rows = rows // 2
    core_tiles = core_rows // TILE
    chip_tiles = core_tiles // 2
    shard_tiles = chip_tiles // depth

    def to(value, distance):
        return lax.ppermute(value, "dp", [(i, i ^ distance) for i in range(samples)])

    def to_core(value):
        return to(value, 1)

    def to_column(value):
        return to(value, 2)

    def to_level(value, step):
        return to(value, 4 * step)

    if chans == 2:
        their_cot = lax.ppermute(own_cot, "chan", [(0, 1), (1, 0)])
        parts = (own_cot, their_cot)
        first = chan
    else:
        cot = lax.all_gather(own_cot, "chan", axis=0, tiled=True)
        parts = (cot[:LANES], cot[LANES:])
        first = 0
    other_x = to_core(lax.dynamic_slice_in_dim(x, (1 - core) * core_rows, core_rows, 0))
    where = jnp.stack([core, column * depth + level]).astype(jnp.int32)
    halves, exponents = [], []
    after = own_cot
    for side in range(2):
        part = parts[side]
        if side == 1:
            part = jnp.where(shards[0][-1, 0, 0] > -1e30, part, jnp.zeros_like(part))
            their_cot = part
        shards = kernel_grad(where, depth, x, other_x, part, to_core(part), after)
        held = [None] * depth
        for message in (1, 0):
            sent = shards[depth + message].astype(jnp.float16)
            came = to_column(sent)
            for slot in range(depth // 2 - 1, -1, -1):
                step = message * (depth // 2) + slot
                held[step] = [(shards[step], 0.0), (came[slot], 0.0)]
        after = sent[0, 0].astype(jnp.float32)
        bits = 1.0
        for bit in [1 << shift for shift in range(depth.bit_length() - 1)]:
            for step in range(depth - bit, 0, -2 * bit):
                held[step ^ bit].append((to_level(summed(held[step], bits), bit), bits))
            bits += 1.0
        lowest = common_exponent(held[0], bits)
        halves.append(scaled_sum(held[0], lowest)[:-1].astype(jnp.float16))
        exponents.append(lowest)
    halves = [jnp.where(first == side, halves[0], halves[1]) for side in range(2)]
    exponents = [jnp.where(first == side, exponents[0], exponents[1]) for side in range(2)]
    halves = [half.reshape(taps, shard_tiles, TILE, LANES) for half in halves]
    shard = jnp.stack(halves, 2)
    exponent = jnp.concatenate(exponents, 0)

    grad = jnp.zeros((taps, rows // TILE, 2, TILE, LANES), jnp.float16)
    near = [shard]
    for step in range(1, depth):
        low = step & -step
        near.append(to_level(near[step ^ low], low))
    far = [to_column(value) for value in near]
    for chip, values, group in ((column, near, depth), (1 - column, far, 2)):
        for start in range(0, depth, group):
            across = to_core(jnp.stack(values[start : start + group]))
            for step in range(start, start + group):
                row = chip * chip_tiles + (level ^ step) * shard_tiles
                for base, part in ((core, values[step]), (1 - core, across[step - start])):
                    grad = lax.dynamic_update_slice_in_dim(grad, part, base * core_tiles + row, 1)
    other = to_core(exponent + 0.0 * token(near[-1][0, 0])[0])
    by_core = [jnp.where(core == side, exponent, other) for side in range(2)]
    factor = jnp.exp2(-jnp.stack(by_core)) * (1.0 / samples)
    grad = grad.reshape(taps, 2, core_tiles, 2, TILE, LANES).astype(jnp.float32)
    grad = (grad * factor[None, :, None]).reshape(taps, rows // TILE, 2, TILE, LANES)
    weight_grad = jnp.transpose(grad, (1, 3, 0, 2, 4)).reshape(rows, taps, outs)

    total = forward(x, w, token(shard[0, 0]))
    if chans == 2:
        mine = lax.dynamic_slice_in_dim(total, chan * own_outs, own_outs, 0)
        theirs = lax.dynamic_slice_in_dim(total, (1 - chan) * own_outs, own_outs, 0)
        result = mine + lax.ppermute(theirs, "chan", [(0, 1), (1, 0)])
        cot = jnp.where(
            chan == 0,
            jnp.concatenate([own_cot, their_cot], 0),
            jnp.concatenate([their_cot, own_cot], 0),
        )
    else:
        result = lax.psum_scatter(total, "chan", scatter_dimension=0, tiled=True)
    result = result.astype(jnp.bfloat16)[None]
    input_grad = input_gradient(cot, w, token(near[depth // 2][0, 0]))[None]
    return (result, input_grad, weight_grad)


def solution(mesh):
    placed = (P("dp", "chan", None), P("chan", None, None), P("dp", "chan", None))
    return jax.shard_map(
        on_device,
        mesh=mesh,
        in_specs=placed,
        out_specs=(P("dp", "chan", None), P("dp", "chan", None), P("chan", None, None)),
        check_vma=False,
    )
```

```python
import functools

import jax
import jax.numpy as jnp
from jax import lax
from jax.experimental import pallas as pl
from jax.experimental.pallas import tpu as pltpu
from jax.sharding import PartitionSpec as P

DILATION_RATE = 12
MAP_HEIGHT = 16
MAP_WIDTH = 72
HW = MAP_HEIGHT * MAP_WIDTH
REACH = (MAP_HEIGHT - DILATION_RATE) * MAP_WIDTH
WINDOW = 384
PAD = WINDOW - REACH
COLUMN_SHIFTS = (-DILATION_RATE, 0, DILATION_RATE)
VMEM_LIMIT = 16 * 1024 * 1024


def column_mask(start, width, shift):
    position = lax.broadcasted_iota(jnp.int32, (1, width), 1) + start
    column = lax.rem(position, MAP_WIDTH) + shift
    return position, (column >= 0) & (column < MAP_WIDTH)


def moved(values, amount):
    amount = amount % values.shape[1]
    return values if amount == 0 else pltpu.roll(values, amount, 1)


def moved_cotangent(cot, group, shift):
    if group == 1:
        _, inside = column_mask(0, HW, -shift)
        values = moved(cot, shift)
    elif group == 0:
        position, inside = column_mask(0, WINDOW, -shift)
        inside = inside & (position < REACH)
        values = moved(cot[:, HW - WINDOW :], shift - PAD)
    else:
        position, inside = column_mask(HW - WINDOW, WINDOW, -shift)
        inside = inside & (position >= HW - REACH)
        values = moved(cot[:, :WINDOW], PAD + shift)
    return jnp.where(inside, values, 0.0).astype(jnp.bfloat16)


def window(group):
    return (slice(0, WINDOW), slice(0, HW), slice(HW - WINDOW, HW))[group]


TILE = 8
LANES = 128
TOP = 30000.0


def kernel_grad_kernel(depth, place_ref, own_x, other_x, own_cot, other_cot, _, *refs):
    near, far = refs[:depth], refs[depth : depth + 2]
    sums, peak_ref = refs[depth + 2 :]
    step = pl.program_id(0)
    rows, width = own_x.shape[0], own_cot.shape[0]
    shards = 2 * depth
    shard_rows = rows // shards
    tiles = shard_rows // TILE
    lanes = width // LANES

    @pl.when(step == 0)
    def _():
        peak_ref[...] = jnp.zeros(peak_ref.shape, jnp.float32)

    for group in range(3):

        @pl.when(step == group)
        def _(group=group):
            where = window(group)
            total = None
            for x_ref, cot_ref in ((own_x, own_cot), (other_x, other_cot)):
                cot = cot_ref[...].astype(jnp.float32)
                cots = [moved_cotangent(cot, group, shift) for shift in COLUMN_SHIFTS]
                term = lax.dot_general(
                    x_ref[:, where],
                    jnp.concatenate(cots, 0),
                    (((1,), (1,)), ((), ())),
                    preferred_element_type=jnp.float32,
                )
                total = term if total is None else total + term
            peak_ref[...] = jnp.maximum(
                peak_ref[...], jnp.max(jnp.abs(total), axis=0, keepdims=True)
            )
            for column in range(3):
                for shard in range(shards):
                    for tile in range(tiles):
                        for lane in range(lanes):
                            row = shard * shard_rows + tile * TILE
                            first = column * width + lane * LANES
                            slot = ((3 * group + column) * tiles + tile) * lanes + lane
                            sums[shard, slot] = total[row : row + TILE, first : first + LANES]

    @pl.when(step == 2)
    def _():
        peak = jnp.max(peak_ref[...], axis=1, keepdims=True)
        exponent = jnp.floor(jnp.log2(TOP / jnp.maximum(peak, 1e-30)))
        exponent = jnp.broadcast_to(exponent, (TILE, LANES))
        scale = jnp.exp2(exponent)
        count = sums.shape[1]
        for distance in range(shards):
            if distance < depth:
                out = near[distance]
            else:
                message, slot = divmod(distance - depth, depth // 2)
                out = far[message].at[slot]
            out[:count] = sums[place_ref[1] ^ distance] * scale
            out[count] = exponent


def kernel_grad(place, depth, x, other_x, own_cot, other_cot, after):
    rows, positions = other_x.shape
    outs = own_cot.shape[0]
    tiles = 9 * rows * outs // (2 * depth * TILE * LANES)
    whole = lambda g, h: (0, 0)
    once = pl.Buffered(1)
    shapes = [(tiles + 1, TILE, LANES)] * depth + [(depth // 2, tiles + 1, TILE, LANES)] * 2
    return pl.pallas_call(
        functools.partial(kernel_grad_kernel, depth),
        out_shape=[jax.ShapeDtypeStruct(shape, jnp.float32) for shape in shapes],
        grid_spec=pltpu.PrefetchScalarGridSpec(
            num_scalar_prefetch=1,
            grid=(3,),
            in_specs=[
                pl.BlockSpec((rows, positions), lambda g, h: (h[0], 0), pipeline_mode=once),
                pl.BlockSpec((rows, positions), whole, pipeline_mode=once),
                pl.BlockSpec((outs, positions), whole, pipeline_mode=once),
                pl.BlockSpec((outs, positions), whole, pipeline_mode=once),
                pl.BlockSpec(memory_space=pl.ANY),
            ],
            out_specs=[
                pl.BlockSpec(shape, functools.partial(lambda n, g, h: (0,) * n, len(shape)))
                for shape in shapes
            ],
            scratch_shapes=[
                pltpu.VMEM((2 * depth, tiles, TILE, LANES), jnp.float32),
                pltpu.VMEM((1, 3 * outs), jnp.float32),
            ],
        ),
        compiler_params=pltpu.CompilerParams(vmem_limit_bytes=VMEM_LIMIT),
        cost_estimate=pl.CostEstimate(
            flops=4 * rows * outs * 3 * (HW + 2 * WINDOW),
            bytes_accessed=4 * rows * positions + 4 * outs * positions + 36 * rows * outs,
            transcendentals=0,
        ),
        name="kernel_grad",
    )(place, x, other_x, own_cot, other_cot, after)


def forward_kernel(x_ref, w_ref, _, out_ref):
    step = pl.program_id(0)
    for group in range(3):

        @pl.when(step == group)
        def _(group=group):
            where = window(group)
            total = None
            for column, shift in enumerate(COLUMN_SHIFTS):
                term = lax.dot_general(
                    w_ref[column],
                    x_ref[:, where],
                    (((0,), (0,)), ((), ())),
                    preferred_element_type=jnp.float32,
                )
                if group == 1:
                    _, inside = column_mask(0, HW, shift)
                    term = moved(term, -shift)
                elif group == 0:
                    position, inside = column_mask(HW - WINDOW, WINDOW, shift)
                    inside = inside & (position >= HW - REACH)
                    term = moved(term, PAD - shift)
                else:
                    position, inside = column_mask(0, WINDOW, shift)
                    inside = inside & (position < REACH)
                    term = moved(term, -PAD - shift)
                term = jnp.where(inside, term, 0.0)
                total = term if total is None else total + term
            if group == 0:
                out_ref[:, : HW - WINDOW] = jnp.zeros((out_ref.shape[0], HW - WINDOW), jnp.float32)
                out_ref[:, HW - WINDOW :] = total
            elif group == 1:
                out_ref[...] += total
            else:
                out_ref[:, :WINDOW] += total


def forward(x, w, after):
    rows, positions = x.shape
    outs = w.shape[2]
    return pl.pallas_call(
        forward_kernel,
        out_shape=jax.ShapeDtypeStruct((outs, positions), jnp.float32),
        grid=(3,),
        in_specs=[
            pl.BlockSpec((rows, positions), lambda g: (0, 0), pipeline_mode=pl.Buffered(1)),
            pl.BlockSpec((3, rows, outs), lambda g: (g, 0, 0)),
            pl.BlockSpec(memory_space=pl.ANY),
        ],
        out_specs=pl.BlockSpec((outs, positions), lambda g: (0, 0)),
        compiler_params=pltpu.CompilerParams(vmem_limit_bytes=VMEM_LIMIT),
        cost_estimate=pl.CostEstimate(
            flops=2 * rows * outs * 3 * (HW + 2 * WINDOW),
            bytes_accessed=2 * rows * positions + 18 * rows * outs + 4 * outs * positions,
            transcendentals=0,
        ),
        name="forward",
    )(x, w, after)


def input_grad_kernel(cot_ref, w_ref, _, out_ref, middle, upper, lower):
    @pl.when(pl.program_id(0) == 0)
    def _():
        cot = cot_ref[...].astype(jnp.float32)
        for group, held in enumerate((upper, middle, lower)):
            for column, shift in enumerate(COLUMN_SHIFTS):
                held[column] = moved_cotangent(cot, group, shift)

    def products(group, held):
        total = None
        for column in range(3):
            term = jnp.dot(
                w_ref[3 * group + column], held[column], preferred_element_type=jnp.float32
            )
            total = term if total is None else total + term
        return total

    edge = HW - WINDOW
    centre = products(1, middle)
    out_ref[:, :WINDOW] = (centre[:, :WINDOW] + products(0, upper)).astype(jnp.bfloat16)
    out_ref[:, WINDOW:edge] = centre[:, WINDOW:edge].astype(jnp.bfloat16)
    out_ref[:, edge:] = (centre[:, edge:] + products(2, lower)).astype(jnp.bfloat16)


def input_gradient(cot, w, after):
    outs, positions = cot.shape
    rows = w.shape[1]
    block = min(rows, 256)
    return pl.pallas_call(
        input_grad_kernel,
        out_shape=jax.ShapeDtypeStruct((rows, positions), jnp.bfloat16),
        grid=(rows // block,),
        in_specs=[
            pl.BlockSpec((outs, positions), lambda g: (0, 0)),
            pl.BlockSpec((9, block, outs), lambda g: (0, g, 0)),
            pl.BlockSpec(memory_space=pl.ANY),
        ],
        out_specs=pl.BlockSpec((block, positions), lambda g: (g, 0)),
        scratch_shapes=[
            pltpu.VMEM((3, outs, HW), jnp.bfloat16),
            pltpu.VMEM((3, outs, WINDOW), jnp.bfloat16),
            pltpu.VMEM((3, outs, WINDOW), jnp.bfloat16),
        ],
        compiler_params=pltpu.CompilerParams(vmem_limit_bytes=VMEM_LIMIT),
        cost_estimate=pl.CostEstimate(
            flops=2 * rows * outs * 3 * (HW + 2 * WINDOW),
            bytes_accessed=2 * outs * positions + 18 * rows * outs + 2 * rows * positions,
            transcendentals=0,
        ),
        name="input_gradient",
    )(cot, w, after)


def common_exponent(values, bits):
    lowest = functools.reduce(
        jnp.minimum, [value[-1:].astype(jnp.float32) + bit for value, bit in values]
    )
    return lowest - bits


def scaled_sum(values, lowest):
    return sum(
        value.astype(jnp.float32) * jnp.exp2(lowest - value[-1:].astype(jnp.float32))
        for value, _ in values
    )


def later(value, *gates):
    for gate in gates:
        gate = gate[(0,) * (gate.ndim - 2)]
        value = jnp.where(gate.astype(jnp.float32) > -1e30, value, jnp.zeros_like(value))
    return value


def summed(values, bits, *gates):
    lowest = common_exponent(values, bits)
    total = later(scaled_sum(values, lowest), *gates).astype(jnp.float16)
    return lax.dynamic_update_slice(
        total, lowest.astype(jnp.float16), (total.shape[0] - 1, 0, 0)
    )


def token(value):
    return value[0].astype(jnp.float32)


def on_device(inputs, weight, cotangent):
    x = inputs[0]
    x_held = pltpu.with_memory_space_constraint(x, pltpu.HBM)
    own_cot = cotangent[0]
    w = jnp.transpose(weight, (1, 0, 2))
    taps, rows, outs = w.shape
    own_outs, positions = own_cot.shape
    samples = lax.axis_size("dp")
    chans = lax.axis_size("chan")
    depth = samples // 4
    place = lax.axis_index("dp")
    chan = lax.axis_index("chan")
    core, column, level = place % 2, (place // 2) % 2, place // 4
    core_rows = rows // 2
    core_tiles = core_rows // TILE
    chip_tiles = core_tiles // 2
    shard_tiles = chip_tiles // depth

    def to(value, distance):
        return lax.ppermute(value, "dp", [(i, i ^ distance) for i in range(samples)])

    def to_core(value):
        return to(value, 1)

    def to_column(value):
        return to(value, 2)

    def to_level(value, step):
        return to(value, 4 * step)

    if chans == 2:
        their_cot = lax.ppermute(own_cot, "chan", [(0, 1), (1, 0)])
        parts = (own_cot, their_cot)
        first = chan
    else:
        cot = lax.all_gather(own_cot, "chan", axis=0, tiled=True)
        parts = (cot[:LANES], cot[LANES:])
        first = 0
    other_x = to_core(lax.dynamic_slice_in_dim(x, (1 - core) * core_rows, core_rows, 0))
    where = jnp.stack([core, column * depth + level]).astype(jnp.int32)
    halves, exponents, arrived, sends = [], [], [], []
    grad = jnp.zeros((taps, rows // TILE, 2, TILE, LANES), jnp.float16)
    after = own_cot
    for side in range(2):
        part = parts[side]
        if side == 1:
            part = later(part, shards[0][-1:, :1, :1])
            their_cot = part
        shards = kernel_grad(where, depth, x_held, other_x, part, to_core(part), after)
        held = [None] * depth
        gates = ()
        for message in (1, 0):
            sent = later(shards[depth + message], *gates).astype(jnp.float16)
            came = to_column(sent)
            gates = (sent,)
            for slot in range(depth // 2 - 1, -1, -1):
                step = message * (depth // 2) + slot
                held[step] = [(shards[step], 0.0), (came[slot], 0.0)]
        after = sent[0, 0].astype(jnp.float32)
        bits = 1.0
        gates = (sends[-1],) if side else ()
        for bit in [1 << shift for shift in range(depth.bit_length() - 1)]:
            for step in range(depth - bit, 0, -2 * bit):
                pair = summed(held[step], bits, *gates)
                held[step ^ bit].append((to_level(pair, bit), bits))
                gates = (pair, halves[0]) if side else (pair,)
                sends.append(pair)
            bits += 1.0
        lowest = common_exponent(held[0], bits)
        total = later(scaled_sum(held[0], lowest)[:-1], *arrived).astype(jnp.float16)
        shard = total.reshape(taps, shard_tiles, 1, TILE, LANES)
        halves.append(shard)
        exponents.append(lowest)

        near = [shard]
        for step in range(1, depth):
            low = step & -step
            source = near[step ^ low]
            if side == 1 and step == depth - 1:
                source = later(source, rest)
            near.append(to_level(source, low))
        if side == 0:
            rest = to_column(jnp.stack(near[1:]))
            far = [to_column(shard)] + [rest[step] for step in range(depth - 1)]
            arrived = [near[depth // 2], far[0]]
            groups = ((column, near), (1 - column, far))
        else:
            far = [to_column(value) for value in near]
            groups = ((column, near), (1 - column, far[:-1]), (1 - column, far[-1:]))
        lane = first if side == 0 else 1 - first
        step = 0
        for chip, values in groups:
            across = to_core(jnp.stack(values))
            for slot, value in enumerate(values):
                row = chip * chip_tiles + (level ^ (step % depth)) * shard_tiles
                step += 1
                for base, piece in ((core, value), (1 - core, across[slot])):
                    grad = lax.dynamic_update_slice(
                        grad, piece, (0, base * core_tiles + row, lane, 0, 0)
                    )
    exponents = [jnp.where(first == side, exponents[0], exponents[1]) for side in range(2)]
    exponent = jnp.concatenate(exponents, 0)
    other = to_core(exponent + 0.0 * token(near[-1][0, 0])[0])
    by_core = [jnp.where(core == side, exponent, other) for side in range(2)]
    factor = jnp.exp2(-jnp.stack(by_core)) * (1.0 / samples)
    grad = grad.reshape(taps, 2, core_tiles, 2, TILE, LANES).astype(jnp.float32)
    grad = (grad * factor[None, :, None]).reshape(taps, rows // TILE, 2, TILE, LANES)
    weight_grad = jnp.transpose(grad, (1, 3, 0, 2, 4)).reshape(rows, taps, outs)

    total = forward(x, w, token(sends[depth - 2]))
    if chans == 2:
        mine = lax.dynamic_slice_in_dim(total, chan * own_outs, own_outs, 0)
        theirs = lax.dynamic_slice_in_dim(total, (1 - chan) * own_outs, own_outs, 0)
        result = mine + lax.ppermute(theirs, "chan", [(0, 1), (1, 0)])
        cot = jnp.where(
            chan == 0,
            jnp.concatenate([own_cot, their_cot], 0),
            jnp.concatenate([their_cot, own_cot], 0),
        )
    else:
        result = lax.psum_scatter(total, "chan", scatter_dimension=0, tiled=True)
    result = result.astype(jnp.bfloat16)[None]
    input_grad = input_gradient(cot, w, token(halves[1][0, 0]))[None]
    return (result, input_grad, weight_grad)


def solution(mesh):
    placed = (P("dp", "chan", None), P("chan", None, None), P("dp", "chan", None))
    return jax.shard_map(
        on_device,
        mesh=mesh,
        in_specs=placed,
        out_specs=(P("dp", "chan", None), P("dp", "chan", None), P("chan", None, None)),
        check_vma=False,
    )
```

```python
import functools

import jax
import jax.numpy as jnp
from jax import lax
from jax.experimental import pallas as pl
from jax.experimental.pallas import tpu as pltpu
from jax.sharding import PartitionSpec as P

DILATION_RATE = 12
MAP_HEIGHT = 16
MAP_WIDTH = 72
HW = MAP_HEIGHT * MAP_WIDTH
REACH = (MAP_HEIGHT - DILATION_RATE) * MAP_WIDTH
WINDOW = 384
PAD = WINDOW - REACH
COLUMN_SHIFTS = (-DILATION_RATE, 0, DILATION_RATE)
VMEM_LIMIT = 16 * 1024 * 1024


def column_mask(start, width, shift):
    position = lax.broadcasted_iota(jnp.int32, (1, width), 1) + start
    column = lax.rem(position, MAP_WIDTH) + shift
    return position, (column >= 0) & (column < MAP_WIDTH)


def moved(values, amount):
    amount = amount % values.shape[1]
    return values if amount == 0 else pltpu.roll(values, amount, 1)


def moved_cotangent(cot, group, shift):
    if group == 1:
        _, inside = column_mask(0, HW, -shift)
        values = moved(cot, shift)
    elif group == 0:
        position, inside = column_mask(0, WINDOW, -shift)
        inside = inside & (position < REACH)
        values = moved(cot[:, HW - WINDOW :], shift - PAD)
    else:
        position, inside = column_mask(HW - WINDOW, WINDOW, -shift)
        inside = inside & (position >= HW - REACH)
        values = moved(cot[:, :WINDOW], PAD + shift)
    return jnp.where(inside, values, 0.0).astype(jnp.bfloat16)


def window(group):
    return (slice(0, WINDOW), slice(0, HW), slice(HW - WINDOW, HW))[group]


TILE = 8
LANES = 128
TOP = 30000.0


def kernel_grad_kernel(depth, place_ref, own_x, other_x, own_cot, other_cot, _, *refs):
    near, far = refs[:depth], refs[depth : depth + 2]
    sums, peak_ref = refs[depth + 2 :]
    step = pl.program_id(0)
    rows, width = own_x.shape[0], own_cot.shape[0]
    shards = 2 * depth
    shard_rows = rows // shards
    tiles = shard_rows // TILE
    lanes = width // LANES

    @pl.when(step == 0)
    def _():
        peak_ref[...] = jnp.zeros(peak_ref.shape, jnp.float32)

    for group in range(3):

        @pl.when(step == group)
        def _(group=group):
            where = window(group)
            total = None
            for x_ref, cot_ref in ((own_x, own_cot), (other_x, other_cot)):
                cot = cot_ref[...].astype(jnp.float32)
                cots = [moved_cotangent(cot, group, shift) for shift in COLUMN_SHIFTS]
                term = lax.dot_general(
                    x_ref[:, where],
                    jnp.concatenate(cots, 0),
                    (((1,), (1,)), ((), ())),
                    preferred_element_type=jnp.float32,
                )
                total = term if total is None else total + term
            peak_ref[...] = jnp.maximum(
                peak_ref[...], jnp.max(jnp.abs(total), axis=0, keepdims=True)
            )
            for column in range(3):
                for shard in range(shards):
                    for tile in range(tiles):
                        for lane in range(lanes):
                            row = shard * shard_rows + tile * TILE
                            first = column * width + lane * LANES
                            slot = ((3 * group + column) * tiles + tile) * lanes + lane
                            sums[shard, slot] = total[row : row + TILE, first : first + LANES]

    @pl.when(step == 2)
    def _():
        peak = jnp.max(peak_ref[...], axis=1, keepdims=True)
        exponent = jnp.floor(jnp.log2(TOP / jnp.maximum(peak, 1e-30)))
        exponent = jnp.broadcast_to(exponent, (TILE, LANES))
        scale = jnp.exp2(exponent)
        count = sums.shape[1]
        for distance in range(shards):
            if distance < depth:
                out = near[distance]
            else:
                message, slot = divmod(distance - depth, depth // 2)
                out = far[message].at[slot]
            out[:count] = sums[place_ref[1] ^ distance] * scale
            out[count] = exponent


def kernel_grad(place, depth, x, other_x, own_cot, other_cot, after):
    rows, positions = other_x.shape
    outs = own_cot.shape[0]
    tiles = 9 * rows * outs // (2 * depth * TILE * LANES)
    whole = lambda g, h: (0, 0)
    once = pl.Buffered(1)
    shapes = [(tiles + 1, TILE, LANES)] * depth + [(depth // 2, tiles + 1, TILE, LANES)] * 2
    return pl.pallas_call(
        functools.partial(kernel_grad_kernel, depth),
        out_shape=[jax.ShapeDtypeStruct(shape, jnp.float32) for shape in shapes],
        grid_spec=pltpu.PrefetchScalarGridSpec(
            num_scalar_prefetch=1,
            grid=(3,),
            in_specs=[
                pl.BlockSpec((rows, positions), lambda g, h: (h[0], 0), pipeline_mode=once),
                pl.BlockSpec((rows, positions), whole, pipeline_mode=once),
                pl.BlockSpec((outs, positions), whole, pipeline_mode=once),
                pl.BlockSpec((outs, positions), whole, pipeline_mode=once),
                pl.BlockSpec(memory_space=pl.ANY),
            ],
            out_specs=[
                pl.BlockSpec(shape, functools.partial(lambda n, g, h: (0,) * n, len(shape)))
                for shape in shapes
            ],
            scratch_shapes=[
                pltpu.VMEM((2 * depth, tiles, TILE, LANES), jnp.float32),
                pltpu.VMEM((1, 3 * outs), jnp.float32),
            ],
        ),
        compiler_params=pltpu.CompilerParams(vmem_limit_bytes=VMEM_LIMIT),
        cost_estimate=pl.CostEstimate(
            flops=4 * rows * outs * 3 * (HW + 2 * WINDOW),
            bytes_accessed=4 * rows * positions + 4 * outs * positions + 36 * rows * outs,
            transcendentals=0,
        ),
        name="kernel_grad",
    )(place, x, other_x, own_cot, other_cot, after)


def forward_kernel(x_ref, w_ref, _, out_ref):
    step = pl.program_id(0)
    for group in range(3):

        @pl.when(step == group)
        def _(group=group):
            where = window(group)
            total = None
            for column, shift in enumerate(COLUMN_SHIFTS):
                term = lax.dot_general(
                    w_ref[column],
                    x_ref[:, where],
                    (((0,), (0,)), ((), ())),
                    preferred_element_type=jnp.float32,
                )
                if group == 1:
                    _, inside = column_mask(0, HW, shift)
                    term = moved(term, -shift)
                elif group == 0:
                    position, inside = column_mask(HW - WINDOW, WINDOW, shift)
                    inside = inside & (position >= HW - REACH)
                    term = moved(term, PAD - shift)
                else:
                    position, inside = column_mask(0, WINDOW, shift)
                    inside = inside & (position < REACH)
                    term = moved(term, -PAD - shift)
                term = jnp.where(inside, term, 0.0)
                total = term if total is None else total + term
            if group == 0:
                out_ref[:, : HW - WINDOW] = jnp.zeros((out_ref.shape[0], HW - WINDOW), jnp.float32)
                out_ref[:, HW - WINDOW :] = total
            elif group == 1:
                out_ref[...] += total
            else:
                out_ref[:, :WINDOW] += total


def forward(x, w, after):
    rows, positions = x.shape
    outs = w.shape[2]
    return pl.pallas_call(
        forward_kernel,
        out_shape=jax.ShapeDtypeStruct((outs, positions), jnp.float32),
        grid=(3,),
        in_specs=[
            pl.BlockSpec((rows, positions), lambda g: (0, 0), pipeline_mode=pl.Buffered(1)),
            pl.BlockSpec((3, rows, outs), lambda g: (g, 0, 0)),
            pl.BlockSpec(memory_space=pl.ANY),
        ],
        out_specs=pl.BlockSpec((outs, positions), lambda g: (0, 0)),
        compiler_params=pltpu.CompilerParams(vmem_limit_bytes=VMEM_LIMIT),
        cost_estimate=pl.CostEstimate(
            flops=2 * rows * outs * 3 * (HW + 2 * WINDOW),
            bytes_accessed=2 * rows * positions + 18 * rows * outs + 4 * outs * positions,
            transcendentals=0,
        ),
        name="forward",
    )(x, w, after)


def input_grad_kernel(cot_ref, w_ref, _, out_ref, middle, upper, lower):
    @pl.when(pl.program_id(0) == 0)
    def _():
        cot = cot_ref[...].astype(jnp.float32)
        for group, held in enumerate((upper, middle, lower)):
            for column, shift in enumerate(COLUMN_SHIFTS):
                held[column] = moved_cotangent(cot, group, shift)

    def products(group, held):
        total = None
        for column in range(3):
            term = jnp.dot(
                w_ref[3 * group + column], held[column], preferred_element_type=jnp.float32
            )
            total = term if total is None else total + term
        return total

    edge = HW - WINDOW
    centre = products(1, middle)
    out_ref[:, :WINDOW] = (centre[:, :WINDOW] + products(0, upper)).astype(jnp.bfloat16)
    out_ref[:, WINDOW:edge] = centre[:, WINDOW:edge].astype(jnp.bfloat16)
    out_ref[:, edge:] = (centre[:, edge:] + products(2, lower)).astype(jnp.bfloat16)


def input_gradient(cot, w, after):
    outs, positions = cot.shape
    rows = w.shape[1]
    block = min(rows, 256)
    return pl.pallas_call(
        input_grad_kernel,
        out_shape=jax.ShapeDtypeStruct((rows, positions), jnp.bfloat16),
        grid=(rows // block,),
        in_specs=[
            pl.BlockSpec((outs, positions), lambda g: (0, 0)),
            pl.BlockSpec((9, block, outs), lambda g: (0, g, 0)),
            pl.BlockSpec(memory_space=pl.ANY),
        ],
        out_specs=pl.BlockSpec((block, positions), lambda g: (g, 0)),
        scratch_shapes=[
            pltpu.VMEM((3, outs, HW), jnp.bfloat16),
            pltpu.VMEM((3, outs, WINDOW), jnp.bfloat16),
            pltpu.VMEM((3, outs, WINDOW), jnp.bfloat16),
        ],
        compiler_params=pltpu.CompilerParams(vmem_limit_bytes=VMEM_LIMIT),
        cost_estimate=pl.CostEstimate(
            flops=2 * rows * outs * 3 * (HW + 2 * WINDOW),
            bytes_accessed=2 * outs * positions + 18 * rows * outs + 2 * rows * positions,
            transcendentals=0,
        ),
        name="input_gradient",
    )(cot, w, after)


def common_exponent(values, bits):
    lowest = functools.reduce(
        jnp.minimum, [value[-1:].astype(jnp.float32) + bit for value, bit in values]
    )
    return lowest - bits


def scaled_sum(values, lowest):
    return sum(
        value.astype(jnp.float32) * jnp.exp2(lowest - value[-1:].astype(jnp.float32))
        for value, _ in values
    )


def later(value, *gates):
    for gate in gates:
        gate = gate[(0,) * (gate.ndim - 2)]
        value = jnp.where(gate.astype(jnp.float32) > -1e30, value, jnp.zeros_like(value))
    return value


def summed(values, bits, *gates):
    lowest = common_exponent(values, bits)
    total = later(scaled_sum(values, lowest), *gates).astype(jnp.float16)
    return lax.dynamic_update_slice(
        total, lowest.astype(jnp.float16), (total.shape[0] - 1, 0, 0)
    )


def token(value):
    return value[0].astype(jnp.float32)


def on_device(inputs, weight, cotangent):
    x = inputs[0]
    x_held = pltpu.with_memory_space_constraint(x, pltpu.HBM)
    own_cot = cotangent[0]
    w = jnp.transpose(weight, (1, 0, 2))
    taps, rows, outs = w.shape
    own_outs, positions = own_cot.shape
    samples = lax.axis_size("dp")
    chans = lax.axis_size("chan")
    depth = samples // 4
    place = lax.axis_index("dp")
    chan = lax.axis_index("chan")
    core, column, level = place % 2, (place // 2) % 2, place // 4
    core_rows = rows // 2
    core_tiles = core_rows // TILE
    chip_tiles = core_tiles // 2
    shard_tiles = chip_tiles // depth

    def to(value, distance):
        return lax.ppermute(value, "dp", [(i, i ^ distance) for i in range(samples)])

    def to_core(value):
        return to(value, 1)

    def to_column(value):
        return to(value, 2)

    def to_level(value, step):
        return to(value, 4 * step)

    if chans == 2:
        their_cot = lax.ppermute(own_cot, "chan", [(0, 1), (1, 0)])
        parts = (own_cot, their_cot)
        first = chan
    else:
        cot = lax.all_gather(own_cot, "chan", axis=0, tiled=True)
        parts = (cot[:LANES], cot[LANES:])
        first = 0
    other_x = to_core(lax.dynamic_slice_in_dim(x, (1 - core) * core_rows, core_rows, 0))
    where = jnp.stack([core, column * depth + level]).astype(jnp.int32)
    halves, exponents, arrived, sends, gathers = [], [], [], [], []
    bits_of_depth = [1 << shift for shift in range(depth.bit_length() - 1)]
    grad = jnp.zeros((taps, rows // TILE, 2, TILE, LANES), jnp.float16)
    after = own_cot
    for side in range(2):
        part = parts[side]
        if side == 1:
            part = later(part, shards[0][-1:, :1, :1])
            their_cot = part
        shards = kernel_grad(where, depth, x_held, other_x, part, to_core(part), after)
        held = [None] * depth
        gates = ()
        for message in (1, 0):
            sent = later(shards[depth + message], *gates).astype(jnp.float16)
            came = to_column(sent)
            gates = (sent,)
            for slot in range(depth // 2 - 1, -1, -1):
                step = message * (depth // 2) + slot
                held[step] = [(shards[step], 0.0), (came[slot], 0.0)]
        after = sent[0, 0].astype(jnp.float32)
        bits = 1.0
        gates = (sends[-1],) if side else ()
        for bit in bits_of_depth:
            for step in range(depth - bit, 0, -2 * bit):
                pair = summed(held[step], bits, *gates)
                held[step ^ bit].append((to_level(pair, bit), bits))
                gates = (pair, halves[0]) if side and step == 1 else (pair,)
                sends.append(pair)
            bits += 1.0
        lowest = common_exponent(held[0], bits)
        total = later(scaled_sum(held[0], lowest)[:-1], *arrived).astype(jnp.float16)
        shard = total.reshape(taps, shard_tiles, 1, TILE, LANES)
        halves.append(shard)
        exponents.append(lowest)

        near = [shard] + [None] * (depth - 1)
        for bit in bits_of_depth[::-1]:
            near[bit] = to_level(shard, bit)
        own = to_column(shard)
        arrived = [own]
        gathers.append((near, own))

    for side, (near, own) in enumerate(gathers):
        for step in range(1, depth):
            if near[step] is None:
                low = step & -step
                source = near[step ^ low] if side else later(near[step ^ low], gathers[1][0][1])
                near[step] = to_level(source, low)
        steps = list(range(depth))
        cuts = [steps[1:2], steps[2:]] if side == 0 else [steps[1:]]
        here = [jnp.stack([near[step] for step in cut]) for cut in cuts]
        if side == 1:
            here = [later(values, returned) for values in here]
        there = [to_column(values) for values in here]
        if side == 0:
            returned = there[1]
        here, there = [near[0][None]] + here, [own[None]] + there
        pieces = [(column, step, near[step]) for step in steps]
        arrivals = [(steps[0], own)] + [
            (step, values[slot])
            for cut, values in zip(cuts, there[1:])
            for slot, step in enumerate(cut)
        ]
        pieces += [(1 - column, step, value) for step, value in arrivals]
        if side == 0:
            messages = [(pieces, jnp.concatenate(here + there))]
        else:
            count = depth + 1
            messages = [
                (pieces[:count], jnp.concatenate(here + there[:1])),
                (pieces[count:], there[1]),
            ]
        lane = first if side == 0 else 1 - first
        for listed, message in messages:
            across = to_core(message)
            for slot, (chip, step, piece) in enumerate(listed):
                row = chip * chip_tiles + (level ^ step) * shard_tiles
                for base, value in ((core, piece), (1 - core, across[slot])):
                    grad = lax.dynamic_update_slice(
                        grad, value, (0, base * core_tiles + row, lane, 0, 0)
                    )
    exponents = [jnp.where(first == side, exponents[0], exponents[1]) for side in range(2)]
    exponent = jnp.concatenate(exponents, 0)
    other = to_core(later(exponent, returned))
    by_core = [jnp.where(core == side, exponent, other) for side in range(2)]
    factor = jnp.exp2(-jnp.stack(by_core)) * (1.0 / samples)
    grad = grad.reshape(taps, 2, core_tiles, 2, TILE, LANES).astype(jnp.float32)
    grad = (grad * factor[None, :, None]).reshape(taps, rows // TILE, 2, TILE, LANES)
    weight_grad = jnp.transpose(grad, (1, 3, 0, 2, 4)).reshape(rows, taps, outs)

    total = forward(x, w, token(halves[1][0, 0]))
    if chans == 2:
        mine = lax.dynamic_slice_in_dim(total, chan * own_outs, own_outs, 0)
        theirs = lax.dynamic_slice_in_dim(total, (1 - chan) * own_outs, own_outs, 0)
        result = mine + lax.ppermute(theirs, "chan", [(0, 1), (1, 0)])
        cot = jnp.where(
            chan == 0,
            jnp.concatenate([own_cot, their_cot], 0),
            jnp.concatenate([their_cot, own_cot], 0),
        )
    else:
        result = lax.psum_scatter(total, "chan", scatter_dimension=0, tiled=True)
    result = result.astype(jnp.bfloat16)[None]
    input_grad = input_gradient(cot, w, token(returned[0, 0, 0]))[None]
    return (result, input_grad, weight_grad)


def solution(mesh):
    placed = (P("dp", "chan", None), P("chan", None, None), P("dp", "chan", None))
    return jax.shard_map(
        on_device,
        mesh=mesh,
        in_specs=placed,
        out_specs=(P("dp", "chan", None), P("dp", "chan", None), P("chan", None, None)),
        check_vma=False,
    )
```

```python
import functools

import jax
import jax.numpy as jnp
from jax import lax
from jax.experimental import pallas as pl
from jax.experimental.pallas import tpu as pltpu
from jax.sharding import PartitionSpec as P

DILATION_RATE = 12
MAP_HEIGHT = 16
MAP_WIDTH = 72
HW = MAP_HEIGHT * MAP_WIDTH
REACH = (MAP_HEIGHT - DILATION_RATE) * MAP_WIDTH
WINDOW = 384
PAD = WINDOW - REACH
COLUMN_SHIFTS = (-DILATION_RATE, 0, DILATION_RATE)
VMEM_LIMIT = 16 * 1024 * 1024


def column_mask(start, width, shift):
    position = lax.broadcasted_iota(jnp.int32, (1, width), 1) + start
    column = lax.rem(position, MAP_WIDTH) + shift
    return position, (column >= 0) & (column < MAP_WIDTH)


def moved(values, amount):
    amount = amount % values.shape[1]
    return values if amount == 0 else pltpu.roll(values, amount, 1)


def moved_cotangent(cot, group, shift):
    if group == 1:
        _, inside = column_mask(0, HW, -shift)
        values = moved(cot, shift)
    elif group == 0:
        position, inside = column_mask(0, WINDOW, -shift)
        inside = inside & (position < REACH)
        values = moved(cot[:, HW - WINDOW :], shift - PAD)
    else:
        position, inside = column_mask(HW - WINDOW, WINDOW, -shift)
        inside = inside & (position >= HW - REACH)
        values = moved(cot[:, :WINDOW], PAD + shift)
    return jnp.where(inside, values, 0.0).astype(jnp.bfloat16)


def window(group):
    return (slice(0, WINDOW), slice(0, HW), slice(HW - WINDOW, HW))[group]


TILE = 8
LANES = 128
TOP = 30000.0


def kernel_grad_kernel(depth, place_ref, own_x, other_x, own_cot, other_cot, _, *refs):
    near, far = refs[:depth], refs[depth : depth + 2]
    sums, peak_ref = refs[depth + 2 :]
    step = pl.program_id(0)
    rows, width = own_x.shape[0], own_cot.shape[0]
    shards = 2 * depth
    shard_rows = rows // shards
    tiles = shard_rows // TILE
    lanes = width // LANES

    @pl.when(step == 0)
    def _():
        peak_ref[...] = jnp.zeros(peak_ref.shape, jnp.float32)

    for group in range(3):

        @pl.when(step == group)
        def _(group=group):
            where = window(group)
            total = None
            for x_ref, cot_ref in ((own_x, own_cot), (other_x, other_cot)):
                cot = cot_ref[...].astype(jnp.float32)
                cots = [moved_cotangent(cot, group, shift) for shift in COLUMN_SHIFTS]
                term = lax.dot_general(
                    x_ref[:, where],
                    jnp.concatenate(cots, 0),
                    (((1,), (1,)), ((), ())),
                    preferred_element_type=jnp.float32,
                )
                total = term if total is None else total + term
            peak_ref[...] = jnp.maximum(
                peak_ref[...], jnp.max(jnp.abs(total), axis=0, keepdims=True)
            )
            for column in range(3):
                for shard in range(shards):
                    for tile in range(tiles):
                        for lane in range(lanes):
                            row = shard * shard_rows + tile * TILE
                            first = column * width + lane * LANES
                            slot = ((3 * group + column) * tiles + tile) * lanes + lane
                            sums[shard, slot] = total[row : row + TILE, first : first + LANES]

    @pl.when(step == 2)
    def _():
        peak = jnp.max(peak_ref[...], axis=1, keepdims=True)
        exponent = jnp.floor(jnp.log2(TOP / jnp.maximum(peak, 1e-30)))
        exponent = jnp.broadcast_to(exponent, (TILE, LANES))
        scale = jnp.exp2(exponent)
        count = sums.shape[1]
        for distance in range(shards):
            if distance < depth:
                out = near[distance]
            else:
                message, slot = divmod(distance - depth, depth // 2)
                out = far[message].at[slot]
            out[:count] = sums[place_ref[1] ^ distance] * scale
            out[count] = exponent


def kernel_grad(place, depth, x, other_x, own_cot, other_cot, after):
    rows, positions = other_x.shape
    outs = own_cot.shape[0]
    tiles = 9 * rows * outs // (2 * depth * TILE * LANES)
    whole = lambda g, h: (0, 0)
    once = pl.Buffered(1)
    shapes = [(tiles + 1, TILE, LANES)] * depth + [(depth // 2, tiles + 1, TILE, LANES)] * 2
    return pl.pallas_call(
        functools.partial(kernel_grad_kernel, depth),
        out_shape=[jax.ShapeDtypeStruct(shape, jnp.float32) for shape in shapes],
        grid_spec=pltpu.PrefetchScalarGridSpec(
            num_scalar_prefetch=1,
            grid=(3,),
            in_specs=[
                pl.BlockSpec((rows, positions), lambda g, h: (h[0], 0), pipeline_mode=once),
                pl.BlockSpec((rows, positions), whole, pipeline_mode=once),
                pl.BlockSpec((outs, positions), whole, pipeline_mode=once),
                pl.BlockSpec((outs, positions), whole, pipeline_mode=once),
                pl.BlockSpec(memory_space=pl.ANY),
            ],
            out_specs=[
                pl.BlockSpec(shape, functools.partial(lambda n, g, h: (0,) * n, len(shape)))
                for shape in shapes
            ],
            scratch_shapes=[
                pltpu.VMEM((2 * depth, tiles, TILE, LANES), jnp.float32),
                pltpu.VMEM((1, 3 * outs), jnp.float32),
            ],
        ),
        compiler_params=pltpu.CompilerParams(vmem_limit_bytes=VMEM_LIMIT),
        cost_estimate=pl.CostEstimate(
            flops=4 * rows * outs * 3 * (HW + 2 * WINDOW),
            bytes_accessed=4 * rows * positions + 4 * outs * positions + 36 * rows * outs,
            transcendentals=0,
        ),
        name="kernel_grad",
    )(place, x, other_x, own_cot, other_cot, after)


def forward_kernel(x_ref, w_ref, _, out_ref):
    step = pl.program_id(0)
    for group in range(3):

        @pl.when(step == group)
        def _(group=group):
            where = window(group)
            total = None
            for column, shift in enumerate(COLUMN_SHIFTS):
                term = lax.dot_general(
                    w_ref[column],
                    x_ref[:, where],
                    (((0,), (0,)), ((), ())),
                    preferred_element_type=jnp.float32,
                )
                if group == 1:
                    _, inside = column_mask(0, HW, shift)
                    term = moved(term, -shift)
                elif group == 0:
                    position, inside = column_mask(HW - WINDOW, WINDOW, shift)
                    inside = inside & (position >= HW - REACH)
                    term = moved(term, PAD - shift)
                else:
                    position, inside = column_mask(0, WINDOW, shift)
                    inside = inside & (position < REACH)
                    term = moved(term, -PAD - shift)
                term = jnp.where(inside, term, 0.0)
                total = term if total is None else total + term
            if group == 0:
                out_ref[:, : HW - WINDOW] = jnp.zeros((out_ref.shape[0], HW - WINDOW), jnp.float32)
                out_ref[:, HW - WINDOW :] = total
            elif group == 1:
                out_ref[...] += total
            else:
                out_ref[:, :WINDOW] += total


def forward(x, w, after):
    rows, positions = x.shape
    outs = w.shape[2]
    return pl.pallas_call(
        forward_kernel,
        out_shape=jax.ShapeDtypeStruct((outs, positions), jnp.float32),
        grid=(3,),
        in_specs=[
            pl.BlockSpec((rows, positions), lambda g: (0, 0), pipeline_mode=pl.Buffered(1)),
            pl.BlockSpec((3, rows, outs), lambda g: (g, 0, 0)),
            pl.BlockSpec(memory_space=pl.ANY),
        ],
        out_specs=pl.BlockSpec((outs, positions), lambda g: (0, 0)),
        compiler_params=pltpu.CompilerParams(vmem_limit_bytes=VMEM_LIMIT),
        cost_estimate=pl.CostEstimate(
            flops=2 * rows * outs * 3 * (HW + 2 * WINDOW),
            bytes_accessed=2 * rows * positions + 18 * rows * outs + 4 * outs * positions,
            transcendentals=0,
        ),
        name="forward",
    )(x, w, after)


def input_grad_kernel(cot_ref, w_ref, _, out_ref, middle, upper, lower):
    @pl.when(pl.program_id(0) == 0)
    def _():
        cot = cot_ref[...].astype(jnp.float32)
        for group, held in enumerate((upper, middle, lower)):
            for column, shift in enumerate(COLUMN_SHIFTS):
                held[column] = moved_cotangent(cot, group, shift)

    def products(group, held):
        total = None
        for column in range(3):
            term = jnp.dot(
                w_ref[3 * group + column], held[column], preferred_element_type=jnp.float32
            )
            total = term if total is None else total + term
        return total

    edge = HW - WINDOW
    centre = products(1, middle)
    out_ref[:, :WINDOW] = (centre[:, :WINDOW] + products(0, upper)).astype(jnp.bfloat16)
    out_ref[:, WINDOW:edge] = centre[:, WINDOW:edge].astype(jnp.bfloat16)
    out_ref[:, edge:] = (centre[:, edge:] + products(2, lower)).astype(jnp.bfloat16)


def input_gradient(cot, w, after):
    outs, positions = cot.shape
    rows = w.shape[1]
    block = min(rows, 256)
    return pl.pallas_call(
        input_grad_kernel,
        out_shape=jax.ShapeDtypeStruct((rows, positions), jnp.bfloat16),
        grid=(rows // block,),
        in_specs=[
            pl.BlockSpec((outs, positions), lambda g: (0, 0)),
            pl.BlockSpec((9, block, outs), lambda g: (0, g, 0)),
            pl.BlockSpec(memory_space=pl.ANY),
        ],
        out_specs=pl.BlockSpec((block, positions), lambda g: (g, 0)),
        scratch_shapes=[
            pltpu.VMEM((3, outs, HW), jnp.bfloat16),
            pltpu.VMEM((3, outs, WINDOW), jnp.bfloat16),
            pltpu.VMEM((3, outs, WINDOW), jnp.bfloat16),
        ],
        compiler_params=pltpu.CompilerParams(vmem_limit_bytes=VMEM_LIMIT),
        cost_estimate=pl.CostEstimate(
            flops=2 * rows * outs * 3 * (HW + 2 * WINDOW),
            bytes_accessed=2 * outs * positions + 18 * rows * outs + 2 * rows * positions,
            transcendentals=0,
        ),
        name="input_gradient",
    )(cot, w, after)


def common_exponent(values, bits):
    lowest = functools.reduce(
        jnp.minimum, [value[-1:].astype(jnp.float32) + bit for value, bit in values]
    )
    return lowest - bits


def scaled_sum(values, lowest):
    return sum(
        value.astype(jnp.float32) * jnp.exp2(lowest - value[-1:].astype(jnp.float32))
        for value, _ in values
    )


def later(value, *gates):
    for gate in gates:
        gate = gate[(0,) * (gate.ndim - 2)]
        value = jnp.where(gate.astype(jnp.float32) > -1e30, value, jnp.zeros_like(value))
    return value


def summed(values, bits, *gates):
    lowest = common_exponent(values, bits)
    total = later(scaled_sum(values, lowest), *gates).astype(jnp.float16)
    return lax.dynamic_update_slice(
        total, lowest.astype(jnp.float16), (total.shape[0] - 1, 0, 0)
    )


def token(value):
    return value[0].astype(jnp.float32)


def on_device(inputs, weight, cotangent):
    x = inputs[0]
    x_held = pltpu.with_memory_space_constraint(x, pltpu.HBM)
    own_cot = cotangent[0]
    w = jnp.transpose(weight, (1, 0, 2))
    taps, rows, outs = w.shape
    own_outs, positions = own_cot.shape
    samples = lax.axis_size("dp")
    chans = lax.axis_size("chan")
    depth = samples // 4
    place = lax.axis_index("dp")
    chan = lax.axis_index("chan")
    core, column, level = place % 2, (place // 2) % 2, place // 4
    core_rows = rows // 2
    core_tiles = core_rows // TILE
    chip_tiles = core_tiles // 2
    shard_tiles = chip_tiles // depth

    def to(value, distance):
        return lax.ppermute(value, "dp", [(i, i ^ distance) for i in range(samples)])

    def to_core(value):
        return to(value, 1)

    def to_column(value):
        return to(value, 2)

    def to_level(value, step):
        return to(value, 4 * step)

    if chans == 2:
        their_cot = lax.ppermute(own_cot, "chan", [(0, 1), (1, 0)])
        parts = (own_cot, their_cot)
        first = chan
    else:
        cot = lax.all_gather(own_cot, "chan", axis=0, tiled=True)
        parts = (cot[:LANES], cot[LANES:])
        first = 0
    other_x = to_core(lax.dynamic_slice_in_dim(x, (1 - core) * core_rows, core_rows, 0))
    where = jnp.stack([core, column * depth + level]).astype(jnp.int32)
    halves, exponents, sends, gathers = [], [], [], []
    bits_of_depth = [1 << shift for shift in range(depth.bit_length() - 1)]
    grad = jnp.zeros((taps, rows // TILE, 2, TILE, LANES), jnp.float16)
    after = own_cot
    for side in range(2):
        part = parts[side]
        if side == 0:
            held_part = pltpu.with_memory_space_constraint(part, pltpu.HBM)
        if side == 1:
            part = later(part, shards[0][-1:, :1, :1])
            their_cot = part
        shards = kernel_grad(
            where, depth, x_held, other_x, part if side else held_part, to_core(part), after
        )
        held = [None] * depth
        gates = ()
        for message in (1, 0):
            sent = later(shards[depth + message], *gates).astype(jnp.float16)
            came = to_column(sent)
            gates = (sent,)
            for slot in range(depth // 2 - 1, -1, -1):
                step = message * (depth // 2) + slot
                held[step] = [(shards[step], 0.0), (came[slot], 0.0)]
        after = sent[0, 0].astype(jnp.float32)
        bits = 1.0
        gates = (sends[-1],) if side else ()
        for bit in bits_of_depth:
            for step in range(depth - bit, 0, -2 * bit):
                pair = summed(held[step], bits, *gates)
                held[step ^ bit].append((to_level(pair, bit), bits))
                gates = (pair, halves[0]) if side and step == 1 else (pair,)
                sends.append(pair)
                if side and step == depth - 1:
                    total = forward(x, w, token(pair))
                    gates += (total[:TILE, :LANES],)
            bits += 1.0
        lowest = common_exponent(held[0], bits)
        kept = scaled_sum(held[0], lowest)[:-1]
        kept = later(kept, gathers[0][1]) if side else kept
        shard = kept.astype(jnp.float16).reshape(taps, shard_tiles, 1, TILE, LANES)
        halves.append(shard)
        exponents.append(lowest)
        near = [shard] + [None] * (depth - 1)
        for bit in bits_of_depth[::-1]:
            near[bit] = to_level(shard, bit)
        gathers.append((near, to_column(shard)))

    for side, (near, own) in enumerate(gathers):
        for step in range(1, depth):
            if near[step] is None:
                low = step & -step
                near[step] = to_level(near[step ^ low], low)
        steps = list(range(depth))
        cuts = [steps[1:2], steps[2:]] if side == 0 else [steps[1:-1], steps[-1:]]
        here = [jnp.stack([near[step] for step in cut]) for cut in cuts]
        there = [to_column(values) for values in here]
        if side == 0:
            returned = there[1]
        here, there = [near[0][None]] + here, [own[None]] + there
        pieces = [(column, step, near[step]) for step in steps]
        arrivals = [(steps[0], own)] + [
            (step, values[slot])
            for cut, values in zip(cuts, there[1:])
            for slot, step in enumerate(cut)
        ]
        pieces += [(1 - column, step, value) for step, value in arrivals]
        if side == 0:
            messages = [(pieces, jnp.concatenate(here + there))]
        else:
            messages = [
                (pieces[:-1], jnp.concatenate(here + there[:-1])),
                (pieces[-1:], there[-1]),
            ]
        lane = first if side == 0 else 1 - first
        for listed, message in messages:
            across = to_core(message)
            for slot, (chip, step, piece) in enumerate(listed):
                row = chip * chip_tiles + (level ^ step) * shard_tiles
                for base, value in ((core, piece), (1 - core, across[slot])):
                    grad = lax.dynamic_update_slice(
                        grad, value, (0, base * core_tiles + row, lane, 0, 0)
                    )
    exponents = [jnp.where(first == side, exponents[0], exponents[1]) for side in range(2)]
    exponent = jnp.concatenate(exponents, 0)
    other = to_core(later(exponent, returned))
    by_core = [jnp.where(core == side, exponent, other) for side in range(2)]
    factor = jnp.exp2(-jnp.stack(by_core)) * (1.0 / samples)
    grad = grad.reshape(taps, 2, core_tiles, 2, TILE, LANES).astype(jnp.float32)
    grad = (grad * factor[None, :, None]).reshape(taps, rows // TILE, 2, TILE, LANES)
    weight_grad = jnp.transpose(grad, (1, 3, 0, 2, 4)).reshape(rows, taps, outs)

    if chans == 2:
        mine = lax.dynamic_slice_in_dim(total, chan * own_outs, own_outs, 0)
        theirs = lax.dynamic_slice_in_dim(total, (1 - chan) * own_outs, own_outs, 0)
        theirs = jnp.where(token(halves[1][0, 0])[0, 0] > -1e30, theirs, 0.0)
        result = mine + lax.ppermute(theirs, "chan", [(0, 1), (1, 0)])
        cot = jnp.where(
            chan == 0,
            jnp.concatenate([own_cot, their_cot], 0),
            jnp.concatenate([their_cot, own_cot], 0),
        )
    else:
        result = lax.psum_scatter(total, "chan", scatter_dimension=0, tiled=True)
    result = result.astype(jnp.bfloat16)[None]
    input_grad = input_gradient(cot, w, token(returned[0, 0, 0]))[None]
    return (result, input_grad, weight_grad)


def solution(mesh):
    placed = (P("dp", "chan", None), P("chan", None, None), P("dp", "chan", None))
    return jax.shard_map(
        on_device,
        mesh=mesh,
        in_specs=placed,
        out_specs=(P("dp", "chan", None), P("dp", "chan", None), P("chan", None, None)),
        check_vma=False,
    )
```

```python
import functools

import jax
import jax.numpy as jnp
from jax import lax
from jax.experimental import pallas as pl
from jax.experimental.pallas import tpu as pltpu
from jax.sharding import PartitionSpec as P

DILATION_RATE = 12
MAP_HEIGHT = 16
MAP_WIDTH = 72
HW = MAP_HEIGHT * MAP_WIDTH
REACH = (MAP_HEIGHT - DILATION_RATE) * MAP_WIDTH
WINDOW = 384
PAD = WINDOW - REACH
COLUMN_SHIFTS = (-DILATION_RATE, 0, DILATION_RATE)
VMEM_LIMIT = 16 * 1024 * 1024


def column_mask(start, width, shift):
    position = lax.broadcasted_iota(jnp.int32, (1, width), 1) + start
    column = lax.rem(position, MAP_WIDTH) + shift
    return position, (column >= 0) & (column < MAP_WIDTH)


def moved(values, amount):
    amount = amount % values.shape[1]
    return values if amount == 0 else pltpu.roll(values, amount, 1)


def moved_cotangent(cot, group, shift):
    if group == 1:
        _, inside = column_mask(0, HW, -shift)
        values = moved(cot, shift)
    elif group == 0:
        position, inside = column_mask(0, WINDOW, -shift)
        inside = inside & (position < REACH)
        values = moved(cot[:, HW - WINDOW :], shift - PAD)
    else:
        position, inside = column_mask(HW - WINDOW, WINDOW, -shift)
        inside = inside & (position >= HW - REACH)
        values = moved(cot[:, :WINDOW], PAD + shift)
    return jnp.where(inside, values, 0.0).astype(jnp.bfloat16)


def window(group):
    return (slice(0, WINDOW), slice(0, HW), slice(HW - WINDOW, HW))[group]


TILE = 8
LANES = 128
TOP = 30000.0


def kernel_grad_kernel(depth, place_ref, own_x, other_x, own_cot, other_cot, _, *refs):
    near, far = refs[:depth], refs[depth : depth + 2]
    sums, peak_ref = refs[depth + 2 :]
    step = pl.program_id(0)
    rows, width = own_x.shape[0], own_cot.shape[0]
    shards = 2 * depth
    shard_rows = rows // shards
    tiles = shard_rows // TILE
    lanes = width // LANES

    @pl.when(step == 0)
    def _():
        peak_ref[...] = jnp.zeros(peak_ref.shape, jnp.float32)

    for group in range(3):

        @pl.when(step == group)
        def _(group=group):
            where = window(group)
            total = None
            for x_ref, cot_ref in ((own_x, own_cot), (other_x, other_cot)):
                cot = cot_ref[...].astype(jnp.float32)
                cots = [moved_cotangent(cot, group, shift) for shift in COLUMN_SHIFTS]
                term = lax.dot_general(
                    x_ref[:, where],
                    jnp.concatenate(cots, 0),
                    (((1,), (1,)), ((), ())),
                    preferred_element_type=jnp.float32,
                )
                total = term if total is None else total + term
            peak_ref[...] = jnp.maximum(
                peak_ref[...], jnp.max(jnp.abs(total), axis=0, keepdims=True)
            )
            for column in range(3):
                for shard in range(shards):
                    for tile in range(tiles):
                        for lane in range(lanes):
                            row = shard * shard_rows + tile * TILE
                            first = column * width + lane * LANES
                            slot = ((3 * group + column) * tiles + tile) * lanes + lane
                            sums[shard, slot] = total[row : row + TILE, first : first + LANES]

    @pl.when(step == 2)
    def _():
        peak = jnp.max(peak_ref[...], axis=1, keepdims=True)
        exponent = jnp.floor(jnp.log2(TOP / jnp.maximum(peak, 1e-30)))
        exponent = jnp.broadcast_to(exponent, (TILE, LANES))
        scale = jnp.exp2(exponent)
        count = sums.shape[1]
        for distance in range(shards):
            if distance < depth:
                out = near[distance]
            else:
                message, slot = divmod(distance - depth, depth // 2)
                out = far[message].at[slot]
            out[:count] = sums[place_ref[1] ^ distance] * scale
            out[count] = exponent


def kernel_grad(place, depth, x, other_x, own_cot, other_cot, after):
    rows, positions = other_x.shape
    outs = own_cot.shape[0]
    tiles = 9 * rows * outs // (2 * depth * TILE * LANES)
    whole = lambda g, h: (0, 0)
    once = pl.Buffered(1)
    shapes = [(tiles + 1, TILE, LANES)] * depth + [(depth // 2, tiles + 1, TILE, LANES)] * 2
    return pl.pallas_call(
        functools.partial(kernel_grad_kernel, depth),
        out_shape=[jax.ShapeDtypeStruct(shape, jnp.float32) for shape in shapes],
        grid_spec=pltpu.PrefetchScalarGridSpec(
            num_scalar_prefetch=1,
            grid=(3,),
            in_specs=[
                pl.BlockSpec((rows, positions), lambda g, h: (h[0], 0), pipeline_mode=once),
                pl.BlockSpec((rows, positions), whole, pipeline_mode=once),
                pl.BlockSpec((outs, positions), whole, pipeline_mode=once),
                pl.BlockSpec((outs, positions), whole, pipeline_mode=once),
                pl.BlockSpec(memory_space=pl.ANY),
            ],
            out_specs=[
                pl.BlockSpec(shape, functools.partial(lambda n, g, h: (0,) * n, len(shape)))
                for shape in shapes
            ],
            scratch_shapes=[
                pltpu.VMEM((2 * depth, tiles, TILE, LANES), jnp.float32),
                pltpu.VMEM((1, 3 * outs), jnp.float32),
            ],
        ),
        compiler_params=pltpu.CompilerParams(vmem_limit_bytes=VMEM_LIMIT),
        cost_estimate=pl.CostEstimate(
            flops=4 * rows * outs * 3 * (HW + 2 * WINDOW),
            bytes_accessed=4 * rows * positions + 4 * outs * positions + 36 * rows * outs,
            transcendentals=0,
        ),
        name="kernel_grad",
    )(place, x, other_x, own_cot, other_cot, after)


def forward_kernel(x_ref, w_ref, _, out_ref):
    step = pl.program_id(0)
    for group in range(3):

        @pl.when(step == group)
        def _(group=group):
            where = window(group)
            total = None
            for column, shift in enumerate(COLUMN_SHIFTS):
                term = lax.dot_general(
                    w_ref[column],
                    x_ref[:, where],
                    (((0,), (0,)), ((), ())),
                    preferred_element_type=jnp.float32,
                )
                if group == 1:
                    _, inside = column_mask(0, HW, shift)
                    term = moved(term, -shift)
                elif group == 0:
                    position, inside = column_mask(HW - WINDOW, WINDOW, shift)
                    inside = inside & (position >= HW - REACH)
                    term = moved(term, PAD - shift)
                else:
                    position, inside = column_mask(0, WINDOW, shift)
                    inside = inside & (position < REACH)
                    term = moved(term, -PAD - shift)
                term = jnp.where(inside, term, 0.0)
                total = term if total is None else total + term
            if group == 0:
                out_ref[:, : HW - WINDOW] = jnp.zeros((out_ref.shape[0], HW - WINDOW), jnp.float32)
                out_ref[:, HW - WINDOW :] = total
            elif group == 1:
                out_ref[...] += total
            else:
                out_ref[:, :WINDOW] += total


def forward(x, w, after):
    rows, positions = x.shape
    outs = w.shape[2]
    return pl.pallas_call(
        forward_kernel,
        out_shape=jax.ShapeDtypeStruct((outs, positions), jnp.float32),
        grid=(3,),
        in_specs=[
            pl.BlockSpec((rows, positions), lambda g: (0, 0), pipeline_mode=pl.Buffered(1)),
            pl.BlockSpec((3, rows, outs), lambda g: (g, 0, 0)),
            pl.BlockSpec(memory_space=pl.ANY),
        ],
        out_specs=pl.BlockSpec((outs, positions), lambda g: (0, 0)),
        compiler_params=pltpu.CompilerParams(vmem_limit_bytes=VMEM_LIMIT),
        cost_estimate=pl.CostEstimate(
            flops=2 * rows * outs * 3 * (HW + 2 * WINDOW),
            bytes_accessed=2 * rows * positions + 18 * rows * outs + 4 * outs * positions,
            transcendentals=0,
        ),
        name="forward",
    )(x, w, after)


def input_grad_kernel(cot_ref, w_ref, _, out_ref, middle, upper, lower):
    @pl.when(pl.program_id(0) == 0)
    def _():
        cot = cot_ref[...].astype(jnp.float32)
        for group, held in enumerate((upper, middle, lower)):
            for column, shift in enumerate(COLUMN_SHIFTS):
                held[column] = moved_cotangent(cot, group, shift)

    def products(group, held):
        total = None
        for column in range(3):
            term = jnp.dot(
                w_ref[3 * group + column], held[column], preferred_element_type=jnp.float32
            )
            total = term if total is None else total + term
        return total

    edge = HW - WINDOW
    centre = products(1, middle)
    out_ref[:, :WINDOW] = (centre[:, :WINDOW] + products(0, upper)).astype(jnp.bfloat16)
    out_ref[:, WINDOW:edge] = centre[:, WINDOW:edge].astype(jnp.bfloat16)
    out_ref[:, edge:] = (centre[:, edge:] + products(2, lower)).astype(jnp.bfloat16)


def input_gradient(cot, w, after):
    outs, positions = cot.shape
    rows = w.shape[1]
    block = min(rows, 256)
    return pl.pallas_call(
        input_grad_kernel,
        out_shape=jax.ShapeDtypeStruct((rows, positions), jnp.bfloat16),
        grid=(rows // block,),
        in_specs=[
            pl.BlockSpec((outs, positions), lambda g: (0, 0)),
            pl.BlockSpec((9, block, outs), lambda g: (0, g, 0)),
            pl.BlockSpec(memory_space=pl.ANY),
        ],
        out_specs=pl.BlockSpec((block, positions), lambda g: (g, 0)),
        scratch_shapes=[
            pltpu.VMEM((3, outs, HW), jnp.bfloat16),
            pltpu.VMEM((3, outs, WINDOW), jnp.bfloat16),
            pltpu.VMEM((3, outs, WINDOW), jnp.bfloat16),
        ],
        compiler_params=pltpu.CompilerParams(vmem_limit_bytes=VMEM_LIMIT),
        cost_estimate=pl.CostEstimate(
            flops=2 * rows * outs * 3 * (HW + 2 * WINDOW),
            bytes_accessed=2 * outs * positions + 18 * rows * outs + 2 * rows * positions,
            transcendentals=0,
        ),
        name="input_gradient",
    )(cot, w, after)


def common_exponent(values, bits):
    lowest = functools.reduce(
        jnp.minimum, [value[-1:].astype(jnp.float32) + bit for value, bit in values]
    )
    return lowest - bits


def scaled_sum(values, lowest):
    return sum(
        value.astype(jnp.float32) * jnp.exp2(lowest - value[-1:].astype(jnp.float32))
        for value, _ in values
    )


def later(value, *gates):
    for gate in gates:
        gate = gate[(0,) * (gate.ndim - 2)]
        value = jnp.where(gate.astype(jnp.float32) > -1e30, value, jnp.zeros_like(value))
    return value


def summed(values, bits, *gates):
    lowest = common_exponent(values, bits)
    total = later(scaled_sum(values, lowest), *gates).astype(jnp.float16)
    return lax.dynamic_update_slice(
        total, lowest.astype(jnp.float16), (total.shape[0] - 1, 0, 0)
    )


def token(value):
    return value[0].astype(jnp.float32)


def on_device(inputs, weight, cotangent):
    x = inputs[0]
    x_held = pltpu.with_memory_space_constraint(x, pltpu.HBM)
    own_cot = cotangent[0]
    w = jnp.transpose(weight, (1, 0, 2))
    taps, rows, outs = w.shape
    own_outs, positions = own_cot.shape
    samples = lax.axis_size("dp")
    chans = lax.axis_size("chan")
    depth = samples // 4
    place = lax.axis_index("dp")
    chan = lax.axis_index("chan")
    core, column, level = place % 2, (place // 2) % 2, place // 4
    core_rows = rows // 2
    core_tiles = core_rows // TILE
    chip_tiles = core_tiles // 2
    shard_tiles = chip_tiles // depth

    def to(value, distance):
        return lax.ppermute(value, "dp", [(i, i ^ distance) for i in range(samples)])

    def to_core(value):
        return to(value, 1)

    def to_column(value):
        return to(value, 2)

    def to_level(value, step):
        return to(value, 4 * step)

    if chans == 2:
        their_cot = lax.ppermute(own_cot, "chan", [(0, 1), (1, 0)])
        parts = (own_cot, their_cot)
        first = chan
    else:
        cot = lax.all_gather(own_cot, "chan", axis=0, tiled=True)
        parts = (cot[:LANES], cot[LANES:])
        first = 0
    other_x = to_core(lax.dynamic_slice_in_dim(x, (1 - core) * core_rows, core_rows, 0))
    where = jnp.stack([core, column * depth + level]).astype(jnp.int32)
    halves, exponents, sends, reduced, gathers = [], [], [], [], []
    bits_of_depth = [1 << shift for shift in range(depth.bit_length() - 1)]
    grad = jnp.zeros((taps, rows // TILE, 2, TILE, LANES), jnp.float16)
    after = own_cot
    for side in range(2):
        part = parts[side]
        if side == 0:
            held_part = pltpu.with_memory_space_constraint(part, pltpu.HBM)
        if side == 1:
            part = later(part, shards[0][-1:, :1, :1])
            their_cot = part
        shards = kernel_grad(
            where, depth, x_held, other_x, part if side else held_part, to_core(part), after
        )
        held = [None] * depth
        gates = ()
        for message in (1, 0):
            sent = later(shards[depth + message], *gates).astype(jnp.float16)
            came = to_column(sent)
            gates = (sent,)
            for slot in range(depth // 2 - 1, -1, -1):
                step = message * (depth // 2) + slot
                held[step] = [(shards[step], 0.0), (came[slot], 0.0)]
        after = sent[0, 0].astype(jnp.float32)
        bits = 1.0
        gates = (sends[-1],) if side else ()
        for bit in bits_of_depth:
            for step in range(depth - bit, 0, -2 * bit):
                pair = summed(held[step], bits, *gates)
                held[step ^ bit].append((to_level(pair, bit), bits))
                gates = (pair,)
                sends.append(pair)
                if side and step == depth - 1:
                    total = forward(x, w, token(pair))
                    gates += (total[:TILE, :LANES],)
            bits += 1.0
        reduced.append((held[0], bits))

    for side, (values, bits) in enumerate(reduced):
        lowest = common_exponent(values, bits)
        gate = gathers[0][1] if side else sends[-1]
        kept = later(scaled_sum(values, lowest)[:-1], gate)
        shard = kept.astype(jnp.float16).reshape(taps, shard_tiles, 1, TILE, LANES)
        halves.append(shard)
        exponents.append(later(lowest, shard))
        near = [shard] + [None] * (depth - 1)
        for bit in bits_of_depth[::-1]:
            near[bit] = to_level(shard, bit)
        gathers.append((near, to_column(shard)))

    for side, (near, own) in enumerate(gathers):
        for step in range(1, depth):
            if near[step] is None:
                low = step & -step
                near[step] = to_level(near[step ^ low], low)
        steps = list(range(depth))
        cuts = [steps[1:2], steps[2:]] if side == 0 else [steps[1:-1], steps[-1:]]
        here = [jnp.stack([near[step] for step in cut]) for cut in cuts]
        there = [to_column(values) for values in here]
        if side == 0:
            returned = there[1]
        here, there = [near[0][None]] + here, [own[None]] + there
        pieces = [(column, step, near[step]) for step in steps]
        arrivals = [(steps[0], own)] + [
            (step, values[slot])
            for cut, values in zip(cuts, there[1:])
            for slot, step in enumerate(cut)
        ]
        pieces += [(1 - column, step, value) for step, value in arrivals]
        if side == 0:
            messages = [(pieces, jnp.concatenate(here + there))]
        else:
            messages = [
                (pieces[:-1], jnp.concatenate(here + there[:-1])),
                (pieces[-1:], there[-1]),
            ]
        lane = first if side == 0 else 1 - first
        for listed, message in messages:
            across = to_core(message)
            for slot, (chip, step, piece) in enumerate(listed):
                row = chip * chip_tiles + (level ^ step) * shard_tiles
                for base, value in ((core, piece), (1 - core, across[slot])):
                    grad = lax.dynamic_update_slice(
                        grad, value, (0, base * core_tiles + row, lane, 0, 0)
                    )
    exponents = [jnp.where(first == side, exponents[0], exponents[1]) for side in range(2)]
    exponent = jnp.concatenate(exponents, 0)
    other = to_core(later(exponent, returned))
    by_core = [jnp.where(core == side, exponent, other) for side in range(2)]
    factor = jnp.exp2(-jnp.stack(by_core)) * (1.0 / samples)
    grad = grad.reshape(taps, 2, core_tiles, 2, TILE, LANES).astype(jnp.float32)
    grad = (grad * factor[None, :, None]).reshape(taps, rows // TILE, 2, TILE, LANES)
    weight_grad = jnp.transpose(grad, (1, 3, 0, 2, 4)).reshape(rows, taps, outs)

    if chans == 2:
        mine = lax.dynamic_slice_in_dim(total, chan * own_outs, own_outs, 0)
        theirs = lax.dynamic_slice_in_dim(total, (1 - chan) * own_outs, own_outs, 0)
        theirs = jnp.where(token(halves[1][0, 0])[0, 0] > -1e30, theirs, 0.0)
        result = mine + lax.ppermute(theirs, "chan", [(0, 1), (1, 0)])
        cot = jnp.where(
            chan == 0,
            jnp.concatenate([own_cot, their_cot], 0),
            jnp.concatenate([their_cot, own_cot], 0),
        )
    else:
        result = lax.psum_scatter(total, "chan", scatter_dimension=0, tiled=True)
    result = result.astype(jnp.bfloat16)[None]
    input_grad = input_gradient(cot, w, token(near[-1][0, 0]))[None]
    return (result, input_grad, weight_grad)


def solution(mesh):
    placed = (P("dp", "chan", None), P("chan", None, None), P("dp", "chan", None))
    return jax.shard_map(
        on_device,
        mesh=mesh,
        in_specs=placed,
        out_specs=(P("dp", "chan", None), P("dp", "chan", None), P("chan", None, None)),
        check_vma=False,
    )
```

```python
import functools

import jax
import jax.numpy as jnp
from jax import lax
from jax.experimental import pallas as pl
from jax.experimental.pallas import tpu as pltpu
from jax.sharding import PartitionSpec as P

DILATION_RATE = 12
MAP_HEIGHT = 16
MAP_WIDTH = 72
HW = MAP_HEIGHT * MAP_WIDTH
REACH = (MAP_HEIGHT - DILATION_RATE) * MAP_WIDTH
WINDOW = 384
PAD = WINDOW - REACH
COLUMN_SHIFTS = (-DILATION_RATE, 0, DILATION_RATE)
VMEM_LIMIT = 16 * 1024 * 1024


def column_mask(start, width, shift):
    position = lax.broadcasted_iota(jnp.int32, (1, width), 1) + start
    column = lax.rem(position, MAP_WIDTH) + shift
    return position, (column >= 0) & (column < MAP_WIDTH)


def moved(values, amount):
    amount = amount % values.shape[1]
    return values if amount == 0 else pltpu.roll(values, amount, 1)


def moved_cotangent(cot, group, shift):
    if group == 1:
        _, inside = column_mask(0, HW, -shift)
        values = moved(cot, shift)
    elif group == 0:
        position, inside = column_mask(0, WINDOW, -shift)
        inside = inside & (position < REACH)
        values = moved(cot[:, HW - WINDOW :], shift - PAD)
    else:
        position, inside = column_mask(HW - WINDOW, WINDOW, -shift)
        inside = inside & (position >= HW - REACH)
        values = moved(cot[:, :WINDOW], PAD + shift)
    return jnp.where(inside, values, 0.0).astype(jnp.bfloat16)


def window(group):
    return (slice(0, WINDOW), slice(0, HW), slice(HW - WINDOW, HW))[group]


TILE = 8
LANES = 128
TOP = 30000.0


def kernel_grad_kernel(depth, place_ref, own_x, other_x, own_cot, other_cot, _, *refs):
    near, far = refs[:depth], refs[depth : depth + 2]
    sums, peak_ref = refs[depth + 2 :]
    step = pl.program_id(0)
    rows, width = own_x.shape[0], own_cot.shape[0]
    shards = 2 * depth
    shard_rows = rows // shards
    tiles = shard_rows // TILE
    lanes = width // LANES

    @pl.when(step == 0)
    def _():
        peak_ref[...] = jnp.zeros(peak_ref.shape, jnp.float32)

    for group in range(3):

        @pl.when(step == group)
        def _(group=group):
            where = window(group)
            total = None
            for x_ref, cot_ref in ((own_x, own_cot), (other_x, other_cot)):
                cot = cot_ref[...].astype(jnp.float32)
                cots = [moved_cotangent(cot, group, shift) for shift in COLUMN_SHIFTS]
                term = lax.dot_general(
                    x_ref[:, where],
                    jnp.concatenate(cots, 0),
                    (((1,), (1,)), ((), ())),
                    preferred_element_type=jnp.float32,
                )
                total = term if total is None else total + term
            peak_ref[...] = jnp.maximum(
                peak_ref[...], jnp.max(jnp.abs(total), axis=0, keepdims=True)
            )
            for column in range(3):
                for shard in range(shards):
                    for tile in range(tiles):
                        for lane in range(lanes):
                            row = shard * shard_rows + tile * TILE
                            first = column * width + lane * LANES
                            slot = ((3 * group + column) * tiles + tile) * lanes + lane
                            sums[shard, slot] = total[row : row + TILE, first : first + LANES]

    @pl.when(step == 2)
    def _():
        peak = jnp.max(peak_ref[...], axis=1, keepdims=True)
        exponent = jnp.floor(jnp.log2(TOP / jnp.maximum(peak, 1e-30)))
        exponent = jnp.broadcast_to(exponent, (TILE, LANES))
        scale = jnp.exp2(exponent)
        count = sums.shape[1]
        for distance in range(shards):
            if distance < depth:
                out = near[distance]
            else:
                message, slot = divmod(distance - depth, depth // 2)
                out = far[message].at[slot]
            out[:count] = sums[place_ref[1] ^ distance] * scale
            out[count] = exponent


def kernel_grad(place, depth, x, other_x, own_cot, other_cot, after):
    rows, positions = other_x.shape
    outs = own_cot.shape[0]
    tiles = 9 * rows * outs // (2 * depth * TILE * LANES)
    whole = lambda g, h: (0, 0)
    once = pl.Buffered(1)
    shapes = [(tiles + 1, TILE, LANES)] * depth + [(depth // 2, tiles + 1, TILE, LANES)] * 2
    return pl.pallas_call(
        functools.partial(kernel_grad_kernel, depth),
        out_shape=[jax.ShapeDtypeStruct(shape, jnp.float32) for shape in shapes],
        grid_spec=pltpu.PrefetchScalarGridSpec(
            num_scalar_prefetch=1,
            grid=(3,),
            in_specs=[
                pl.BlockSpec((rows, positions), lambda g, h: (h[0], 0), pipeline_mode=once),
                pl.BlockSpec((rows, positions), whole, pipeline_mode=once),
                pl.BlockSpec((outs, positions), whole, pipeline_mode=once),
                pl.BlockSpec((outs, positions), whole, pipeline_mode=once),
                pl.BlockSpec(memory_space=pl.ANY),
            ],
            out_specs=[
                pl.BlockSpec(shape, functools.partial(lambda n, g, h: (0,) * n, len(shape)))
                for shape in shapes
            ],
            scratch_shapes=[
                pltpu.VMEM((2 * depth, tiles, TILE, LANES), jnp.float32),
                pltpu.VMEM((1, 3 * outs), jnp.float32),
            ],
        ),
        compiler_params=pltpu.CompilerParams(vmem_limit_bytes=VMEM_LIMIT),
        cost_estimate=pl.CostEstimate(
            flops=4 * rows * outs * 3 * (HW + 2 * WINDOW),
            bytes_accessed=4 * rows * positions + 4 * outs * positions + 36 * rows * outs,
            transcendentals=0,
        ),
        name="kernel_grad",
    )(place, x, other_x, own_cot, other_cot, after)


def forward_kernel(x_ref, w_ref, _, out_ref):
    step = pl.program_id(0)
    for group in range(3):

        @pl.when(step == group)
        def _(group=group):
            where = window(group)
            total = None
            for column, shift in enumerate(COLUMN_SHIFTS):
                term = lax.dot_general(
                    w_ref[column],
                    x_ref[:, where],
                    (((0,), (0,)), ((), ())),
                    preferred_element_type=jnp.float32,
                )
                if group == 1:
                    _, inside = column_mask(0, HW, shift)
                    term = moved(term, -shift)
                elif group == 0:
                    position, inside = column_mask(HW - WINDOW, WINDOW, shift)
                    inside = inside & (position >= HW - REACH)
                    term = moved(term, PAD - shift)
                else:
                    position, inside = column_mask(0, WINDOW, shift)
                    inside = inside & (position < REACH)
                    term = moved(term, -PAD - shift)
                term = jnp.where(inside, term, 0.0)
                total = term if total is None else total + term
            if group == 0:
                out_ref[:, : HW - WINDOW] = jnp.zeros((out_ref.shape[0], HW - WINDOW), jnp.float32)
                out_ref[:, HW - WINDOW :] = total
            elif group == 1:
                out_ref[...] += total
            else:
                out_ref[:, :WINDOW] += total


def forward(x, w, after):
    rows, positions = x.shape
    outs = w.shape[2]
    return pl.pallas_call(
        forward_kernel,
        out_shape=jax.ShapeDtypeStruct((outs, positions), jnp.float32),
        grid=(3,),
        in_specs=[
            pl.BlockSpec((rows, positions), lambda g: (0, 0), pipeline_mode=pl.Buffered(1)),
            pl.BlockSpec((3, rows, outs), lambda g: (g, 0, 0)),
            pl.BlockSpec(memory_space=pl.ANY),
        ],
        out_specs=pl.BlockSpec((outs, positions), lambda g: (0, 0)),
        compiler_params=pltpu.CompilerParams(vmem_limit_bytes=VMEM_LIMIT),
        cost_estimate=pl.CostEstimate(
            flops=2 * rows * outs * 3 * (HW + 2 * WINDOW),
            bytes_accessed=2 * rows * positions + 18 * rows * outs + 4 * outs * positions,
            transcendentals=0,
        ),
        name="forward",
    )(x, w, after)


def input_grad_kernel(cot_ref, w_ref, _, out_ref, middle, upper, lower):
    @pl.when(pl.program_id(0) == 0)
    def _():
        cot = cot_ref[...].astype(jnp.float32)
        for group, held in enumerate((upper, middle, lower)):
            for column, shift in enumerate(COLUMN_SHIFTS):
                held[column] = moved_cotangent(cot, group, shift)

    def products(group, held):
        total = None
        for column in range(3):
            term = jnp.dot(
                w_ref[3 * group + column], held[column], preferred_element_type=jnp.float32
            )
            total = term if total is None else total + term
        return total

    edge = HW - WINDOW
    centre = products(1, middle)
    out_ref[:, :WINDOW] = (centre[:, :WINDOW] + products(0, upper)).astype(jnp.bfloat16)
    out_ref[:, WINDOW:edge] = centre[:, WINDOW:edge].astype(jnp.bfloat16)
    out_ref[:, edge:] = (centre[:, edge:] + products(2, lower)).astype(jnp.bfloat16)


def input_gradient(cot, w, after):
    outs, positions = cot.shape
    rows = w.shape[1]
    block = min(rows, 256)
    return pl.pallas_call(
        input_grad_kernel,
        out_shape=jax.ShapeDtypeStruct((rows, positions), jnp.bfloat16),
        grid=(rows // block,),
        in_specs=[
            pl.BlockSpec((outs, positions), lambda g: (0, 0)),
            pl.BlockSpec((9, block, outs), lambda g: (0, g, 0)),
            pl.BlockSpec(memory_space=pl.ANY),
        ],
        out_specs=pl.BlockSpec((block, positions), lambda g: (g, 0)),
        scratch_shapes=[
            pltpu.VMEM((3, outs, HW), jnp.bfloat16),
            pltpu.VMEM((3, outs, WINDOW), jnp.bfloat16),
            pltpu.VMEM((3, outs, WINDOW), jnp.bfloat16),
        ],
        compiler_params=pltpu.CompilerParams(vmem_limit_bytes=VMEM_LIMIT),
        cost_estimate=pl.CostEstimate(
            flops=2 * rows * outs * 3 * (HW + 2 * WINDOW),
            bytes_accessed=2 * outs * positions + 18 * rows * outs + 2 * rows * positions,
            transcendentals=0,
        ),
        name="input_gradient",
    )(cot, w, after)


def common_exponent(values, bits):
    lowest = functools.reduce(
        jnp.minimum, [value[-1:].astype(jnp.float32) + bit for value, bit in values]
    )
    return lowest - bits


def scaled_sum(values, lowest):
    return sum(
        value.astype(jnp.float32) * jnp.exp2(lowest - value[-1:].astype(jnp.float32))
        for value, _ in values
    )


def later(value, *gates):
    for gate in gates:
        gate = gate[(0,) * (gate.ndim - 2)]
        value = jnp.where(gate.astype(jnp.float32) > -1e30, value, jnp.zeros_like(value))
    return value


def summed(values, bits, *gates):
    lowest = common_exponent(values, bits)
    total = later(scaled_sum(values, lowest), *gates).astype(jnp.float16)
    return lax.dynamic_update_slice(
        total, lowest.astype(jnp.float16), (total.shape[0] - 1, 0, 0)
    )


def token(value):
    return value[0].astype(jnp.float32)


def on_device(inputs, weight, cotangent):
    x = inputs[0]
    x_held = pltpu.with_memory_space_constraint(x, pltpu.HBM)
    own_cot = cotangent[0]
    w = jnp.transpose(weight, (1, 0, 2))
    taps, rows, outs = w.shape
    own_outs, positions = own_cot.shape
    samples = lax.axis_size("dp")
    chans = lax.axis_size("chan")
    depth = samples // 4
    place = lax.axis_index("dp")
    chan = lax.axis_index("chan")
    core, column, level = place % 2, (place // 2) % 2, place // 4
    core_rows = rows // 2
    core_tiles = core_rows // TILE
    chip_tiles = core_tiles // 2
    shard_tiles = chip_tiles // depth

    def to(value, distance):
        return lax.ppermute(value, "dp", [(i, i ^ distance) for i in range(samples)])

    def to_core(value):
        return to(value, 1)

    def to_column(value):
        return to(value, 2)

    def to_level(value, step):
        return to(value, 4 * step)

    if chans == 2:
        their_cot = lax.ppermute(own_cot, "chan", [(0, 1), (1, 0)])
        parts = (own_cot, their_cot)
        first = chan
    else:
        cot = lax.all_gather(own_cot, "chan", axis=0, tiled=True)
        parts = (cot[:LANES], cot[LANES:])
        first = 0
    other_x = to_core(lax.dynamic_slice_in_dim(x, (1 - core) * core_rows, core_rows, 0))
    where = jnp.stack([core, column * depth + level]).astype(jnp.int32)
    halves, exponents, sends, reduced, gathers = [], [], [], [], []
    bits_of_depth = [1 << shift for shift in range(depth.bit_length() - 1)]
    grad = jnp.zeros((taps, rows // TILE, 2, TILE, LANES), jnp.float16)
    after = own_cot
    for side in range(2):
        part = parts[side]
        if side == 0:
            held_part = pltpu.with_memory_space_constraint(part, pltpu.HBM)
        if side == 1:
            part = later(part, shards[0][-1:, :1, :1])
            their_cot = part
        shards = kernel_grad(
            where, depth, x_held, other_x, part if side else held_part, to_core(part), after
        )
        held = [None] * depth
        gates = ()
        for message in (1, 0):
            sent = later(shards[depth + message], *gates).astype(jnp.float16)
            came = to_column(sent)
            gates = (sent,)
            for slot in range(depth // 2 - 1, -1, -1):
                step = message * (depth // 2) + slot
                held[step] = [(shards[step], 0.0), (came[slot], 0.0)]
        after = sent[0, 0].astype(jnp.float32)
        bits = 1.0
        gates = (sends[-1],) if side else ()
        for bit in bits_of_depth:
            for step in range(depth - bit, 0, -2 * bit):
                pair = summed(held[step], bits, *gates)
                held[step ^ bit].append((to_level(pair, bit), bits))
                gates = (pair,)
                sends.append(pair)
                if side and step == depth - 1:
                    total = forward(x, w, token(pair))
                    gates += (total[:TILE, :LANES],)
            bits += 1.0
        reduced.append((held[0], bits))

    for side, (values, bits) in enumerate(reduced):
        lowest = common_exponent(values, bits)
        gates = (gathers[0][1], input_grad[:TILE, :LANES]) if side else (sends[-1],)
        kept = later(scaled_sum(values, lowest)[:-1], *gates)
        shard = kept.astype(jnp.float16).reshape(taps, shard_tiles, 1, TILE, LANES)
        halves.append(shard)
        exponents.append(later(lowest, shard))
        near = [shard] + [None] * (depth - 1)
        for bit in bits_of_depth[::-1]:
            near[bit] = to_level(shard, bit)
        gathers.append((near, to_column(shard)))
        if side == 0:
            if chans == 2:
                cot = jnp.where(
                    chan == 0,
                    jnp.concatenate([own_cot, their_cot], 0),
                    jnp.concatenate([their_cot, own_cot], 0),
                )
            input_grad = input_gradient(cot, w, token(shard[0, 0]))

    if chans == 2:
        mine = lax.dynamic_slice_in_dim(total, chan * own_outs, own_outs, 0)
        theirs = lax.dynamic_slice_in_dim(total, (1 - chan) * own_outs, own_outs, 0)
        theirs = jnp.where(token(halves[1][0, 0])[0, 0] > -1e30, theirs, 0.0)
        result = mine + lax.ppermute(theirs, "chan", [(0, 1), (1, 0)])
    else:
        result = lax.psum_scatter(total, "chan", scatter_dimension=0, tiled=True)
    result = result.astype(jnp.bfloat16)[None]

    for side, (near, own) in enumerate(gathers):
        for step in range(1, depth):
            if near[step] is None:
                low = step & -step
                near[step] = to_level(near[step ^ low], low)
        steps = list(range(depth))
        cuts = [steps[1:2], steps[2:]] if side == 0 else [steps[1:-1], steps[-1:]]
        here = [jnp.stack([near[step] for step in cut]) for cut in cuts]
        there = [to_column(values) for values in here]
        if side == 0:
            returned = there[1]
        here, there = [near[0][None]] + here, [own[None]] + there
        pieces = [(column, step, near[step]) for step in steps]
        arrivals = [(steps[0], own)] + [
            (step, values[slot])
            for cut, values in zip(cuts, there[1:])
            for slot, step in enumerate(cut)
        ]
        pieces += [(1 - column, step, value) for step, value in arrivals]
        if side == 0:
            messages = [(pieces, jnp.concatenate(here + there))]
        else:
            there[-1] = later(there[-1], grad, result.reshape(-1, TILE, LANES))
            messages = [
                (pieces[:-1], jnp.concatenate(here + there[:-1])),
                (pieces[-1:], there[-1]),
            ]
        lane = first if side == 0 else 1 - first
        for listed, message in messages:
            across = to_core(message)
            for slot, (chip, step, piece) in enumerate(listed):
                row = chip * chip_tiles + (level ^ step) * shard_tiles
                for base, value in ((core, piece), (1 - core, across[slot])):
                    grad = lax.dynamic_update_slice(
                        grad, value, (0, base * core_tiles + row, lane, 0, 0)
                    )
    exponents = [jnp.where(first == side, exponents[0], exponents[1]) for side in range(2)]
    exponent = jnp.concatenate(exponents, 0)
    other = to_core(later(exponent, returned))
    by_core = [jnp.where(core == side, exponent, other) for side in range(2)]
    factor = jnp.exp2(-jnp.stack(by_core)) * (1.0 / samples)
    grad = grad.reshape(taps, 2, core_tiles, 2, TILE, LANES).astype(jnp.float32)
    grad = (grad * factor[None, :, None]).reshape(taps, rows // TILE, 2, TILE, LANES)
    weight_grad = jnp.transpose(grad, (1, 3, 0, 2, 4)).reshape(rows, taps, outs)

    return (result, input_grad[None], weight_grad)


def solution(mesh):
    placed = (P("dp", "chan", None), P("chan", None, None), P("dp", "chan", None))
    return jax.shard_map(
        on_device,
        mesh=mesh,
        in_specs=placed,
        out_specs=(P("dp", "chan", None), P("dp", "chan", None), P("chan", None, None)),
        check_vma=False,
    )
```

```python
import functools

import jax
import jax.numpy as jnp
from jax import lax
from jax.experimental import pallas as pl
from jax.experimental.pallas import tpu as pltpu
from jax.sharding import PartitionSpec as P

DILATION_RATE = 12
MAP_HEIGHT = 16
MAP_WIDTH = 72
HW = MAP_HEIGHT * MAP_WIDTH
REACH = (MAP_HEIGHT - DILATION_RATE) * MAP_WIDTH
WINDOW = 384
PAD = WINDOW - REACH
COLUMN_SHIFTS = (-DILATION_RATE, 0, DILATION_RATE)
VMEM_LIMIT = 16 * 1024 * 1024


def column_mask(start, width, shift):
    position = lax.broadcasted_iota(jnp.int32, (1, width), 1) + start
    column = lax.rem(position, MAP_WIDTH) + shift
    return position, (column >= 0) & (column < MAP_WIDTH)


def moved(values, amount):
    amount = amount % values.shape[1]
    return values if amount == 0 else pltpu.roll(values, amount, 1)


def moved_cotangent(cot, group, shift):
    if group == 1:
        _, inside = column_mask(0, HW, -shift)
        values = moved(cot, shift)
    elif group == 0:
        position, inside = column_mask(0, WINDOW, -shift)
        inside = inside & (position < REACH)
        values = moved(cot[:, HW - WINDOW :], shift - PAD)
    else:
        position, inside = column_mask(HW - WINDOW, WINDOW, -shift)
        inside = inside & (position >= HW - REACH)
        values = moved(cot[:, :WINDOW], PAD + shift)
    return jnp.where(inside, values, 0.0).astype(jnp.bfloat16)


def window(group):
    return (slice(0, WINDOW), slice(0, HW), slice(HW - WINDOW, HW))[group]


TILE = 8
LANES = 128
TOP = 30000.0


def kernel_grad_kernel(depth, place_ref, own_x, other_x, own_cot, other_cot, _, *refs):
    near, far = refs[:depth], refs[depth : depth + 2]
    sums, peak_ref = refs[depth + 2 :]
    step = pl.program_id(0)
    rows, width = own_x.shape[0], own_cot.shape[0]
    shards = 2 * depth
    shard_rows = rows // shards
    tiles = shard_rows // TILE
    lanes = width // LANES

    @pl.when(step == 0)
    def _():
        peak_ref[...] = jnp.zeros(peak_ref.shape, jnp.float32)

    for group in range(3):

        @pl.when(step == group)
        def _(group=group):
            where = window(group)
            total = None
            for x_ref, cot_ref in ((own_x, own_cot), (other_x, other_cot)):
                cot = cot_ref[...].astype(jnp.float32)
                cots = [moved_cotangent(cot, group, shift) for shift in COLUMN_SHIFTS]
                term = lax.dot_general(
                    x_ref[:, where],
                    jnp.concatenate(cots, 0),
                    (((1,), (1,)), ((), ())),
                    preferred_element_type=jnp.float32,
                )
                total = term if total is None else total + term
            peak_ref[...] = jnp.maximum(
                peak_ref[...], jnp.max(jnp.abs(total), axis=0, keepdims=True)
            )
            for column in range(3):
                for shard in range(shards):
                    for tile in range(tiles):
                        for lane in range(lanes):
                            row = shard * shard_rows + tile * TILE
                            first = column * width + lane * LANES
                            slot = ((3 * group + column) * tiles + tile) * lanes + lane
                            sums[shard, slot] = total[row : row + TILE, first : first + LANES]

    @pl.when(step == 2)
    def _():
        peak = jnp.max(peak_ref[...], axis=1, keepdims=True)
        exponent = jnp.floor(jnp.log2(TOP / jnp.maximum(peak, 1e-30)))
        exponent = jnp.broadcast_to(exponent, (TILE, LANES))
        scale = jnp.exp2(exponent)
        count = sums.shape[1]
        for distance in range(shards):
            if distance < depth:
                out = near[distance]
            else:
                message, slot = divmod(distance - depth, depth // 2)
                out = far[message].at[slot]
            out[:count] = sums[place_ref[1] ^ distance] * scale
            out[count] = exponent


def kernel_grad(place, depth, x, other_x, own_cot, other_cot, after):
    rows, positions = other_x.shape
    outs = own_cot.shape[0]
    tiles = 9 * rows * outs // (2 * depth * TILE * LANES)
    whole = lambda g, h: (0, 0)
    once = pl.Buffered(1)
    shapes = [(tiles + 1, TILE, LANES)] * depth + [(depth // 2, tiles + 1, TILE, LANES)] * 2
    return pl.pallas_call(
        functools.partial(kernel_grad_kernel, depth),
        out_shape=[jax.ShapeDtypeStruct(shape, jnp.float32) for shape in shapes],
        grid_spec=pltpu.PrefetchScalarGridSpec(
            num_scalar_prefetch=1,
            grid=(3,),
            in_specs=[
                pl.BlockSpec((rows, positions), lambda g, h: (h[0], 0), pipeline_mode=once),
                pl.BlockSpec((rows, positions), whole, pipeline_mode=once),
                pl.BlockSpec((outs, positions), whole, pipeline_mode=once),
                pl.BlockSpec((outs, positions), whole, pipeline_mode=once),
                pl.BlockSpec(memory_space=pl.ANY),
            ],
            out_specs=[
                pl.BlockSpec(shape, functools.partial(lambda n, g, h: (0,) * n, len(shape)))
                for shape in shapes
            ],
            scratch_shapes=[
                pltpu.VMEM((2 * depth, tiles, TILE, LANES), jnp.float32),
                pltpu.VMEM((1, 3 * outs), jnp.float32),
            ],
        ),
        compiler_params=pltpu.CompilerParams(vmem_limit_bytes=VMEM_LIMIT),
        cost_estimate=pl.CostEstimate(
            flops=4 * rows * outs * 3 * (HW + 2 * WINDOW),
            bytes_accessed=4 * rows * positions + 4 * outs * positions + 36 * rows * outs,
            transcendentals=0,
        ),
        name="kernel_grad",
    )(place, x, other_x, own_cot, other_cot, after)


def forward_kernel(x_ref, w_ref, _, out_ref):
    step = pl.program_id(0)
    for group in range(3):

        @pl.when(step == group)
        def _(group=group):
            where = window(group)
            total = None
            for column, shift in enumerate(COLUMN_SHIFTS):
                term = lax.dot_general(
                    w_ref[column],
                    x_ref[:, where],
                    (((0,), (0,)), ((), ())),
                    preferred_element_type=jnp.float32,
                )
                if group == 1:
                    _, inside = column_mask(0, HW, shift)
                    term = moved(term, -shift)
                elif group == 0:
                    position, inside = column_mask(HW - WINDOW, WINDOW, shift)
                    inside = inside & (position >= HW - REACH)
                    term = moved(term, PAD - shift)
                else:
                    position, inside = column_mask(0, WINDOW, shift)
                    inside = inside & (position < REACH)
                    term = moved(term, -PAD - shift)
                term = jnp.where(inside, term, 0.0)
                total = term if total is None else total + term
            if group == 0:
                out_ref[:, : HW - WINDOW] = jnp.zeros((out_ref.shape[0], HW - WINDOW), jnp.float32)
                out_ref[:, HW - WINDOW :] = total
            elif group == 1:
                out_ref[...] += total
            else:
                out_ref[:, :WINDOW] += total


def forward(x, w, after):
    rows, positions = x.shape
    outs = w.shape[2]
    return pl.pallas_call(
        forward_kernel,
        out_shape=jax.ShapeDtypeStruct((outs, positions), jnp.float32),
        grid=(3,),
        in_specs=[
            pl.BlockSpec((rows, positions), lambda g: (0, 0), pipeline_mode=pl.Buffered(1)),
            pl.BlockSpec((3, rows, outs), lambda g: (g, 0, 0)),
            pl.BlockSpec(memory_space=pl.ANY),
        ],
        out_specs=pl.BlockSpec((outs, positions), lambda g: (0, 0)),
        compiler_params=pltpu.CompilerParams(vmem_limit_bytes=VMEM_LIMIT),
        cost_estimate=pl.CostEstimate(
            flops=2 * rows * outs * 3 * (HW + 2 * WINDOW),
            bytes_accessed=2 * rows * positions + 18 * rows * outs + 4 * outs * positions,
            transcendentals=0,
        ),
        name="forward",
    )(x, w, after)


def input_grad_kernel(cot_ref, w_ref, _, out_ref, middle, upper, lower):
    @pl.when(pl.program_id(0) == 0)
    def _():
        cot = cot_ref[...].astype(jnp.float32)
        for group, held in enumerate((upper, middle, lower)):
            for column, shift in enumerate(COLUMN_SHIFTS):
                held[column] = moved_cotangent(cot, group, shift)

    def products(group, held):
        total = None
        for column in range(3):
            term = jnp.dot(
                w_ref[3 * group + column], held[column], preferred_element_type=jnp.float32
            )
            total = term if total is None else total + term
        return total

    edge = HW - WINDOW
    centre = products(1, middle)
    out_ref[:, :WINDOW] = (centre[:, :WINDOW] + products(0, upper)).astype(jnp.bfloat16)
    out_ref[:, WINDOW:edge] = centre[:, WINDOW:edge].astype(jnp.bfloat16)
    out_ref[:, edge:] = (centre[:, edge:] + products(2, lower)).astype(jnp.bfloat16)


def input_gradient(cot, w, after):
    outs, positions = cot.shape
    rows = w.shape[1]
    block = min(rows, 256)
    return pl.pallas_call(
        input_grad_kernel,
        out_shape=jax.ShapeDtypeStruct((rows, positions), jnp.bfloat16),
        grid=(rows // block,),
        in_specs=[
            pl.BlockSpec((outs, positions), lambda g: (0, 0)),
            pl.BlockSpec((9, block, outs), lambda g: (0, g, 0)),
            pl.BlockSpec(memory_space=pl.ANY),
        ],
        out_specs=pl.BlockSpec((block, positions), lambda g: (g, 0)),
        scratch_shapes=[
            pltpu.VMEM((3, outs, HW), jnp.bfloat16),
            pltpu.VMEM((3, outs, WINDOW), jnp.bfloat16),
            pltpu.VMEM((3, outs, WINDOW), jnp.bfloat16),
        ],
        compiler_params=pltpu.CompilerParams(vmem_limit_bytes=VMEM_LIMIT),
        cost_estimate=pl.CostEstimate(
            flops=2 * rows * outs * 3 * (HW + 2 * WINDOW),
            bytes_accessed=2 * outs * positions + 18 * rows * outs + 2 * rows * positions,
            transcendentals=0,
        ),
        name="input_gradient",
    )(cot, w, after)


def common_exponent(values, bits):
    lowest = functools.reduce(
        jnp.minimum, [value[-1:].astype(jnp.float32) + bit for value, bit in values]
    )
    return lowest - bits


def scaled_sum(values, lowest):
    return sum(
        value.astype(jnp.float32) * jnp.exp2(lowest - value[-1:].astype(jnp.float32))
        for value, _ in values
    )


def later(value, *gates):
    for gate in gates:
        gate = gate[(0,) * (gate.ndim - 2)]
        value = jnp.where(gate.astype(jnp.float32) > -1e30, value, jnp.zeros_like(value))
    return value


def summed(values, bits, *gates):
    lowest = common_exponent(values, bits)
    total = later(scaled_sum(values, lowest), *gates).astype(jnp.float16)
    return lax.dynamic_update_slice(
        total, lowest.astype(jnp.float16), (total.shape[0] - 1, 0, 0)
    )


def token(value):
    return value[0].astype(jnp.float32)


def on_device(inputs, weight, cotangent):
    x = inputs[0]
    x_held = pltpu.with_memory_space_constraint(x, pltpu.HBM)
    own_cot = cotangent[0]
    w = jnp.transpose(weight, (1, 0, 2))
    taps, rows, outs = w.shape
    own_outs, positions = own_cot.shape
    samples = lax.axis_size("dp")
    chans = lax.axis_size("chan")
    depth = samples // 4
    place = lax.axis_index("dp")
    chan = lax.axis_index("chan")
    core, column, level = place % 2, (place // 2) % 2, place // 4
    core_rows = rows // 2
    core_tiles = core_rows // TILE
    chip_tiles = core_tiles // 2
    shard_tiles = chip_tiles // depth

    def to(value, distance):
        return lax.ppermute(value, "dp", [(i, i ^ distance) for i in range(samples)])

    def to_core(value):
        return to(value, 1)

    def to_column(value):
        return to(value, 2)

    def to_level(value, step):
        return to(value, 4 * step)

    if chans == 2:
        their_cot = lax.ppermute(own_cot, "chan", [(0, 1), (1, 0)])
        parts = (own_cot, their_cot)
        first = chan
    else:
        cot = lax.all_gather(own_cot, "chan", axis=0, tiled=True)
        parts = (cot[:LANES], cot[LANES:])
        first = 0
    other_x = to_core(lax.dynamic_slice_in_dim(x, (1 - core) * core_rows, core_rows, 0))
    where = jnp.stack([core, column * depth + level]).astype(jnp.int32)
    halves, exponents, sends, reduced, gathers = [], [], [], [], []
    bits_of_depth = [1 << shift for shift in range(depth.bit_length() - 1)]
    grad = jnp.zeros((taps, rows // TILE, 2, TILE, LANES), jnp.float16)
    after = own_cot
    for side in range(2):
        part = parts[side]
        if side == 0:
            held_part = pltpu.with_memory_space_constraint(part, pltpu.HBM)
        if side == 1:
            part = later(part, shards[0][-1:, :1, :1])
            their_cot = part
        shards = kernel_grad(
            where, depth, x_held, other_x, part if side else held_part, to_core(part), after
        )
        held = [None] * depth
        gates = ()
        for message in (1, 0):
            sent = later(shards[depth + message], *gates).astype(jnp.float16)
            came = to_column(sent)
            gates = (sent,)
            for slot in range(depth // 2 - 1, -1, -1):
                step = message * (depth // 2) + slot
                held[step] = [(shards[step], 0.0), (came[slot], 0.0)]
        after = sent[0, 0].astype(jnp.float32)
        bits = 1.0
        gates = (sends[-1],) if side else ()
        for bit in bits_of_depth:
            for step in range(depth - bit, 0, -2 * bit):
                pair = summed(held[step], bits, *gates)
                held[step ^ bit].append((to_level(pair, bit), bits))
                gates = (pair,)
                sends.append(pair)
                if side and step == depth - 1:
                    total = forward(x, w, token(pair))
                    gates += (total[:TILE, :LANES],)
            bits += 1.0
        reduced.append((held[0], bits))

    for side, (values, bits) in enumerate(reduced):
        lowest = common_exponent(values, bits)
        gates = (gathers[0][1], input_grad[:TILE, :LANES]) if side else (sends[-1],)
        kept = later(scaled_sum(values, lowest)[:-1], *gates)
        shard = kept.astype(jnp.float16).reshape(taps, shard_tiles, 1, TILE, LANES)
        halves.append(shard)
        exponents.append(later(lowest, shard))
        near = [shard] + [None] * (depth - 1)
        for bit in bits_of_depth[::-1]:
            near[bit] = to_level(shard, bit)
        gathers.append((near, to_column(shard)))
        if side == 0:
            if chans == 2:
                cot = jnp.where(
                    chan == 0,
                    jnp.concatenate([own_cot, their_cot], 0),
                    jnp.concatenate([their_cot, own_cot], 0),
                )
            input_grad = input_gradient(cot, w, token(shard[0, 0]))

    for side, (near, own) in enumerate(gathers):
        for step in range(1, depth):
            if near[step] is None:
                low = step & -step
                near[step] = to_level(near[step ^ low], low)
        steps = list(range(depth))
        cuts = [steps[1:2], steps[2:]] if side == 0 else [steps[1:-1], steps[-1:]]
        here = [jnp.stack([near[step] for step in cut]) for cut in cuts]
        there = [to_column(values) for values in here]
        if side == 0:
            returned = there[1]
        here, there = [near[0][None]] + here, [own[None]] + there
        pieces = [(column, step, near[step]) for step in steps]
        arrivals = [(steps[0], own)] + [
            (step, values[slot])
            for cut, values in zip(cuts, there[1:])
            for slot, step in enumerate(cut)
        ]
        pieces += [(1 - column, step, value) for step, value in arrivals]
        if side == 0:
            messages = [(pieces, jnp.concatenate(here + there))]
        else:
            messages = [
                (pieces[:-1], jnp.concatenate(here + there[:-1])),
                (pieces[-1:], there[-1]),
            ]
        lane = first if side == 0 else 1 - first
        for listed, message in messages:
            across = to_core(message)
            for slot, (chip, step, piece) in enumerate(listed):
                row = chip * chip_tiles + (level ^ step) * shard_tiles
                for base, value in ((core, piece), (1 - core, across[slot])):
                    grad = lax.dynamic_update_slice(
                        grad, value, (0, base * core_tiles + row, lane, 0, 0)
                    )
    exponents = [jnp.where(first == side, exponents[0], exponents[1]) for side in range(2)]
    exponent = jnp.concatenate(exponents, 0)
    other = to_core(later(exponent, returned))
    by_core = [jnp.where(core == side, exponent, other) for side in range(2)]
    factor = jnp.exp2(-jnp.stack(by_core)) * (1.0 / samples)
    grad = grad.reshape(taps, 2, core_tiles, 2, TILE, LANES).astype(jnp.float32)
    grad = (grad * factor[None, :, None]).reshape(taps, rows // TILE, 2, TILE, LANES)
    weight_grad = jnp.transpose(grad, (1, 3, 0, 2, 4)).reshape(rows, taps, outs)

    if chans == 2:
        mine = lax.dynamic_slice_in_dim(total, chan * own_outs, own_outs, 0)
        theirs = lax.dynamic_slice_in_dim(total, (1 - chan) * own_outs, own_outs, 0)
        theirs = jnp.where(token(halves[1][0, 0])[0, 0] > -1e30, theirs, 0.0)
        result = mine + lax.ppermute(theirs, "chan", [(0, 1), (1, 0)])
    else:
        result = lax.psum_scatter(total, "chan", scatter_dimension=0, tiled=True)
    result = result.astype(jnp.bfloat16)[None]
    return (result, input_grad[None], weight_grad)


def solution(mesh):
    placed = (P("dp", "chan", None), P("chan", None, None), P("dp", "chan", None))
    return jax.shard_map(
        on_device,
        mesh=mesh,
        in_specs=placed,
        out_specs=(P("dp", "chan", None), P("dp", "chan", None), P("chan", None, None)),
        check_vma=False,
    )
```

```python
import functools

import jax
import jax.numpy as jnp
from jax import lax
from jax.experimental import pallas as pl
from jax.experimental.pallas import tpu as pltpu
from jax.sharding import PartitionSpec as P

DILATION_RATE = 12
MAP_HEIGHT = 16
MAP_WIDTH = 72
HW = MAP_HEIGHT * MAP_WIDTH
REACH = (MAP_HEIGHT - DILATION_RATE) * MAP_WIDTH
WINDOW = 384
PAD = WINDOW - REACH
COLUMN_SHIFTS = (-DILATION_RATE, 0, DILATION_RATE)
VMEM_LIMIT = 16 * 1024 * 1024


def column_mask(start, width, shift):
    position = lax.broadcasted_iota(jnp.int32, (1, width), 1) + start
    column = lax.rem(position, MAP_WIDTH) + shift
    return position, (column >= 0) & (column < MAP_WIDTH)


def moved(values, amount):
    amount = amount % values.shape[1]
    return values if amount == 0 else pltpu.roll(values, amount, 1)


def moved_cotangent(cot, group, shift):
    if group == 1:
        _, inside = column_mask(0, HW, -shift)
        values = moved(cot, shift)
    elif group == 0:
        position, inside = column_mask(0, WINDOW, -shift)
        inside = inside & (position < REACH)
        values = moved(cot[:, HW - WINDOW :], shift - PAD)
    else:
        position, inside = column_mask(HW - WINDOW, WINDOW, -shift)
        inside = inside & (position >= HW - REACH)
        values = moved(cot[:, :WINDOW], PAD + shift)
    return jnp.where(inside, values, 0.0).astype(jnp.bfloat16)


def window(group):
    return (slice(0, WINDOW), slice(0, HW), slice(HW - WINDOW, HW))[group]


TILE = 8
LANES = 128
TOP = 30000.0


def kernel_grad_kernel(depth, place_ref, own_x, other_x, own_cot, other_cot, _, *refs):
    near, far = refs[:depth], refs[depth : depth + 2]
    sums, peak_ref = refs[depth + 2 :]
    step = pl.program_id(0)
    rows, width = own_x.shape[0], own_cot.shape[0]
    shards = 2 * depth
    shard_rows = rows // shards
    tiles = shard_rows // TILE
    lanes = width // LANES

    @pl.when(step == 0)
    def _():
        peak_ref[...] = jnp.zeros(peak_ref.shape, jnp.float32)

    for group in range(3):

        @pl.when(step == group)
        def _(group=group):
            where = window(group)
            total = None
            for x_ref, cot_ref in ((own_x, own_cot), (other_x, other_cot)):
                cot = cot_ref[...].astype(jnp.float32)
                cots = [moved_cotangent(cot, group, shift) for shift in COLUMN_SHIFTS]
                term = lax.dot_general(
                    x_ref[:, where],
                    jnp.concatenate(cots, 0),
                    (((1,), (1,)), ((), ())),
                    preferred_element_type=jnp.float32,
                )
                total = term if total is None else total + term
            peak_ref[...] = jnp.maximum(
                peak_ref[...], jnp.max(jnp.abs(total), axis=0, keepdims=True)
            )
            for column in range(3):
                for shard in range(shards):
                    for tile in range(tiles):
                        for lane in range(lanes):
                            row = shard * shard_rows + tile * TILE
                            first = column * width + lane * LANES
                            slot = ((3 * group + column) * tiles + tile) * lanes + lane
                            sums[shard, slot] = total[row : row + TILE, first : first + LANES]

    @pl.when(step == 2)
    def _():
        peak = jnp.max(peak_ref[...], axis=1, keepdims=True)
        exponent = jnp.floor(jnp.log2(TOP / jnp.maximum(peak, 1e-30)))
        exponent = jnp.broadcast_to(exponent, (TILE, LANES))
        scale = jnp.exp2(exponent)
        count = sums.shape[1]
        for distance in range(shards):
            if distance < depth:
                out = near[distance]
            else:
                message, slot = divmod(distance - depth, depth // 2)
                out = far[message].at[slot]
            out[:count] = sums[place_ref[1] ^ distance] * scale
            out[count] = exponent


def kernel_grad(place, depth, x, other_x, own_cot, other_cot, after):
    rows, positions = other_x.shape
    outs = own_cot.shape[0]
    tiles = 9 * rows * outs // (2 * depth * TILE * LANES)
    whole = lambda g, h: (0, 0)
    once = pl.Buffered(1)
    shapes = [(tiles + 1, TILE, LANES)] * depth + [(depth // 2, tiles + 1, TILE, LANES)] * 2
    return pl.pallas_call(
        functools.partial(kernel_grad_kernel, depth),
        out_shape=[jax.ShapeDtypeStruct(shape, jnp.float32) for shape in shapes],
        grid_spec=pltpu.PrefetchScalarGridSpec(
            num_scalar_prefetch=1,
            grid=(3,),
            in_specs=[
                pl.BlockSpec((rows, positions), lambda g, h: (h[0], 0), pipeline_mode=once),
                pl.BlockSpec((rows, positions), whole, pipeline_mode=once),
                pl.BlockSpec((outs, positions), whole, pipeline_mode=once),
                pl.BlockSpec((outs, positions), whole, pipeline_mode=once),
                pl.BlockSpec(memory_space=pl.ANY),
            ],
            out_specs=[
                pl.BlockSpec(shape, functools.partial(lambda n, g, h: (0,) * n, len(shape)))
                for shape in shapes
            ],
            scratch_shapes=[
                pltpu.VMEM((2 * depth, tiles, TILE, LANES), jnp.float32),
                pltpu.VMEM((1, 3 * outs), jnp.float32),
            ],
        ),
        compiler_params=pltpu.CompilerParams(vmem_limit_bytes=VMEM_LIMIT),
        cost_estimate=pl.CostEstimate(
            flops=4 * rows * outs * 3 * (HW + 2 * WINDOW),
            bytes_accessed=4 * rows * positions + 4 * outs * positions + 36 * rows * outs,
            transcendentals=0,
        ),
        name="kernel_grad",
    )(place, x, other_x, own_cot, other_cot, after)


def forward_kernel(x_ref, w_ref, _, out_ref):
    step = pl.program_id(0)
    for group in range(3):

        @pl.when(step == group)
        def _(group=group):
            where = window(group)
            total = None
            for column, shift in enumerate(COLUMN_SHIFTS):
                term = lax.dot_general(
                    w_ref[column],
                    x_ref[:, where],
                    (((0,), (0,)), ((), ())),
                    preferred_element_type=jnp.float32,
                )
                if group == 1:
                    _, inside = column_mask(0, HW, shift)
                    term = moved(term, -shift)
                elif group == 0:
                    position, inside = column_mask(HW - WINDOW, WINDOW, shift)
                    inside = inside & (position >= HW - REACH)
                    term = moved(term, PAD - shift)
                else:
                    position, inside = column_mask(0, WINDOW, shift)
                    inside = inside & (position < REACH)
                    term = moved(term, -PAD - shift)
                term = jnp.where(inside, term, 0.0)
                total = term if total is None else total + term
            if group == 0:
                out_ref[:, : HW - WINDOW] = jnp.zeros((out_ref.shape[0], HW - WINDOW), jnp.float32)
                out_ref[:, HW - WINDOW :] = total
            elif group == 1:
                out_ref[...] += total
            else:
                out_ref[:, :WINDOW] += total


def forward(x, w, after):
    rows, positions = x.shape
    outs = w.shape[2]
    return pl.pallas_call(
        forward_kernel,
        out_shape=jax.ShapeDtypeStruct((outs, positions), jnp.float32),
        grid=(3,),
        in_specs=[
            pl.BlockSpec((rows, positions), lambda g: (0, 0), pipeline_mode=pl.Buffered(1)),
            pl.BlockSpec((3, rows, outs), lambda g: (g, 0, 0)),
            pl.BlockSpec(memory_space=pl.ANY),
        ],
        out_specs=pl.BlockSpec((outs, positions), lambda g: (0, 0)),
        compiler_params=pltpu.CompilerParams(vmem_limit_bytes=VMEM_LIMIT),
        cost_estimate=pl.CostEstimate(
            flops=2 * rows * outs * 3 * (HW + 2 * WINDOW),
            bytes_accessed=2 * rows * positions + 18 * rows * outs + 4 * outs * positions,
            transcendentals=0,
        ),
        name="forward",
    )(x, w, after)


def input_grad_kernel(cot_ref, w_ref, _, out_ref, middle, upper, lower):
    @pl.when(pl.program_id(0) == 0)
    def _():
        cot = cot_ref[...].astype(jnp.float32)
        for group, held in enumerate((upper, middle, lower)):
            for column, shift in enumerate(COLUMN_SHIFTS):
                held[column] = moved_cotangent(cot, group, shift)

    def products(group, held):
        total = None
        for column in range(3):
            term = jnp.dot(
                w_ref[3 * group + column], held[column], preferred_element_type=jnp.float32
            )
            total = term if total is None else total + term
        return total

    edge = HW - WINDOW
    centre = products(1, middle)
    out_ref[:, :WINDOW] = (centre[:, :WINDOW] + products(0, upper)).astype(jnp.bfloat16)
    out_ref[:, WINDOW:edge] = centre[:, WINDOW:edge].astype(jnp.bfloat16)
    out_ref[:, edge:] = (centre[:, edge:] + products(2, lower)).astype(jnp.bfloat16)


def input_gradient(cot, w, after):
    outs, positions = cot.shape
    rows = w.shape[1]
    block = min(rows, 256)
    return pl.pallas_call(
        input_grad_kernel,
        out_shape=jax.ShapeDtypeStruct((rows, positions), jnp.bfloat16),
        grid=(rows // block,),
        in_specs=[
            pl.BlockSpec((outs, positions), lambda g: (0, 0)),
            pl.BlockSpec((9, block, outs), lambda g: (0, g, 0)),
            pl.BlockSpec(memory_space=pl.ANY),
        ],
        out_specs=pl.BlockSpec((block, positions), lambda g: (g, 0)),
        scratch_shapes=[
            pltpu.VMEM((3, outs, HW), jnp.bfloat16),
            pltpu.VMEM((3, outs, WINDOW), jnp.bfloat16),
            pltpu.VMEM((3, outs, WINDOW), jnp.bfloat16),
        ],
        compiler_params=pltpu.CompilerParams(vmem_limit_bytes=VMEM_LIMIT),
        cost_estimate=pl.CostEstimate(
            flops=2 * rows * outs * 3 * (HW + 2 * WINDOW),
            bytes_accessed=2 * outs * positions + 18 * rows * outs + 2 * rows * positions,
            transcendentals=0,
        ),
        name="input_gradient",
    )(cot, w, after)


def common_exponent(values, bits):
    lowest = functools.reduce(
        jnp.minimum, [value[-1:].astype(jnp.float32) + bit for value, bit in values]
    )
    return lowest - bits


def scaled_sum(values, lowest):
    return sum(
        value.astype(jnp.float32) * jnp.exp2(lowest - value[-1:].astype(jnp.float32))
        for value, _ in values
    )


def later(value, *gates):
    for gate in gates:
        gate = gate[(0,) * (gate.ndim - 2)]
        value = jnp.where(gate.astype(jnp.float32) > -1e30, value, jnp.zeros_like(value))
    return value


def summed(values, bits, *gates):
    lowest = common_exponent(values, bits)
    total = later(scaled_sum(values, lowest), *gates).astype(jnp.float16)
    return lax.dynamic_update_slice(
        total, lowest.astype(jnp.float16), (total.shape[0] - 1, 0, 0)
    )


def token(value):
    return value[0].astype(jnp.float32)


def on_device(inputs, weight, cotangent):
    x = inputs[0]
    x_held = pltpu.with_memory_space_constraint(x, pltpu.HBM)
    own_cot = cotangent[0]
    w = jnp.transpose(weight, (1, 0, 2))
    taps, rows, outs = w.shape
    own_outs, positions = own_cot.shape
    samples = lax.axis_size("dp")
    chans = lax.axis_size("chan")
    depth = samples // 4
    place = lax.axis_index("dp")
    chan = lax.axis_index("chan")
    core, column, level = place % 2, (place // 2) % 2, place // 4
    core_rows = rows // 2
    core_tiles = core_rows // TILE
    chip_tiles = core_tiles // 2
    shard_tiles = chip_tiles // depth

    def to(value, distance):
        return lax.ppermute(value, "dp", [(i, i ^ distance) for i in range(samples)])

    def to_core(value):
        return to(value, 1)

    def to_column(value):
        return to(value, 2)

    def to_level(value, step):
        return to(value, 4 * step)

    if chans == 2:
        their_cot = lax.ppermute(own_cot, "chan", [(0, 1), (1, 0)])
        parts = (own_cot, their_cot)
        first = chan
    else:
        cot = lax.all_gather(own_cot, "chan", axis=0, tiled=True)
        parts = (cot[:LANES], cot[LANES:])
        first = 0
    other_x = to_core(lax.dynamic_slice_in_dim(x, (1 - core) * core_rows, core_rows, 0))
    where = jnp.stack([core, column * depth + level]).astype(jnp.int32)
    halves, exponents, sends, reduced, gathers = [], [], [], [], []
    bits_of_depth = [1 << shift for shift in range(depth.bit_length() - 1)]
    grad = jnp.zeros((taps, rows // TILE, 2, TILE, LANES), jnp.float16)
    after = own_cot
    for side in range(2):
        part = parts[side]
        if side == 0:
            held_part = pltpu.with_memory_space_constraint(part, pltpu.HBM)
        if side == 1:
            part = later(part, shards[0][-1:, :1, :1])
            their_cot = part
        shards = kernel_grad(
            where, depth, x_held, other_x, part if side else held_part, to_core(part), after
        )
        held = [None] * depth
        gates = ()
        for message in (1, 0):
            sent = later(shards[depth + message], *gates).astype(jnp.float16)
            came = to_column(sent)
            gates = (sent,)
            for slot in range(depth // 2 - 1, -1, -1):
                step = message * (depth // 2) + slot
                held[step] = [(shards[step], 0.0), (came[slot], 0.0)]
        after = sent[0, 0].astype(jnp.float32)
        bits = 1.0
        gates = (sends[-1],) if side else ()
        for bit in bits_of_depth:
            for step in range(depth - bit, 0, -2 * bit):
                pair = summed(held[step], bits, *gates)
                held[step ^ bit].append((to_level(pair, bit), bits))
                gates = (pair,)
                sends.append(pair)
                if side and step == depth - 1:
                    total = forward(x, w, token(pair))
                    gates += (total[:TILE, :LANES],)
            bits += 1.0
        reduced.append((held[0], bits))

    for side, (values, bits) in enumerate(reduced):
        lowest = common_exponent(values, bits)
        gates = (gathers[0][1], input_grad[:TILE, :LANES]) if side else (sends[-1],)
        kept = later(scaled_sum(values, lowest)[:-1], *gates)
        shard = kept.astype(jnp.float16).reshape(taps, shard_tiles, 1, TILE, LANES)
        halves.append(shard)
        exponents.append(later(lowest, shard))
        near = [shard] + [None] * (depth - 1)
        for bit in bits_of_depth[::-1]:
            near[bit] = to_level(shard, bit)
        for step in range(1, depth):
            if near[step] is None:
                low = step & -step
                near[step] = to_level(near[step ^ low], low)
        gathers.append((near, to_column(shard)))
        if side == 0:
            if chans == 2:
                cot = jnp.where(
                    chan == 0,
                    jnp.concatenate([own_cot, their_cot], 0),
                    jnp.concatenate([their_cot, own_cot], 0),
                )
            input_grad = input_gradient(cot, w, token(shard[0, 0]))

    if chans == 2:
        mine = lax.dynamic_slice_in_dim(total, chan * own_outs, own_outs, 0)
        theirs = lax.dynamic_slice_in_dim(total, (1 - chan) * own_outs, own_outs, 0)
        theirs = jnp.where(token(halves[1][0, 0])[0, 0] > -1e30, theirs, 0.0)
        result = mine + lax.ppermute(theirs, "chan", [(0, 1), (1, 0)])
    else:
        result = lax.psum_scatter(total, "chan", scatter_dimension=0, tiled=True)
    result = result.astype(jnp.bfloat16)[None]
    for side, (near, own) in enumerate(gathers):
        steps = list(range(depth))
        cuts = [steps[1:-1], steps[-1:]]
        here = [jnp.stack([near[step] for step in cut]) for cut in cuts]
        there = [to_column(values) for values in here]
        if side == 0:
            returned = there[1]
        here, there = [near[0][None]] + here, [own[None]] + there
        if side == 1:
            there[-1] = later(there[-1], result[0, :TILE, :LANES])
        pieces = [(column, step, near[step]) for step in steps]
        arrivals = [(steps[0], own)] + [
            (step, values[slot])
            for cut, values in zip(cuts, there[1:])
            for slot, step in enumerate(cut)
        ]
        pieces += [(1 - column, step, value) for step, value in arrivals]
        if side == 0:
            messages = [(pieces, jnp.concatenate(here + there))]
        else:
            messages = [
                (pieces[:-1], jnp.concatenate(here + there[:-1])),
                (pieces[-1:], there[-1]),
            ]
        lane = first if side == 0 else 1 - first
        for listed, message in messages:
            across = to_core(message)
            for slot, (chip, step, piece) in enumerate(listed):
                row = chip * chip_tiles + (level ^ step) * shard_tiles
                for base, value in ((core, piece), (1 - core, across[slot])):
                    grad = lax.dynamic_update_slice(
                        grad, value, (0, base * core_tiles + row, lane, 0, 0)
                    )
    exponents = [jnp.where(first == side, exponents[0], exponents[1]) for side in range(2)]
    exponent = jnp.concatenate(exponents, 0)
    other = to_core(later(exponent, returned))
    by_core = [jnp.where(core == side, exponent, other) for side in range(2)]
    factor = jnp.exp2(-jnp.stack(by_core)) * (1.0 / samples)
    grad = grad.reshape(taps, 2, core_tiles, 2, TILE, LANES).astype(jnp.float32)
    grad = (grad * factor[None, :, None]).reshape(taps, rows // TILE, 2, TILE, LANES)
    weight_grad = jnp.transpose(grad, (1, 3, 0, 2, 4)).reshape(rows, taps, outs)

    return (result, input_grad[None], weight_grad)


def solution(mesh):
    placed = (P("dp", "chan", None), P("chan", None, None), P("dp", "chan", None))
    return jax.shard_map(
        on_device,
        mesh=mesh,
        in_specs=placed,
        out_specs=(P("dp", "chan", None), P("dp", "chan", None), P("chan", None, None)),
        check_vma=False,
    )
```

```python
import functools

import jax
import jax.numpy as jnp
from jax import lax
from jax.experimental import pallas as pl
from jax.experimental.pallas import tpu as pltpu
from jax.sharding import PartitionSpec as P

DILATION_RATE = 12
MAP_HEIGHT = 16
MAP_WIDTH = 72
HW = MAP_HEIGHT * MAP_WIDTH
REACH = (MAP_HEIGHT - DILATION_RATE) * MAP_WIDTH
WINDOW = 384
PAD = WINDOW - REACH
COLUMN_SHIFTS = (-DILATION_RATE, 0, DILATION_RATE)
VMEM_LIMIT = 16 * 1024 * 1024


def column_mask(start, width, shift):
    position = lax.broadcasted_iota(jnp.int32, (1, width), 1) + start
    column = lax.rem(position, MAP_WIDTH) + shift
    return position, (column >= 0) & (column < MAP_WIDTH)


def moved(values, amount):
    amount = amount % values.shape[1]
    return values if amount == 0 else pltpu.roll(values, amount, 1)


def moved_cotangent(cot, group, shift):
    if group == 1:
        _, inside = column_mask(0, HW, -shift)
        values = moved(cot, shift)
    elif group == 0:
        position, inside = column_mask(0, WINDOW, -shift)
        inside = inside & (position < REACH)
        values = moved(cot[:, HW - WINDOW :], shift - PAD)
    else:
        position, inside = column_mask(HW - WINDOW, WINDOW, -shift)
        inside = inside & (position >= HW - REACH)
        values = moved(cot[:, :WINDOW], PAD + shift)
    return jnp.where(inside, values, 0.0).astype(jnp.bfloat16)


def window(group):
    return (slice(0, WINDOW), slice(0, HW), slice(HW - WINDOW, HW))[group]


TILE = 8
LANES = 128
TOP = 30000.0


def kernel_grad_kernel(depth, place_ref, own_x, other_x, own_cot, other_cot, _, *refs):
    near, far = refs[:depth], refs[depth : depth + 2]
    sums, peak_ref = refs[depth + 2 :]
    step = pl.program_id(0)
    rows, width = own_x.shape[0], own_cot.shape[0]
    shards = 2 * depth
    shard_rows = rows // shards
    tiles = shard_rows // TILE
    lanes = width // LANES

    @pl.when(step == 0)
    def _():
        peak_ref[...] = jnp.zeros(peak_ref.shape, jnp.float32)

    for group in range(3):

        @pl.when(step == group)
        def _(group=group):
            where = window(group)
            total = None
            for x_ref, cot_ref in ((own_x, own_cot), (other_x, other_cot)):
                cot = cot_ref[...].astype(jnp.float32)
                cots = [moved_cotangent(cot, group, shift) for shift in COLUMN_SHIFTS]
                term = lax.dot_general(
                    x_ref[:, where],
                    jnp.concatenate(cots, 0),
                    (((1,), (1,)), ((), ())),
                    preferred_element_type=jnp.float32,
                )
                total = term if total is None else total + term
            peak_ref[...] = jnp.maximum(
                peak_ref[...], jnp.max(jnp.abs(total), axis=0, keepdims=True)
            )
            for column in range(3):
                for shard in range(shards):
                    for tile in range(tiles):
                        for lane in range(lanes):
                            row = shard * shard_rows + tile * TILE
                            first = column * width + lane * LANES
                            slot = ((3 * group + column) * tiles + tile) * lanes + lane
                            sums[shard, slot] = total[row : row + TILE, first : first + LANES]

    @pl.when(step == 2)
    def _():
        peak = jnp.max(peak_ref[...], axis=1, keepdims=True)
        exponent = jnp.floor(jnp.log2(TOP / jnp.maximum(peak, 1e-30)))
        exponent = jnp.broadcast_to(exponent, (TILE, LANES))
        scale = jnp.exp2(exponent)
        count = sums.shape[1]
        for distance in range(shards):
            if distance < depth:
                out = near[distance]
            else:
                message, slot = divmod(distance - depth, depth // 2)
                out = far[message].at[slot]
            out[:count] = sums[place_ref[1] ^ distance] * scale
            out[count] = exponent


def kernel_grad(place, depth, x, other_x, own_cot, other_cot, after):
    rows, positions = other_x.shape
    outs = own_cot.shape[0]
    tiles = 9 * rows * outs // (2 * depth * TILE * LANES)
    whole = lambda g, h: (0, 0)
    once = pl.Buffered(1)
    shapes = [(tiles + 1, TILE, LANES)] * depth + [(depth // 2, tiles + 1, TILE, LANES)] * 2
    return pl.pallas_call(
        functools.partial(kernel_grad_kernel, depth),
        out_shape=[jax.ShapeDtypeStruct(shape, jnp.float32) for shape in shapes],
        grid_spec=pltpu.PrefetchScalarGridSpec(
            num_scalar_prefetch=1,
            grid=(3,),
            in_specs=[
                pl.BlockSpec((rows, positions), lambda g, h: (h[0], 0), pipeline_mode=once),
                pl.BlockSpec((rows, positions), whole, pipeline_mode=once),
                pl.BlockSpec((outs, positions), whole, pipeline_mode=once),
                pl.BlockSpec((outs, positions), whole, pipeline_mode=once),
                pl.BlockSpec(memory_space=pl.ANY),
            ],
            out_specs=[
                pl.BlockSpec(shape, functools.partial(lambda n, g, h: (0,) * n, len(shape)))
                for shape in shapes
            ],
            scratch_shapes=[
                pltpu.VMEM((2 * depth, tiles, TILE, LANES), jnp.float32),
                pltpu.VMEM((1, 3 * outs), jnp.float32),
            ],
        ),
        compiler_params=pltpu.CompilerParams(vmem_limit_bytes=VMEM_LIMIT),
        cost_estimate=pl.CostEstimate(
            flops=4 * rows * outs * 3 * (HW + 2 * WINDOW),
            bytes_accessed=4 * rows * positions + 4 * outs * positions + 36 * rows * outs,
            transcendentals=0,
        ),
        name="kernel_grad",
    )(place, x, other_x, own_cot, other_cot, after)


def forward_kernel(x_ref, w_ref, _, out_ref):
    step = pl.program_id(0)
    for group in range(3):

        @pl.when(step == group)
        def _(group=group):
            where = window(group)
            total = None
            for column, shift in enumerate(COLUMN_SHIFTS):
                term = lax.dot_general(
                    w_ref[column],
                    x_ref[:, where],
                    (((0,), (0,)), ((), ())),
                    preferred_element_type=jnp.float32,
                )
                if group == 1:
                    _, inside = column_mask(0, HW, shift)
                    term = moved(term, -shift)
                elif group == 0:
                    position, inside = column_mask(HW - WINDOW, WINDOW, shift)
                    inside = inside & (position >= HW - REACH)
                    term = moved(term, PAD - shift)
                else:
                    position, inside = column_mask(0, WINDOW, shift)
                    inside = inside & (position < REACH)
                    term = moved(term, -PAD - shift)
                term = jnp.where(inside, term, 0.0)
                total = term if total is None else total + term
            if group == 0:
                out_ref[:, : HW - WINDOW] = jnp.zeros((out_ref.shape[0], HW - WINDOW), jnp.float32)
                out_ref[:, HW - WINDOW :] = total
            elif group == 1:
                out_ref[...] += total
            else:
                out_ref[:, :WINDOW] += total


def forward(x, w, after):
    rows, positions = x.shape
    outs = w.shape[2]
    return pl.pallas_call(
        forward_kernel,
        out_shape=jax.ShapeDtypeStruct((outs, positions), jnp.float32),
        grid=(3,),
        in_specs=[
            pl.BlockSpec((rows, positions), lambda g: (0, 0), pipeline_mode=pl.Buffered(1)),
            pl.BlockSpec((3, rows, outs), lambda g: (g, 0, 0)),
            pl.BlockSpec(memory_space=pl.ANY),
        ],
        out_specs=pl.BlockSpec((outs, positions), lambda g: (0, 0)),
        compiler_params=pltpu.CompilerParams(vmem_limit_bytes=VMEM_LIMIT),
        cost_estimate=pl.CostEstimate(
            flops=2 * rows * outs * 3 * (HW + 2 * WINDOW),
            bytes_accessed=2 * rows * positions + 18 * rows * outs + 4 * outs * positions,
            transcendentals=0,
        ),
        name="forward",
    )(x, w, after)


def input_grad_kernel(cot_ref, w_ref, _, out_ref, middle, upper, lower):
    @pl.when(pl.program_id(0) == 0)
    def _():
        cot = cot_ref[...].astype(jnp.float32)
        for group, held in enumerate((upper, middle, lower)):
            for column, shift in enumerate(COLUMN_SHIFTS):
                held[column] = moved_cotangent(cot, group, shift)

    def products(group, held):
        total = None
        for column in range(3):
            term = jnp.dot(
                w_ref[3 * group + column], held[column], preferred_element_type=jnp.float32
            )
            total = term if total is None else total + term
        return total

    edge = HW - WINDOW
    centre = products(1, middle)
    out_ref[:, :WINDOW] = (centre[:, :WINDOW] + products(0, upper)).astype(jnp.bfloat16)
    out_ref[:, WINDOW:edge] = centre[:, WINDOW:edge].astype(jnp.bfloat16)
    out_ref[:, edge:] = (centre[:, edge:] + products(2, lower)).astype(jnp.bfloat16)


def input_gradient(cot, w, after):
    outs, positions = cot.shape
    rows = w.shape[1]
    block = min(rows, 256)
    return pl.pallas_call(
        input_grad_kernel,
        out_shape=jax.ShapeDtypeStruct((rows, positions), jnp.bfloat16),
        grid=(rows // block,),
        in_specs=[
            pl.BlockSpec((outs, positions), lambda g: (0, 0)),
            pl.BlockSpec((9, block, outs), lambda g: (0, g, 0)),
            pl.BlockSpec(memory_space=pl.ANY),
        ],
        out_specs=pl.BlockSpec((block, positions), lambda g: (g, 0)),
        scratch_shapes=[
            pltpu.VMEM((3, outs, HW), jnp.bfloat16),
            pltpu.VMEM((3, outs, WINDOW), jnp.bfloat16),
            pltpu.VMEM((3, outs, WINDOW), jnp.bfloat16),
        ],
        compiler_params=pltpu.CompilerParams(vmem_limit_bytes=VMEM_LIMIT),
        cost_estimate=pl.CostEstimate(
            flops=2 * rows * outs * 3 * (HW + 2 * WINDOW),
            bytes_accessed=2 * outs * positions + 18 * rows * outs + 2 * rows * positions,
            transcendentals=0,
        ),
        name="input_gradient",
    )(cot, w, after)


def common_exponent(values, bits):
    lowest = functools.reduce(
        jnp.minimum, [value[-1:].astype(jnp.float32) + bit for value, bit in values]
    )
    return lowest - bits


def scaled_sum(values, lowest):
    return sum(
        value.astype(jnp.float32) * jnp.exp2(lowest - value[-1:].astype(jnp.float32))
        for value, _ in values
    )


def later(value, *gates):
    for gate in gates:
        gate = gate[(0,) * (gate.ndim - 2)]
        value = jnp.where(gate.astype(jnp.float32) > -1e30, value, jnp.zeros_like(value))
    return value


def summed(values, bits, *gates):
    lowest = common_exponent(values, bits)
    total = later(scaled_sum(values, lowest), *gates).astype(jnp.float16)
    return lax.dynamic_update_slice(
        total, lowest.astype(jnp.float16), (total.shape[0] - 1, 0, 0)
    )


def token(value):
    return value[0].astype(jnp.float32)


def on_device(inputs, weight, cotangent):
    x = inputs[0]
    x_held = pltpu.with_memory_space_constraint(x, pltpu.HBM)
    own_cot = cotangent[0]
    w = jnp.transpose(weight, (1, 0, 2))
    taps, rows, outs = w.shape
    own_outs, positions = own_cot.shape
    samples = lax.axis_size("dp")
    chans = lax.axis_size("chan")
    depth = samples // 4
    place = lax.axis_index("dp")
    chan = lax.axis_index("chan")
    core, column, level = place % 2, (place // 2) % 2, place // 4
    core_rows = rows // 2
    core_tiles = core_rows // TILE
    chip_tiles = core_tiles // 2
    shard_tiles = chip_tiles // depth

    def to(value, distance):
        return lax.ppermute(value, "dp", [(i, i ^ distance) for i in range(samples)])

    def to_core(value):
        return to(value, 1)

    def to_column(value):
        return to(value, 2)

    def to_level(value, step):
        return to(value, 4 * step)

    if chans == 2:
        their_cot = lax.ppermute(own_cot, "chan", [(0, 1), (1, 0)])
        parts = (own_cot, their_cot)
        first = chan
    else:
        cot = lax.all_gather(own_cot, "chan", axis=0, tiled=True)
        parts = (cot[:LANES], cot[LANES:])
        first = 0
    other_x = to_core(lax.dynamic_slice_in_dim(x, (1 - core) * core_rows, core_rows, 0))
    where = jnp.stack([core, column * depth + level]).astype(jnp.int32)
    halves, exponents, sends, reduced, gathers = [], [], [], [], []
    bits_of_depth = [1 << shift for shift in range(depth.bit_length() - 1)]
    grad = jnp.zeros((taps, rows // TILE, 2, TILE, LANES), jnp.float16)
    after = own_cot
    for side in range(2):
        part = parts[side]
        if side == 0:
            held_part = pltpu.with_memory_space_constraint(part, pltpu.HBM)
        if side == 1:
            part = later(part, shards[0][-1:, :1, :1])
            their_cot = part
        shards = kernel_grad(
            where, depth, x_held, other_x, part if side else held_part, to_core(part), after
        )
        held = [None] * depth
        gates = ()
        for message in (1, 0):
            sent = later(shards[depth + message], *gates).astype(jnp.float16)
            came = to_column(sent)
            gates = (sent,)
            for slot in range(depth // 2 - 1, -1, -1):
                step = message * (depth // 2) + slot
                held[step] = [(shards[step], 0.0), (came[slot], 0.0)]
        after = sent[0, 0].astype(jnp.float32)
        bits = 1.0
        gates = (sends[-1],) if side else ()
        for bit in bits_of_depth:
            for step in range(depth - bit, 0, -2 * bit):
                pair = summed(held[step], bits, *gates)
                held[step ^ bit].append((to_level(pair, bit), bits))
                gates = (pair,)
                sends.append(pair)
                if side and step == depth - 1:
                    total = forward(x, w, token(pair))
                    gates += (total[:TILE, :LANES],)
            bits += 1.0
        reduced.append((held[0], bits))

    for side, (values, bits) in enumerate(reduced):
        lowest = common_exponent(values, bits)
        gates = (gathers[0][1], input_grad[:TILE, :LANES]) if side else (sends[-1],)
        kept = later(scaled_sum(values, lowest)[:-1], *gates)
        shard = kept.astype(jnp.float16).reshape(taps, shard_tiles, 1, TILE, LANES)
        halves.append(shard)
        exponents.append(later(lowest, shard))
        near = [shard] + [None] * (depth - 1)
        for bit in bits_of_depth[::-1]:
            near[bit] = to_level(shard, bit)
        for step in range(1, depth):
            if near[step] is None:
                low = step & -step
                near[step] = to_level(near[step ^ low], low)
        gathers.append((near, to_column(shard)))
        if side == 0:
            if chans == 2:
                cot = jnp.where(
                    chan == 0,
                    jnp.concatenate([own_cot, their_cot], 0),
                    jnp.concatenate([their_cot, own_cot], 0),
                )
            input_grad = input_gradient(cot, w, token(shard[0, 0]))

    for side, (near, own) in enumerate(gathers):
        steps = list(range(depth))
        cuts = [steps[1:-1], steps[-1:]]
        here = [jnp.stack([near[step] for step in cut]) for cut in cuts]
        there = [to_column(values) for values in here]
        if side == 0:
            returned = there[1]
        here, there = [near[0][None]] + here, [own[None]] + there
        pieces = [(column, step, near[step]) for step in steps]
        arrivals = [(steps[0], own)] + [
            (step, values[slot])
            for cut, values in zip(cuts, there[1:])
            for slot, step in enumerate(cut)
        ]
        pieces += [(1 - column, step, value) for step, value in arrivals]
        if side == 0:
            messages = [(pieces, jnp.concatenate(here + there))]
        else:
            messages = [
                (pieces[:-1], jnp.concatenate(here + there[:-1])),
                (pieces[-1:], there[-1]),
            ]
        lane = first if side == 0 else 1 - first
        for listed, message in messages:
            if side == 1 and message is there[-1]:
                message = later(message, crossed)
            across = to_core(message)
            crossed = across if side == 0 else crossed
            for slot, (chip, step, piece) in enumerate(listed):
                row = chip * chip_tiles + (level ^ step) * shard_tiles
                for base, value in ((core, piece), (1 - core, across[slot])):
                    grad = lax.dynamic_update_slice(
                        grad, value, (0, base * core_tiles + row, lane, 0, 0)
                    )
    exponents = [jnp.where(first == side, exponents[0], exponents[1]) for side in range(2)]
    exponent = jnp.concatenate(exponents, 0)
    other = to_core(later(exponent, returned))
    by_core = [jnp.where(core == side, exponent, other) for side in range(2)]
    factor = jnp.exp2(-jnp.stack(by_core)) * (1.0 / samples)
    grad = grad.reshape(taps, 2, core_tiles, 2, TILE, LANES).astype(jnp.float32)
    grad = (grad * factor[None, :, None]).reshape(taps, rows // TILE, 2, TILE, LANES)
    weight_grad = jnp.transpose(grad, (1, 3, 0, 2, 4)).reshape(rows, taps, outs)

    if chans == 2:
        mine = lax.dynamic_slice_in_dim(total, chan * own_outs, own_outs, 0)
        theirs = lax.dynamic_slice_in_dim(total, (1 - chan) * own_outs, own_outs, 0)
        theirs = jnp.where(token(halves[1][0, 0])[0, 0] > -1e30, theirs, 0.0)
        result = mine + lax.ppermute(theirs, "chan", [(0, 1), (1, 0)])
    else:
        result = lax.psum_scatter(total, "chan", scatter_dimension=0, tiled=True)
    result = result.astype(jnp.bfloat16)[None]
    return (result, input_grad[None], weight_grad)


def solution(mesh):
    placed = (P("dp", "chan", None), P("chan", None, None), P("dp", "chan", None))
    return jax.shard_map(
        on_device,
        mesh=mesh,
        in_specs=placed,
        out_specs=(P("dp", "chan", None), P("dp", "chan", None), P("chan", None, None)),
        check_vma=False,
    )
```

```python
import functools

import jax
import jax.numpy as jnp
from jax import lax
from jax.experimental import pallas as pl
from jax.experimental.pallas import tpu as pltpu
from jax.sharding import PartitionSpec as P

DILATION_RATE = 12
MAP_HEIGHT = 16
MAP_WIDTH = 72
HW = MAP_HEIGHT * MAP_WIDTH
REACH = (MAP_HEIGHT - DILATION_RATE) * MAP_WIDTH
WINDOW = 384
PAD = WINDOW - REACH
COLUMN_SHIFTS = (-DILATION_RATE, 0, DILATION_RATE)
VMEM_LIMIT = 16 * 1024 * 1024


def column_mask(start, width, shift):
    position = lax.broadcasted_iota(jnp.int32, (1, width), 1) + start
    column = lax.rem(position, MAP_WIDTH) + shift
    return position, (column >= 0) & (column < MAP_WIDTH)


def moved(values, amount):
    amount = amount % values.shape[1]
    return values if amount == 0 else pltpu.roll(values, amount, 1)


def moved_cotangent(cot, group, shift):
    if group == 1:
        _, inside = column_mask(0, HW, -shift)
        values = moved(cot, shift)
    elif group == 0:
        position, inside = column_mask(0, WINDOW, -shift)
        inside = inside & (position < REACH)
        values = moved(cot[:, HW - WINDOW :], shift - PAD)
    else:
        position, inside = column_mask(HW - WINDOW, WINDOW, -shift)
        inside = inside & (position >= HW - REACH)
        values = moved(cot[:, :WINDOW], PAD + shift)
    return jnp.where(inside, values, 0.0).astype(jnp.bfloat16)


def window(group):
    return (slice(0, WINDOW), slice(0, HW), slice(HW - WINDOW, HW))[group]


TILE = 8
LANES = 128
TOP = 30000.0


def kernel_grad_kernel(depth, place_ref, own_x, other_x, own_cot, other_cot, _, *refs):
    near, far = refs[:depth], refs[depth : depth + 2]
    sums, peak_ref = refs[depth + 2 :]
    step = pl.program_id(0)
    rows, width = own_x.shape[0], own_cot.shape[0]
    shards = 2 * depth
    shard_rows = rows // shards
    tiles = shard_rows // TILE
    lanes = width // LANES

    @pl.when(step == 0)
    def _():
        peak_ref[...] = jnp.zeros(peak_ref.shape, jnp.float32)

    for group in range(3):

        @pl.when(step == group)
        def _(group=group):
            where = window(group)
            total = None
            for x_ref, cot_ref in ((own_x, own_cot), (other_x, other_cot)):
                cot = cot_ref[...].astype(jnp.float32)
                cots = [moved_cotangent(cot, group, shift) for shift in COLUMN_SHIFTS]
                term = lax.dot_general(
                    x_ref[:, where],
                    jnp.concatenate(cots, 0),
                    (((1,), (1,)), ((), ())),
                    preferred_element_type=jnp.float32,
                )
                total = term if total is None else total + term
            peak_ref[...] = jnp.maximum(
                peak_ref[...], jnp.max(jnp.abs(total), axis=0, keepdims=True)
            )
            for column in range(3):
                for shard in range(shards):
                    for tile in range(tiles):
                        for lane in range(lanes):
                            row = shard * shard_rows + tile * TILE
                            first = column * width + lane * LANES
                            slot = ((3 * group + column) * tiles + tile) * lanes + lane
                            sums[shard, slot] = total[row : row + TILE, first : first + LANES]

    @pl.when(step == 2)
    def _():
        peak = jnp.max(peak_ref[...], axis=1, keepdims=True)
        exponent = jnp.floor(jnp.log2(TOP / jnp.maximum(peak, 1e-30)))
        exponent = jnp.broadcast_to(exponent, (TILE, LANES))
        scale = jnp.exp2(exponent)
        count = sums.shape[1]
        for distance in range(shards):
            if distance < depth:
                out = near[distance]
            else:
                message, slot = divmod(distance - depth, depth // 2)
                out = far[message].at[slot]
            out[:count] = sums[place_ref[1] ^ distance] * scale
            out[count] = exponent


def kernel_grad(place, depth, x, other_x, own_cot, other_cot, after):
    rows, positions = other_x.shape
    outs = own_cot.shape[0]
    tiles = 9 * rows * outs // (2 * depth * TILE * LANES)
    whole = lambda g, h: (0, 0)
    once = pl.Buffered(1)
    shapes = [(tiles + 1, TILE, LANES)] * depth + [(depth // 2, tiles + 1, TILE, LANES)] * 2
    return pl.pallas_call(
        functools.partial(kernel_grad_kernel, depth),
        out_shape=[jax.ShapeDtypeStruct(shape, jnp.float32) for shape in shapes],
        grid_spec=pltpu.PrefetchScalarGridSpec(
            num_scalar_prefetch=1,
            grid=(3,),
            in_specs=[
                pl.BlockSpec((rows, positions), lambda g, h: (h[0], 0), pipeline_mode=once),
                pl.BlockSpec((rows, positions), whole, pipeline_mode=once),
                pl.BlockSpec((outs, positions), whole, pipeline_mode=once),
                pl.BlockSpec((outs, positions), whole, pipeline_mode=once),
                pl.BlockSpec(memory_space=pl.ANY),
            ],
            out_specs=[
                pl.BlockSpec(shape, functools.partial(lambda n, g, h: (0,) * n, len(shape)))
                for shape in shapes
            ],
            scratch_shapes=[
                pltpu.VMEM((2 * depth, tiles, TILE, LANES), jnp.float32),
                pltpu.VMEM((1, 3 * outs), jnp.float32),
            ],
        ),
        compiler_params=pltpu.CompilerParams(vmem_limit_bytes=VMEM_LIMIT),
        cost_estimate=pl.CostEstimate(
            flops=4 * rows * outs * 3 * (HW + 2 * WINDOW),
            bytes_accessed=4 * rows * positions + 4 * outs * positions + 36 * rows * outs,
            transcendentals=0,
        ),
        name="kernel_grad",
    )(place, x, other_x, own_cot, other_cot, after)


def forward_kernel(x_ref, w_ref, _, out_ref):
    step = pl.program_id(0)
    for group in range(3):

        @pl.when(step == group)
        def _(group=group):
            where = window(group)
            total = None
            for column, shift in enumerate(COLUMN_SHIFTS):
                term = lax.dot_general(
                    w_ref[column],
                    x_ref[:, where],
                    (((0,), (0,)), ((), ())),
                    preferred_element_type=jnp.float32,
                )
                if group == 1:
                    _, inside = column_mask(0, HW, shift)
                    term = moved(term, -shift)
                elif group == 0:
                    position, inside = column_mask(HW - WINDOW, WINDOW, shift)
                    inside = inside & (position >= HW - REACH)
                    term = moved(term, PAD - shift)
                else:
                    position, inside = column_mask(0, WINDOW, shift)
                    inside = inside & (position < REACH)
                    term = moved(term, -PAD - shift)
                term = jnp.where(inside, term, 0.0)
                total = term if total is None else total + term
            if group == 0:
                out_ref[:, : HW - WINDOW] = jnp.zeros((out_ref.shape[0], HW - WINDOW), jnp.float32)
                out_ref[:, HW - WINDOW :] = total
            elif group == 1:
                out_ref[...] += total
            else:
                out_ref[:, :WINDOW] += total


def forward(x, w, after):
    rows, positions = x.shape
    outs = w.shape[2]
    return pl.pallas_call(
        forward_kernel,
        out_shape=jax.ShapeDtypeStruct((outs, positions), jnp.float32),
        grid=(3,),
        in_specs=[
            pl.BlockSpec((rows, positions), lambda g: (0, 0), pipeline_mode=pl.Buffered(1)),
            pl.BlockSpec((3, rows, outs), lambda g: (g, 0, 0)),
            pl.BlockSpec(memory_space=pl.ANY),
        ],
        out_specs=pl.BlockSpec((outs, positions), lambda g: (0, 0)),
        compiler_params=pltpu.CompilerParams(vmem_limit_bytes=VMEM_LIMIT),
        cost_estimate=pl.CostEstimate(
            flops=2 * rows * outs * 3 * (HW + 2 * WINDOW),
            bytes_accessed=2 * rows * positions + 18 * rows * outs + 4 * outs * positions,
            transcendentals=0,
        ),
        name="forward",
    )(x, w, after)


def input_grad_kernel(cot_ref, w_ref, _, out_ref, middle, upper, lower):
    @pl.when(pl.program_id(0) == 0)
    def _():
        cot = cot_ref[...].astype(jnp.float32)
        for group, held in enumerate((upper, middle, lower)):
            for column, shift in enumerate(COLUMN_SHIFTS):
                held[column] = moved_cotangent(cot, group, shift)

    def products(group, held):
        total = None
        for column in range(3):
            term = jnp.dot(
                w_ref[3 * group + column], held[column], preferred_element_type=jnp.float32
            )
            total = term if total is None else total + term
        return total

    edge = HW - WINDOW
    centre = products(1, middle)
    out_ref[:, :WINDOW] = (centre[:, :WINDOW] + products(0, upper)).astype(jnp.bfloat16)
    out_ref[:, WINDOW:edge] = centre[:, WINDOW:edge].astype(jnp.bfloat16)
    out_ref[:, edge:] = (centre[:, edge:] + products(2, lower)).astype(jnp.bfloat16)


def input_gradient(cot, w, after):
    outs, positions = cot.shape
    rows = w.shape[1]
    block = min(rows, 256)
    return pl.pallas_call(
        input_grad_kernel,
        out_shape=jax.ShapeDtypeStruct((rows, positions), jnp.bfloat16),
        grid=(rows // block,),
        in_specs=[
            pl.BlockSpec((outs, positions), lambda g: (0, 0)),
            pl.BlockSpec((9, block, outs), lambda g: (0, g, 0)),
            pl.BlockSpec(memory_space=pl.ANY),
        ],
        out_specs=pl.BlockSpec((block, positions), lambda g: (g, 0)),
        scratch_shapes=[
            pltpu.VMEM((3, outs, HW), jnp.bfloat16),
            pltpu.VMEM((3, outs, WINDOW), jnp.bfloat16),
            pltpu.VMEM((3, outs, WINDOW), jnp.bfloat16),
        ],
        compiler_params=pltpu.CompilerParams(vmem_limit_bytes=VMEM_LIMIT),
        cost_estimate=pl.CostEstimate(
            flops=2 * rows * outs * 3 * (HW + 2 * WINDOW),
            bytes_accessed=2 * outs * positions + 18 * rows * outs + 2 * rows * positions,
            transcendentals=0,
        ),
        name="input_gradient",
    )(cot, w, after)


def common_exponent(values, bits):
    lowest = functools.reduce(
        jnp.minimum, [value[-1:].astype(jnp.float32) + bit for value, bit in values]
    )
    return lowest - bits


def scaled_sum(values, lowest):
    return sum(
        value.astype(jnp.float32) * jnp.exp2(lowest - value[-1:].astype(jnp.float32))
        for value, _ in values
    )


def later(value, *gates):
    for gate in gates:
        gate = gate[(0,) * (gate.ndim - 2)]
        value = jnp.where(gate.astype(jnp.float32) > -1e30, value, jnp.zeros_like(value))
    return value


def summed(values, bits, *gates):
    lowest = common_exponent(values, bits)
    total = later(scaled_sum(values, lowest), *gates).astype(jnp.float16)
    return lax.dynamic_update_slice(
        total, lowest.astype(jnp.float16), (total.shape[0] - 1, 0, 0)
    )


def token(value):
    return value[0].astype(jnp.float32)


def on_device(inputs, weight, cotangent):
    x = inputs[0]
    x_held = pltpu.with_memory_space_constraint(x, pltpu.HBM)
    own_cot = cotangent[0]
    w = jnp.transpose(weight, (1, 0, 2))
    taps, rows, outs = w.shape
    own_outs, positions = own_cot.shape
    samples = lax.axis_size("dp")
    chans = lax.axis_size("chan")
    depth = samples // 4
    place = lax.axis_index("dp")
    chan = lax.axis_index("chan")
    core, column, level = place % 2, (place // 2) % 2, place // 4
    core_rows = rows // 2
    core_tiles = core_rows // TILE
    chip_tiles = core_tiles // 2
    shard_tiles = chip_tiles // depth

    def to(value, distance):
        return lax.ppermute(value, "dp", [(i, i ^ distance) for i in range(samples)])

    def to_core(value):
        return to(value, 1)

    def to_column(value):
        return to(value, 2)

    def to_level(value, step):
        return to(value, 4 * step)

    if chans == 2:
        their_cot = lax.ppermute(own_cot, "chan", [(0, 1), (1, 0)])
        parts = (own_cot, their_cot)
        first = chan
    else:
        cot = lax.all_gather(own_cot, "chan", axis=0, tiled=True)
        parts = (cot[:LANES], cot[LANES:])
        first = 0
    other_x = to_core(lax.dynamic_slice_in_dim(x, (1 - core) * core_rows, core_rows, 0))
    where = jnp.stack([core, column * depth + level]).astype(jnp.int32)
    halves, exponents, sends, reduced, gathers = [], [], [], [], []
    bits_of_depth = [1 << shift for shift in range(depth.bit_length() - 1)]
    grad = jnp.zeros((taps, rows // TILE, 2, TILE, LANES), jnp.float16)
    after = own_cot
    for side in range(2):
        part = parts[side]
        if side == 0:
            held_part = pltpu.with_memory_space_constraint(part, pltpu.HBM)
        if side == 1:
            part = later(part, shards[0][-1:, :1, :1])
            their_cot = part
        shards = kernel_grad(
            where, depth, x_held, other_x, part if side else held_part, to_core(part), after
        )
        held = [None] * depth
        gates = ()
        for message in (1, 0):
            sent = later(shards[depth + message], *gates).astype(jnp.float16)
            came = to_column(sent)
            gates = (sent,)
            for slot in range(depth // 2 - 1, -1, -1):
                step = message * (depth // 2) + slot
                held[step] = [(shards[step], 0.0), (came[slot], 0.0)]
        after = sent[0, 0].astype(jnp.float32)
        bits = 1.0
        gates = (sends[-1],) if side else ()
        for bit in bits_of_depth:
            for step in range(depth - bit, 0, -2 * bit):
                pair = summed(held[step], bits, *gates)
                held[step ^ bit].append((to_level(pair, bit), bits))
                gates = (pair,)
                sends.append(pair)
                if side and step == depth - 1:
                    total = forward(x, w, token(pair))
                    gates += (total[:TILE, :LANES],)
            bits += 1.0
        reduced.append((held[0], bits))

    for side, (values, bits) in enumerate(reduced):
        lowest = common_exponent(values, bits)
        gates = (gathers[0][1],) if side else (sends[-1],)
        kept = later(scaled_sum(values, lowest)[:-1], *gates)
        shard = kept.astype(jnp.float16).reshape(taps, shard_tiles, 1, TILE, LANES)
        halves.append(shard)
        exponents.append(later(lowest, shard))
        near = [shard] + [None] * (depth - 1)
        for bit in bits_of_depth[::-1]:
            source = later(shard, gathers[0][0][depth // 2]) if side and bit == 1 else shard
            near[bit] = to_level(source, bit)
        for step in range(1, depth):
            if near[step] is None:
                low = step & -step
                near[step] = to_level(near[step ^ low], low)
        gathers.append((near, to_column(shard)))
        if side == 0:
            if chans == 2:
                cot = jnp.where(
                    chan == 0,
                    jnp.concatenate([own_cot, their_cot], 0),
                    jnp.concatenate([their_cot, own_cot], 0),
                )
            input_grad = input_gradient(cot, w, token(shard[0, 0]))

    for side, (near, own) in enumerate(gathers):
        steps = list(range(depth))
        cuts = [steps[1:-1], steps[-1:]]
        here = [jnp.stack([near[step] for step in cut]) for cut in cuts]
        there = [to_column(values) for values in here]
        if side == 0:
            returned = there[1]
        here, there = [near[0][None]] + here, [own[None]] + there
        pieces = [(column, step, near[step]) for step in steps]
        arrivals = [(steps[0], own)] + [
            (step, values[slot])
            for cut, values in zip(cuts, there[1:])
            for slot, step in enumerate(cut)
        ]
        pieces += [(1 - column, step, value) for step, value in arrivals]
        if side == 0:
            messages = [(pieces, jnp.concatenate(here + there))]
        else:
            messages = [
                (pieces[:-1], jnp.concatenate(here + there[:-1])),
                (pieces[-1:], there[-1]),
            ]
        lane = first if side == 0 else 1 - first
        for listed, message in messages:
            if side == 1 and message is there[-1]:
                message = later(message, crossed)
            across = to_core(message)
            crossed = across if side == 0 else crossed
            for slot, (chip, step, piece) in reversed(list(enumerate(listed))):
                row = chip * chip_tiles + (level ^ step) * shard_tiles
                for base, value in ((core, piece), (1 - core, across[slot])):
                    grad = lax.dynamic_update_slice(
                        grad, value, (0, base * core_tiles + row, lane, 0, 0)
                    )
    exponents = [jnp.where(first == side, exponents[0], exponents[1]) for side in range(2)]
    exponent = jnp.concatenate(exponents, 0)
    other = to_core(later(exponent, returned))
    by_core = [jnp.where(core == side, exponent, other) for side in range(2)]
    factor = jnp.exp2(-jnp.stack(by_core)) * (1.0 / samples)
    grad = grad.reshape(taps, 2, core_tiles, 2, TILE, LANES).astype(jnp.float32)
    grad = (grad * factor[None, :, None]).reshape(taps, rows // TILE, 2, TILE, LANES)
    weight_grad = jnp.transpose(grad, (1, 3, 0, 2, 4)).reshape(rows, taps, outs)

    if chans == 2:
        mine = lax.dynamic_slice_in_dim(total, chan * own_outs, own_outs, 0)
        theirs = lax.dynamic_slice_in_dim(total, (1 - chan) * own_outs, own_outs, 0)
        theirs = jnp.where(token(halves[1][0, 0])[0, 0] > -1e30, theirs, 0.0)
        result = mine + lax.ppermute(theirs, "chan", [(0, 1), (1, 0)])
    else:
        result = lax.psum_scatter(total, "chan", scatter_dimension=0, tiled=True)
    result = result.astype(jnp.bfloat16)[None]
    return (result, input_grad[None], weight_grad)


def solution(mesh):
    placed = (P("dp", "chan", None), P("chan", None, None), P("dp", "chan", None))
    return jax.shard_map(
        on_device,
        mesh=mesh,
        in_specs=placed,
        out_specs=(P("dp", "chan", None), P("dp", "chan", None), P("chan", None, None)),
        check_vma=False,
    )
```

```python
import functools

import jax
import jax.numpy as jnp
from jax import lax
from jax.experimental import pallas as pl
from jax.experimental.pallas import tpu as pltpu
from jax.sharding import PartitionSpec as P

DILATION_RATE = 12
MAP_HEIGHT = 16
MAP_WIDTH = 72
HW = MAP_HEIGHT * MAP_WIDTH
REACH = (MAP_HEIGHT - DILATION_RATE) * MAP_WIDTH
WINDOW = 384
PAD = WINDOW - REACH
COLUMN_SHIFTS = (-DILATION_RATE, 0, DILATION_RATE)
VMEM_LIMIT = 16 * 1024 * 1024


def column_mask(start, width, shift):
    position = lax.broadcasted_iota(jnp.int32, (1, width), 1) + start
    column = lax.rem(position, MAP_WIDTH) + shift
    return position, (column >= 0) & (column < MAP_WIDTH)


def moved(values, amount):
    amount = amount % values.shape[1]
    return values if amount == 0 else pltpu.roll(values, amount, 1)


def moved_cotangent(cot, group, shift):
    if group == 1:
        _, inside = column_mask(0, HW, -shift)
        values = moved(cot, shift)
    elif group == 0:
        position, inside = column_mask(0, WINDOW, -shift)
        inside = inside & (position < REACH)
        values = moved(cot[:, HW - WINDOW :], shift - PAD)
    else:
        position, inside = column_mask(HW - WINDOW, WINDOW, -shift)
        inside = inside & (position >= HW - REACH)
        values = moved(cot[:, :WINDOW], PAD + shift)
    return jnp.where(inside, values, 0.0).astype(jnp.bfloat16)


def window(group):
    return (slice(0, WINDOW), slice(0, HW), slice(HW - WINDOW, HW))[group]


TILE = 8
LANES = 128
TOP = 30000.0


def kernel_grad_kernel(depth, place_ref, own_x, other_x, own_cot, other_cot, _, *refs):
    near, far = refs[:depth], refs[depth : depth + 2]
    sums, peak_ref, moved_ref, centre = refs[depth + 2 :]
    step = pl.program_id(0)
    rows, width = own_x.shape[0], own_cot.shape[0]
    shards = 2 * depth
    shard_rows = rows // shards
    tiles = shard_rows // TILE
    lanes = width // LANES

    def products(cots):
        total = None
        for x_ref, cot in zip((own_x, other_x), cots):
            term = lax.dot_general(
                x_ref[...], cot, (((1,), (1,)), ((), ())), preferred_element_type=jnp.float32
            )
            total = term if total is None else total + term
        return total

    def moved_cotangents(cot_ref, group):
        cot = cot_ref[...].astype(jnp.float32)
        return jnp.concatenate(
            [moved_cotangent(cot, group, shift) for shift in COLUMN_SHIFTS], 0
        )

    def keep(group, total):
        peak_ref[...] = jnp.maximum(
            peak_ref[...], jnp.max(jnp.abs(total), axis=0, keepdims=True)
        )
        for column in range(3):
            for shard in range(shards):
                for tile in range(tiles):
                    for lane in range(lanes):
                        row = shard * shard_rows + tile * TILE
                        first = column * width + lane * LANES
                        slot = ((3 * group + column) * tiles + tile) * lanes + lane
                        sums[shard, slot] = total[row : row + TILE, first : first + LANES]

    @pl.when(step == 0)
    def _():
        peak_ref[...] = jnp.zeros(peak_ref.shape, jnp.float32)
        for sample, cot_ref in enumerate((own_cot, other_cot)):
            moved_ref[sample] = moved_cotangents(cot_ref, 1)

    for part in range(3):

        @pl.when(step == part)
        def _(part=part):
            where = slice(part * WINDOW, (part + 1) * WINDOW)
            middle = products([moved_ref[0, :, where], moved_ref[1, :, where]])
            if part == 0:
                centre[...] = middle
            elif part == 1:
                centre[...] += middle
            else:
                keep(1, centre[...] + middle)
            if part != 1:
                keep(part, products([moved_cotangents(ref, part) for ref in (own_cot, other_cot)]))

    @pl.when(step == 2)
    def _():
        peak = jnp.max(peak_ref[...], axis=1, keepdims=True)
        exponent = jnp.floor(jnp.log2(TOP / jnp.maximum(peak, 1e-30)))
        exponent = jnp.broadcast_to(exponent, (TILE, LANES))
        scale = jnp.exp2(exponent)
        count = sums.shape[1]
        for distance in range(shards):
            if distance < depth:
                out = near[distance]
            else:
                message, slot = divmod(distance - depth, depth // 2)
                out = far[message].at[slot]
            out[:count] = sums[place_ref[1] ^ distance] * scale
            out[count] = exponent


def kernel_grad(place, depth, x, other_x, own_cot, other_cot, after):
    rows, positions = other_x.shape
    outs = own_cot.shape[0]
    tiles = 9 * rows * outs // (2 * depth * TILE * LANES)
    whole = lambda g, h: (0, 0)
    once = pl.Buffered(1)
    shapes = [(tiles + 1, TILE, LANES)] * depth + [(depth // 2, tiles + 1, TILE, LANES)] * 2
    return pl.pallas_call(
        functools.partial(kernel_grad_kernel, depth),
        out_shape=[jax.ShapeDtypeStruct(shape, jnp.float32) for shape in shapes],
        grid_spec=pltpu.PrefetchScalarGridSpec(
            num_scalar_prefetch=1,
            grid=(3,),
            in_specs=[
                pl.BlockSpec((rows, WINDOW), lambda g, h: (h[0], g)),
                pl.BlockSpec((rows, WINDOW), lambda g, h: (0, g)),
                pl.BlockSpec((outs, positions), whole, pipeline_mode=once),
                pl.BlockSpec((outs, positions), whole, pipeline_mode=once),
                pl.BlockSpec(memory_space=pl.ANY),
            ],
            out_specs=[
                pl.BlockSpec(shape, functools.partial(lambda n, g, h: (0,) * n, len(shape)))
                for shape in shapes
            ],
            scratch_shapes=[
                pltpu.VMEM((2 * depth, tiles, TILE, LANES), jnp.float32),
                pltpu.VMEM((1, 3 * outs), jnp.float32),
                pltpu.VMEM((2, 3 * outs, positions), jnp.bfloat16),
                pltpu.VMEM((rows, 3 * outs), jnp.float32),
            ],
        ),
        compiler_params=pltpu.CompilerParams(vmem_limit_bytes=VMEM_LIMIT),
        cost_estimate=pl.CostEstimate(
            flops=4 * rows * outs * 3 * (HW + 2 * WINDOW),
            bytes_accessed=4 * rows * positions + 4 * outs * positions + 36 * rows * outs,
            transcendentals=0,
        ),
        name="kernel_grad",
    )(place, x, other_x, own_cot, other_cot, after)


def forward_kernel(x_ref, w_ref, _, out_ref):
    step = pl.program_id(0)
    for group in range(3):

        @pl.when(step == group)
        def _(group=group):
            where = window(group)
            total = None
            for column, shift in enumerate(COLUMN_SHIFTS):
                term = lax.dot_general(
                    w_ref[column],
                    x_ref[:, where],
                    (((0,), (0,)), ((), ())),
                    preferred_element_type=jnp.float32,
                )
                if group == 1:
                    _, inside = column_mask(0, HW, shift)
                    term = moved(term, -shift)
                elif group == 0:
                    position, inside = column_mask(HW - WINDOW, WINDOW, shift)
                    inside = inside & (position >= HW - REACH)
                    term = moved(term, PAD - shift)
                else:
                    position, inside = column_mask(0, WINDOW, shift)
                    inside = inside & (position < REACH)
                    term = moved(term, -PAD - shift)
                term = jnp.where(inside, term, 0.0)
                total = term if total is None else total + term
            if group == 0:
                out_ref[:, : HW - WINDOW] = jnp.zeros((out_ref.shape[0], HW - WINDOW), jnp.float32)
                out_ref[:, HW - WINDOW :] = total
            elif group == 1:
                out_ref[...] += total
            else:
                out_ref[:, :WINDOW] += total


def forward(x, w, after):
    rows, positions = x.shape
    outs = w.shape[2]
    return pl.pallas_call(
        forward_kernel,
        out_shape=jax.ShapeDtypeStruct((outs, positions), jnp.float32),
        grid=(3,),
        in_specs=[
            pl.BlockSpec((rows, positions), lambda g: (0, 0), pipeline_mode=pl.Buffered(1)),
            pl.BlockSpec((3, rows, outs), lambda g: (g, 0, 0)),
            pl.BlockSpec(memory_space=pl.ANY),
        ],
        out_specs=pl.BlockSpec((outs, positions), lambda g: (0, 0)),
        compiler_params=pltpu.CompilerParams(vmem_limit_bytes=VMEM_LIMIT),
        cost_estimate=pl.CostEstimate(
            flops=2 * rows * outs * 3 * (HW + 2 * WINDOW),
            bytes_accessed=2 * rows * positions + 18 * rows * outs + 4 * outs * positions,
            transcendentals=0,
        ),
        name="forward",
    )(x, w, after)


def input_grad_kernel(cot_ref, w_ref, _, out_ref, middle, upper, lower):
    @pl.when(pl.program_id(0) == 0)
    def _():
        cot = cot_ref[...].astype(jnp.float32)
        for group, held in enumerate((upper, middle, lower)):
            for column, shift in enumerate(COLUMN_SHIFTS):
                held[column] = moved_cotangent(cot, group, shift)

    def products(group, held):
        total = None
        for column in range(3):
            term = jnp.dot(
                w_ref[3 * group + column], held[column], preferred_element_type=jnp.float32
            )
            total = term if total is None else total + term
        return total

    edge = HW - WINDOW
    centre = products(1, middle)
    out_ref[:, :WINDOW] = (centre[:, :WINDOW] + products(0, upper)).astype(jnp.bfloat16)
    out_ref[:, WINDOW:edge] = centre[:, WINDOW:edge].astype(jnp.bfloat16)
    out_ref[:, edge:] = (centre[:, edge:] + products(2, lower)).astype(jnp.bfloat16)


def input_gradient(cot, w, after):
    outs, positions = cot.shape
    rows = w.shape[1]
    block = min(rows, 256)
    return pl.pallas_call(
        input_grad_kernel,
        out_shape=jax.ShapeDtypeStruct((rows, positions), jnp.bfloat16),
        grid=(rows // block,),
        in_specs=[
            pl.BlockSpec((outs, positions), lambda g: (0, 0)),
            pl.BlockSpec((9, block, outs), lambda g: (0, g, 0)),
            pl.BlockSpec(memory_space=pl.ANY),
        ],
        out_specs=pl.BlockSpec((block, positions), lambda g: (g, 0)),
        scratch_shapes=[
            pltpu.VMEM((3, outs, HW), jnp.bfloat16),
            pltpu.VMEM((3, outs, WINDOW), jnp.bfloat16),
            pltpu.VMEM((3, outs, WINDOW), jnp.bfloat16),
        ],
        compiler_params=pltpu.CompilerParams(vmem_limit_bytes=VMEM_LIMIT),
        cost_estimate=pl.CostEstimate(
            flops=2 * rows * outs * 3 * (HW + 2 * WINDOW),
            bytes_accessed=2 * outs * positions + 18 * rows * outs + 2 * rows * positions,
            transcendentals=0,
        ),
        name="input_gradient",
    )(cot, w, after)


def common_exponent(values, bits):
    lowest = functools.reduce(
        jnp.minimum, [value[-1:].astype(jnp.float32) + bit for value, bit in values]
    )
    return lowest - bits


def scaled_sum(values, lowest):
    return sum(
        value.astype(jnp.float32) * jnp.exp2(lowest - value[-1:].astype(jnp.float32))
        for value, _ in values
    )


def later(value, *gates):
    for gate in gates:
        gate = gate[(0,) * (gate.ndim - 2)]
        value = jnp.where(gate.astype(jnp.float32) > -1e30, value, jnp.zeros_like(value))
    return value


def summed(values, bits, *gates):
    lowest = common_exponent(values, bits)
    total = later(scaled_sum(values, lowest), *gates).astype(jnp.float16)
    return lax.dynamic_update_slice(
        total, lowest.astype(jnp.float16), (total.shape[0] - 1, 0, 0)
    )


def token(value):
    return value[0].astype(jnp.float32)


def on_device(inputs, weight, cotangent):
    x = inputs[0]
    x_held = pltpu.with_memory_space_constraint(x, pltpu.HBM)
    own_cot = cotangent[0]
    w = jnp.transpose(weight, (1, 0, 2))
    taps, rows, outs = w.shape
    own_outs, positions = own_cot.shape
    samples = lax.axis_size("dp")
    chans = lax.axis_size("chan")
    depth = samples // 4
    place = lax.axis_index("dp")
    chan = lax.axis_index("chan")
    core, column, level = place % 2, (place // 2) % 2, place // 4
    core_rows = rows // 2
    core_tiles = core_rows // TILE
    chip_tiles = core_tiles // 2
    shard_tiles = chip_tiles // depth

    def to(value, distance):
        return lax.ppermute(value, "dp", [(i, i ^ distance) for i in range(samples)])

    def to_core(value):
        return to(value, 1)

    def to_column(value):
        return to(value, 2)

    def to_level(value, step):
        return to(value, 4 * step)

    if chans == 2:
        their_cot = lax.ppermute(own_cot, "chan", [(0, 1), (1, 0)])
        parts = (own_cot, their_cot)
        first = chan
    else:
        cot = lax.all_gather(own_cot, "chan", axis=0, tiled=True)
        parts = (cot[:LANES], cot[LANES:])
        first = 0
    other_x = to_core(lax.dynamic_slice_in_dim(x, (1 - core) * core_rows, core_rows, 0))
    where = jnp.stack([core, column * depth + level]).astype(jnp.int32)
    halves, exponents, sends, reduced, gathers = [], [], [], [], []
    bits_of_depth = [1 << shift for shift in range(depth.bit_length() - 1)]
    grad = jnp.zeros((taps, rows // TILE, 2, TILE, LANES), jnp.float16)
    after = own_cot
    for side in range(2):
        part = parts[side]
        if side == 0:
            held_part = pltpu.with_memory_space_constraint(part, pltpu.HBM)
        if side == 1:
            part = later(part, shards[0][-1:, :1, :1])
            their_cot = part
        shards = kernel_grad(
            where, depth, x_held, other_x, part if side else held_part, to_core(part), after
        )
        held = [None] * depth
        gates = ()
        for message in (1, 0):
            sent = later(shards[depth + message], *gates).astype(jnp.float16)
            came = to_column(sent)
            gates = (sent,)
            for slot in range(depth // 2 - 1, -1, -1):
                step = message * (depth // 2) + slot
                held[step] = [(shards[step], 0.0), (came[slot], 0.0)]
        after = sent[0, 0].astype(jnp.float32)
        bits = 1.0
        gates = (sends[-1],) if side else ()
        for bit in bits_of_depth:
            for step in range(depth - bit, 0, -2 * bit):
                pair = summed(held[step], bits, *gates)
                held[step ^ bit].append((to_level(pair, bit), bits))
                gates = (pair,)
                sends.append(pair)
                if side and step == depth - 1:
                    total = forward(x, w, token(pair))
                    gates += (total[:TILE, :LANES],)
            bits += 1.0
        reduced.append((held[0], bits))

    for side, (values, bits) in enumerate(reduced):
        lowest = common_exponent(values, bits)
        gates = (gathers[0][1], input_grad[:TILE, :LANES]) if side else (sends[-1],)
        kept = later(scaled_sum(values, lowest)[:-1], *gates)
        shard = kept.astype(jnp.float16).reshape(taps, shard_tiles, 1, TILE, LANES)
        halves.append(shard)
        exponents.append(later(lowest, shard))
        near = [shard] + [None] * (depth - 1)
        for bit in bits_of_depth[::-1]:
            near[bit] = to_level(shard, bit)
        for step in range(1, depth):
            if near[step] is None:
                low = step & -step
                near[step] = to_level(near[step ^ low], low)
        gathers.append((near, to_column(shard)))
        if side == 0:
            if chans == 2:
                cot = jnp.where(
                    chan == 0,
                    jnp.concatenate([own_cot, their_cot], 0),
                    jnp.concatenate([their_cot, own_cot], 0),
                )
            input_grad = input_gradient(cot, w, token(shard[0, 0]))

    for side, (near, own) in enumerate(gathers):
        steps = list(range(depth))
        cuts = [steps[1:-1], steps[-1:]]
        here = [jnp.stack([near[step] for step in cut]) for cut in cuts]
        there = [to_column(values) for values in here]
        if side == 0:
            returned = there[1]
        here, there = [near[0][None]] + here, [own[None]] + there
        pieces = [(column, step, near[step]) for step in steps]
        arrivals = [(steps[0], own)] + [
            (step, values[slot])
            for cut, values in zip(cuts, there[1:])
            for slot, step in enumerate(cut)
        ]
        pieces += [(1 - column, step, value) for step, value in arrivals]
        if side == 0:
            messages = [(pieces, jnp.concatenate(here + there))]
        else:
            messages = [
                (pieces[:-1], jnp.concatenate(here + there[:-1])),
                (pieces[-1:], there[-1]),
            ]
        lane = first if side == 0 else 1 - first
        for listed, message in messages:
            if side == 1 and message is there[-1]:
                message = later(message, crossed)
            across = to_core(message)
            crossed = across if side == 0 else crossed
            for slot, (chip, step, piece) in enumerate(listed):
                row = chip * chip_tiles + (level ^ step) * shard_tiles
                for base, value in ((core, piece), (1 - core, across[slot])):
                    grad = lax.dynamic_update_slice(
                        grad, value, (0, base * core_tiles + row, lane, 0, 0)
                    )
    exponents = [jnp.where(first == side, exponents[0], exponents[1]) for side in range(2)]
    exponent = jnp.concatenate(exponents, 0)
    other = to_core(later(exponent, returned))
    by_core = [jnp.where(core == side, exponent, other) for side in range(2)]
    factor = jnp.exp2(-jnp.stack(by_core)) * (1.0 / samples)
    grad = grad.reshape(taps, 2, core_tiles, 2, TILE, LANES).astype(jnp.float32)
    grad = (grad * factor[None, :, None]).reshape(taps, rows // TILE, 2, TILE, LANES)
    weight_grad = jnp.transpose(grad, (1, 3, 0, 2, 4)).reshape(rows, taps, outs)

    if chans == 2:
        mine = lax.dynamic_slice_in_dim(total, chan * own_outs, own_outs, 0)
        theirs = lax.dynamic_slice_in_dim(total, (1 - chan) * own_outs, own_outs, 0)
        theirs = jnp.where(token(halves[1][0, 0])[0, 0] > -1e30, theirs, 0.0)
        result = mine + lax.ppermute(theirs, "chan", [(0, 1), (1, 0)])
    else:
        result = lax.psum_scatter(total, "chan", scatter_dimension=0, tiled=True)
    result = result.astype(jnp.bfloat16)[None]
    return (result, input_grad[None], weight_grad)


def solution(mesh):
    placed = (P("dp", "chan", None), P("chan", None, None), P("dp", "chan", None))
    return jax.shard_map(
        on_device,
        mesh=mesh,
        in_specs=placed,
        out_specs=(P("dp", "chan", None), P("dp", "chan", None), P("chan", None, None)),
        check_vma=False,
    )
```

```python
import functools

import jax
import jax.numpy as jnp
from jax import lax
from jax.experimental import pallas as pl
from jax.experimental.pallas import tpu as pltpu
from jax.sharding import PartitionSpec as P

DILATION_RATE = 12
MAP_HEIGHT = 16
MAP_WIDTH = 72
HW = MAP_HEIGHT * MAP_WIDTH
REACH = (MAP_HEIGHT - DILATION_RATE) * MAP_WIDTH
WINDOW = 384
PAD = WINDOW - REACH
COLUMN_SHIFTS = (-DILATION_RATE, 0, DILATION_RATE)
VMEM_LIMIT = 16 * 1024 * 1024


def column_mask(start, width, shift):
    position = lax.broadcasted_iota(jnp.int32, (1, width), 1) + start
    column = lax.rem(position, MAP_WIDTH) + shift
    return position, (column >= 0) & (column < MAP_WIDTH)


def moved(values, amount):
    amount = amount % values.shape[1]
    return values if amount == 0 else pltpu.roll(values, amount, 1)


def moved_cotangent(cot, group, shift):
    if group == 1:
        _, inside = column_mask(0, HW, -shift)
        values = moved(cot, shift)
    elif group == 0:
        position, inside = column_mask(0, WINDOW, -shift)
        inside = inside & (position < REACH)
        values = moved(cot[:, HW - WINDOW :], shift - PAD)
    else:
        position, inside = column_mask(HW - WINDOW, WINDOW, -shift)
        inside = inside & (position >= HW - REACH)
        values = moved(cot[:, :WINDOW], PAD + shift)
    return jnp.where(inside, values, 0.0).astype(jnp.bfloat16)


def window(group):
    return (slice(0, WINDOW), slice(0, HW), slice(HW - WINDOW, HW))[group]


TILE = 8
LANES = 128
TOP = 30000.0


def kernel_grad_kernel(depth, place_ref, own_x, other_x, own_cot, other_cot, _, *refs):
    near, far = refs[:depth], refs[depth : depth + 2]
    sums, peak_ref = refs[depth + 2 :]
    step = pl.program_id(0)
    rows, width = own_x.shape[0], own_cot.shape[0]
    shards = 2 * depth
    shard_rows = rows // shards
    tiles = shard_rows // TILE
    lanes = width // LANES

    @pl.when(step == 0)
    def _():
        peak_ref[...] = jnp.zeros(peak_ref.shape, jnp.float32)

    for group in range(3):

        @pl.when(step == group)
        def _(group=group):
            where = window(group)
            total = None
            for x_ref, cot_ref in ((own_x, own_cot), (other_x, other_cot)):
                cot = cot_ref[...].astype(jnp.float32)
                cots = [moved_cotangent(cot, group, shift) for shift in COLUMN_SHIFTS]
                term = lax.dot_general(
                    x_ref[:, where],
                    jnp.concatenate(cots, 0),
                    (((1,), (1,)), ((), ())),
                    preferred_element_type=jnp.float32,
                )
                total = term if total is None else total + term
            peak_ref[...] = jnp.maximum(
                peak_ref[...], jnp.max(jnp.abs(total), axis=0, keepdims=True)
            )
            for column in range(3):
                for shard in range(shards):
                    for tile in range(tiles):
                        for lane in range(lanes):
                            row = shard * shard_rows + tile * TILE
                            first = column * width + lane * LANES
                            slot = ((3 * group + column) * tiles + tile) * lanes + lane
                            sums[shard, slot] = total[row : row + TILE, first : first + LANES]

    @pl.when(step == 2)
    def _():
        peak = jnp.max(peak_ref[...], axis=1, keepdims=True)
        exponent = jnp.floor(jnp.log2(TOP / jnp.maximum(peak, 1e-30)))
        exponent = jnp.broadcast_to(exponent, (TILE, LANES))
        scale = jnp.exp2(exponent)
        count = sums.shape[1]
        for distance in range(shards):
            if distance < depth:
                out = near[distance]
            else:
                message, slot = divmod(distance - depth, depth // 2)
                out = far[message].at[slot]
            out[:count] = sums[place_ref[1] ^ distance] * scale
            out[count] = exponent


def kernel_grad(place, depth, x, other_x, own_cot, other_cot, after):
    rows, positions = other_x.shape
    outs = own_cot.shape[0]
    tiles = 9 * rows * outs // (2 * depth * TILE * LANES)
    whole = lambda g, h: (0, 0)
    once = pl.Buffered(1)
    shapes = [(tiles + 1, TILE, LANES)] * depth + [(depth // 2, tiles + 1, TILE, LANES)] * 2
    return pl.pallas_call(
        functools.partial(kernel_grad_kernel, depth),
        out_shape=[jax.ShapeDtypeStruct(shape, jnp.float32) for shape in shapes],
        grid_spec=pltpu.PrefetchScalarGridSpec(
            num_scalar_prefetch=1,
            grid=(3,),
            in_specs=[
                pl.BlockSpec((rows, positions), lambda g, h: (h[0], 0), pipeline_mode=once),
                pl.BlockSpec((rows, positions), whole, pipeline_mode=once),
                pl.BlockSpec((outs, positions), whole, pipeline_mode=once),
                pl.BlockSpec((outs, positions), whole, pipeline_mode=once),
                pl.BlockSpec(memory_space=pl.ANY),
            ],
            out_specs=[
                pl.BlockSpec(shape, functools.partial(lambda n, g, h: (0,) * n, len(shape)))
                for shape in shapes
            ],
            scratch_shapes=[
                pltpu.VMEM((2 * depth, tiles, TILE, LANES), jnp.float32),
                pltpu.VMEM((1, 3 * outs), jnp.float32),
            ],
        ),
        compiler_params=pltpu.CompilerParams(vmem_limit_bytes=VMEM_LIMIT),
        cost_estimate=pl.CostEstimate(
            flops=4 * rows * outs * 3 * (HW + 2 * WINDOW),
            bytes_accessed=4 * rows * positions + 4 * outs * positions + 36 * rows * outs,
            transcendentals=0,
        ),
        name="kernel_grad",
    )(place, x, other_x, own_cot, other_cot, after)


def forward_kernel(x_ref, w_ref, _, out_ref):
    step = pl.program_id(0)
    for group in range(3):

        @pl.when(step == group)
        def _(group=group):
            where = window(group)
            total = None
            for column, shift in enumerate(COLUMN_SHIFTS):
                term = lax.dot_general(
                    w_ref[column],
                    x_ref[:, where],
                    (((0,), (0,)), ((), ())),
                    preferred_element_type=jnp.float32,
                )
                if group == 1:
                    _, inside = column_mask(0, HW, shift)
                    term = moved(term, -shift)
                elif group == 0:
                    position, inside = column_mask(HW - WINDOW, WINDOW, shift)
                    inside = inside & (position >= HW - REACH)
                    term = moved(term, PAD - shift)
                else:
                    position, inside = column_mask(0, WINDOW, shift)
                    inside = inside & (position < REACH)
                    term = moved(term, -PAD - shift)
                term = jnp.where(inside, term, 0.0)
                total = term if total is None else total + term
            if group == 0:
                out_ref[:, : HW - WINDOW] = jnp.zeros((out_ref.shape[0], HW - WINDOW), jnp.float32)
                out_ref[:, HW - WINDOW :] = total
            elif group == 1:
                out_ref[...] += total
            else:
                out_ref[:, :WINDOW] += total


def forward(x, w, after):
    rows, positions = x.shape
    outs = w.shape[2]
    return pl.pallas_call(
        forward_kernel,
        out_shape=jax.ShapeDtypeStruct((outs, positions), jnp.float32),
        grid=(3,),
        in_specs=[
            pl.BlockSpec((rows, positions), lambda g: (0, 0), pipeline_mode=pl.Buffered(1)),
            pl.BlockSpec((3, rows, outs), lambda g: (g, 0, 0)),
            pl.BlockSpec(memory_space=pl.ANY),
        ],
        out_specs=pl.BlockSpec((outs, positions), lambda g: (0, 0)),
        compiler_params=pltpu.CompilerParams(vmem_limit_bytes=VMEM_LIMIT),
        cost_estimate=pl.CostEstimate(
            flops=2 * rows * outs * 3 * (HW + 2 * WINDOW),
            bytes_accessed=2 * rows * positions + 18 * rows * outs + 4 * outs * positions,
            transcendentals=0,
        ),
        name="forward",
    )(x, w, after)


def input_grad_kernel(cot_ref, w_ref, _, out_ref, middle, upper, lower):
    @pl.when(pl.program_id(0) == 0)
    def _():
        cot = cot_ref[...].astype(jnp.float32)
        for group, held in enumerate((upper, middle, lower)):
            for column, shift in enumerate(COLUMN_SHIFTS):
                held[column] = moved_cotangent(cot, group, shift)

    def products(group, held):
        total = None
        for column in range(3):
            term = jnp.dot(
                w_ref[3 * group + column], held[column], preferred_element_type=jnp.float32
            )
            total = term if total is None else total + term
        return total

    edge = HW - WINDOW
    centre = products(1, middle)
    out_ref[:, :WINDOW] = (centre[:, :WINDOW] + products(0, upper)).astype(jnp.bfloat16)
    out_ref[:, WINDOW:edge] = centre[:, WINDOW:edge].astype(jnp.bfloat16)
    out_ref[:, edge:] = (centre[:, edge:] + products(2, lower)).astype(jnp.bfloat16)


def input_gradient(cot, w, after):
    outs, positions = cot.shape
    rows = w.shape[1]
    block = min(rows, 256)
    return pl.pallas_call(
        input_grad_kernel,
        out_shape=jax.ShapeDtypeStruct((rows, positions), jnp.bfloat16),
        grid=(rows // block,),
        in_specs=[
            pl.BlockSpec((outs, positions), lambda g: (0, 0)),
            pl.BlockSpec((9, block, outs), lambda g: (0, g, 0)),
            pl.BlockSpec(memory_space=pl.ANY),
        ],
        out_specs=pl.BlockSpec((block, positions), lambda g: (g, 0)),
        scratch_shapes=[
            pltpu.VMEM((3, outs, HW), jnp.bfloat16),
            pltpu.VMEM((3, outs, WINDOW), jnp.bfloat16),
            pltpu.VMEM((3, outs, WINDOW), jnp.bfloat16),
        ],
        compiler_params=pltpu.CompilerParams(vmem_limit_bytes=VMEM_LIMIT),
        cost_estimate=pl.CostEstimate(
            flops=2 * rows * outs * 3 * (HW + 2 * WINDOW),
            bytes_accessed=2 * outs * positions + 18 * rows * outs + 2 * rows * positions,
            transcendentals=0,
        ),
        name="input_gradient",
    )(cot, w, after)


def common_exponent(values, bits):
    lowest = functools.reduce(
        jnp.minimum, [value[-1:].astype(jnp.float32) + bit for value, bit in values]
    )
    return lowest - bits


def scaled_sum(values, lowest):
    return sum(
        value.astype(jnp.float32) * jnp.exp2(lowest - value[-1:].astype(jnp.float32))
        for value, _ in values
    )


def later(value, *gates):
    for gate in gates:
        gate = gate[(0,) * (gate.ndim - 2)]
        value = jnp.where(gate.astype(jnp.float32) > -1e30, value, jnp.zeros_like(value))
    return value


def summed(values, bits, *gates):
    lowest = common_exponent(values, bits)
    total = later(scaled_sum(values, lowest), *gates).astype(jnp.float16)
    return lax.dynamic_update_slice(
        total, lowest.astype(jnp.float16), (total.shape[0] - 1, 0, 0)
    )


def token(value):
    return value[0].astype(jnp.float32)


def on_device(inputs, weight, cotangent):
    x = inputs[0]
    x_held = pltpu.with_memory_space_constraint(x, pltpu.HBM)
    own_cot = cotangent[0]
    w = jnp.transpose(weight, (1, 0, 2))
    taps, rows, outs = w.shape
    own_outs, positions = own_cot.shape
    samples = lax.axis_size("dp")
    chans = lax.axis_size("chan")
    depth = samples // 4
    place = lax.axis_index("dp")
    chan = lax.axis_index("chan")
    core, column, level = place % 2, (place // 2) % 2, place // 4
    core_rows = rows // 2
    core_tiles = core_rows // TILE
    chip_tiles = core_tiles // 2
    shard_tiles = chip_tiles // depth

    def to(value, distance):
        return lax.ppermute(value, "dp", [(i, i ^ distance) for i in range(samples)])

    def to_core(value):
        return to(value, 1)

    def to_column(value):
        return to(value, 2)

    def to_level(value, step):
        return to(value, 4 * step)

    if chans == 2:
        their_cot = lax.ppermute(own_cot, "chan", [(0, 1), (1, 0)])
        parts = (own_cot, their_cot)
        first = chan
    else:
        cot = lax.all_gather(own_cot, "chan", axis=0, tiled=True)
        parts = (cot[:LANES], cot[LANES:])
        first = 0
    other_x = to_core(lax.dynamic_slice_in_dim(x, (1 - core) * core_rows, core_rows, 0))
    where = jnp.stack([core, column * depth + level]).astype(jnp.int32)
    halves, exponents, sends, reduced, gathers = [], [], [], [], []
    bits_of_depth = [1 << shift for shift in range(depth.bit_length() - 1)]
    grad = jnp.zeros((taps, rows // TILE, 2, TILE, LANES), jnp.float16)
    after = own_cot
    for side in range(2):
        part = parts[side]
        if side == 0:
            held_part = pltpu.with_memory_space_constraint(part, pltpu.HBM)
        if side == 1:
            part = later(part, shards[0][-1:, :1, :1])
            their_cot = part
        shards = kernel_grad(
            where, depth, x_held, other_x, part if side else held_part, to_core(part), after
        )
        held = [None] * depth
        gates = ()
        for message in (1, 0):
            sent = later(shards[depth + message], *gates).astype(jnp.float16)
            came = to_column(sent)
            gates = (sent,)
            for slot in range(depth // 2 - 1, -1, -1):
                step = message * (depth // 2) + slot
                held[step] = [(shards[step], 0.0), (came[slot], 0.0)]
        after = sent[0, 0].astype(jnp.float32)
        bits = 1.0
        gates = (sends[-1],) if side else ()
        for bit in bits_of_depth:
            for step in range(depth - bit, 0, -2 * bit):
                pair = summed(held[step], bits, *gates)
                held[step ^ bit].append((to_level(pair, bit), bits))
                gates = (pair,)
                sends.append(pair)
                if side and step == depth - 1:
                    total = forward(x, w, token(pair))
                    gates += (total[:TILE, :LANES],)
            bits += 1.0
        reduced.append((held[0], bits))

    for side, (values, bits) in enumerate(reduced):
        lowest = common_exponent(values, bits)
        gates = (gathers[0][1], input_grad[:TILE, :LANES]) if side else (sends[-1],)
        kept = later(scaled_sum(values, lowest)[:-1], *gates)
        shard = kept.astype(jnp.float16).reshape(taps, shard_tiles, 1, TILE, LANES)
        halves.append(shard)
        exponents.append(later(lowest, shard))
        near = [shard] + [None] * (depth - 1)
        for bit in bits_of_depth[::-1]:
            near[bit] = to_level(shard, bit)
        for step in range(1, depth):
            if near[step] is None:
                low = step & -step
                near[step] = to_level(near[step ^ low], low)
        gathers.append((near, to_column(shard)))
        if side == 0:
            if chans == 2:
                cot = jnp.where(
                    chan == 0,
                    jnp.concatenate([own_cot, their_cot], 0),
                    jnp.concatenate([their_cot, own_cot], 0),
                )
            input_grad = input_gradient(cot, w, token(shard[0, 0]))

    for side, (near, own) in enumerate(gathers):
        steps = list(range(depth))
        cuts = [steps[1:-1], steps[-1:]]
        here = [jnp.stack([near[step] for step in cut]) for cut in cuts]
        there = [to_column(values) for values in here]
        if side == 0:
            returned = there[1]
        here, there = [near[0][None]] + here, [own[None]] + there
        pieces = [(column, step, near[step]) for step in steps]
        arrivals = [(steps[0], own)] + [
            (step, values[slot])
            for cut, values in zip(cuts, there[1:])
            for slot, step in enumerate(cut)
        ]
        pieces += [(1 - column, step, value) for step, value in arrivals]
        if side == 0:
            messages = [(pieces, jnp.concatenate(here + there))]
        else:
            messages = [
                (pieces[:-1], jnp.concatenate(here + there[:-1])),
                (pieces[-1:], there[-1]),
            ]
        lane = first if side == 0 else 1 - first
        for listed, message in messages:
            if side == 1 and message is there[-1]:
                message = later(message, crossed)
            across = to_core(message)
            crossed = across if side == 0 else crossed
            for slot, (chip, step, piece) in reversed(list(enumerate(listed))):
                row = chip * chip_tiles + (level ^ step) * shard_tiles
                for base, value in ((core, piece), (1 - core, across[slot])):
                    grad = lax.dynamic_update_slice(
                        grad, value, (0, base * core_tiles + row, lane, 0, 0)
                    )
    exponents = [jnp.where(first == side, exponents[0], exponents[1]) for side in range(2)]
    exponent = jnp.concatenate(exponents, 0)
    other = to_core(later(exponent, returned))
    by_core = [jnp.where(core == side, exponent, other) for side in range(2)]
    factor = jnp.exp2(-jnp.stack(by_core)) * (1.0 / samples)
    grad = grad.reshape(taps, 2, core_tiles, 2, TILE, LANES).astype(jnp.float32)
    grad = (grad * factor[None, :, None]).reshape(taps, rows // TILE, 2, TILE, LANES)
    weight_grad = jnp.transpose(grad, (1, 3, 0, 2, 4)).reshape(rows, taps, outs)

    if chans == 2:
        mine = lax.dynamic_slice_in_dim(total, chan * own_outs, own_outs, 0)
        theirs = lax.dynamic_slice_in_dim(total, (1 - chan) * own_outs, own_outs, 0)
        theirs = jnp.where(token(halves[1][0, 0])[0, 0] > -1e30, theirs, 0.0)
        result = mine + lax.ppermute(theirs, "chan", [(0, 1), (1, 0)])
    else:
        result = lax.psum_scatter(total, "chan", scatter_dimension=0, tiled=True)
    result = result.astype(jnp.bfloat16)[None]
    return (result, input_grad[None], weight_grad)


def solution(mesh):
    placed = (P("dp", "chan", None), P("chan", None, None), P("dp", "chan", None))
    return jax.shard_map(
        on_device,
        mesh=mesh,
        in_specs=placed,
        out_specs=(P("dp", "chan", None), P("dp", "chan", None), P("chan", None, None)),
        check_vma=False,
    )
```

```python
import functools

import jax
import jax.numpy as jnp
from jax import lax
from jax.experimental import pallas as pl
from jax.experimental.pallas import tpu as pltpu
from jax.sharding import PartitionSpec as P

DILATION_RATE = 12
MAP_HEIGHT = 16
MAP_WIDTH = 72
HW = MAP_HEIGHT * MAP_WIDTH
REACH = (MAP_HEIGHT - DILATION_RATE) * MAP_WIDTH
WINDOW = 384
PAD = WINDOW - REACH
COLUMN_SHIFTS = (-DILATION_RATE, 0, DILATION_RATE)
VMEM_LIMIT = 16 * 1024 * 1024


def column_mask(start, width, shift):
    position = lax.broadcasted_iota(jnp.int32, (1, width), 1) + start
    column = lax.rem(position, MAP_WIDTH) + shift
    return position, (column >= 0) & (column < MAP_WIDTH)


def moved(values, amount):
    amount = amount % values.shape[1]
    return values if amount == 0 else pltpu.roll(values, amount, 1)


def moved_cotangent(cot, group, shift):
    if group == 1:
        _, inside = column_mask(0, HW, -shift)
        values = moved(cot, shift)
    elif group == 0:
        position, inside = column_mask(0, WINDOW, -shift)
        inside = inside & (position < REACH)
        values = moved(cot[:, HW - WINDOW :], shift - PAD)
    else:
        position, inside = column_mask(HW - WINDOW, WINDOW, -shift)
        inside = inside & (position >= HW - REACH)
        values = moved(cot[:, :WINDOW], PAD + shift)
    return jnp.where(inside, values, 0.0).astype(jnp.bfloat16)


def window(group):
    return (slice(0, WINDOW), slice(0, HW), slice(HW - WINDOW, HW))[group]


TILE = 8
LANES = 128
TOP = 30000.0


def kernel_grad_kernel(depth, place_ref, own_x, other_x, own_cot, other_cot, _, *refs):
    near, far = refs[:depth], refs[depth : depth + 2]
    sums, peak_ref = refs[depth + 2 :]
    step = pl.program_id(0)
    rows, width = own_x.shape[0], own_cot.shape[0]
    shards = 2 * depth
    shard_rows = rows // shards
    tiles = shard_rows // TILE
    lanes = width // LANES

    @pl.when(step == 0)
    def _():
        peak_ref[...] = jnp.zeros(peak_ref.shape, jnp.float32)

    for group in range(3):

        @pl.when(step == group)
        def _(group=group):
            where = window(group)
            total = None
            for x_ref, cot_ref in ((own_x, own_cot), (other_x, other_cot)):
                cot = cot_ref[...].astype(jnp.float32)
                cots = [moved_cotangent(cot, group, shift) for shift in COLUMN_SHIFTS]
                term = lax.dot_general(
                    x_ref[:, where],
                    jnp.concatenate(cots, 0),
                    (((1,), (1,)), ((), ())),
                    preferred_element_type=jnp.float32,
                )
                total = term if total is None else total + term
            peak_ref[...] = jnp.maximum(
                peak_ref[...], jnp.max(jnp.abs(total), axis=0, keepdims=True)
            )
            for column in range(3):
                for shard in range(shards):
                    for tile in range(tiles):
                        for lane in range(lanes):
                            row = shard * shard_rows + tile * TILE
                            first = column * width + lane * LANES
                            slot = ((3 * group + column) * tiles + tile) * lanes + lane
                            sums[shard, slot] = total[row : row + TILE, first : first + LANES]

    @pl.when(step == 2)
    def _():
        peak = jnp.max(peak_ref[...], axis=1, keepdims=True)
        exponent = jnp.floor(jnp.log2(TOP / jnp.maximum(peak, 1e-30)))
        exponent = jnp.broadcast_to(exponent, (TILE, LANES))
        scale = jnp.exp2(exponent)
        count = sums.shape[1]
        for distance in range(shards):
            if distance < depth:
                out = near[distance]
            else:
                message, slot = divmod(distance - depth, depth // 2)
                out = far[message].at[slot]
            out[:count] = sums[place_ref[1] ^ distance] * scale
            out[count] = exponent


def kernel_grad(place, depth, x, other_x, own_cot, other_cot, after):
    rows, positions = other_x.shape
    outs = own_cot.shape[0]
    tiles = 9 * rows * outs // (2 * depth * TILE * LANES)
    whole = lambda g, h: (0, 0)
    once = pl.Buffered(1)
    shapes = [(tiles + 1, TILE, LANES)] * depth + [(depth // 2, tiles + 1, TILE, LANES)] * 2
    return pl.pallas_call(
        functools.partial(kernel_grad_kernel, depth),
        out_shape=[jax.ShapeDtypeStruct(shape, jnp.float32) for shape in shapes],
        grid_spec=pltpu.PrefetchScalarGridSpec(
            num_scalar_prefetch=1,
            grid=(3,),
            in_specs=[
                pl.BlockSpec((rows, positions), lambda g, h: (h[0], 0), pipeline_mode=once),
                pl.BlockSpec((rows, positions), whole, pipeline_mode=once),
                pl.BlockSpec((outs, positions), whole, pipeline_mode=once),
                pl.BlockSpec((outs, positions), whole, pipeline_mode=once),
                pl.BlockSpec(memory_space=pl.ANY),
            ],
            out_specs=[
                pl.BlockSpec(shape, functools.partial(lambda n, g, h: (0,) * n, len(shape)))
                for shape in shapes
            ],
            scratch_shapes=[
                pltpu.VMEM((2 * depth, tiles, TILE, LANES), jnp.float32),
                pltpu.VMEM((1, 3 * outs), jnp.float32),
            ],
        ),
        compiler_params=pltpu.CompilerParams(vmem_limit_bytes=VMEM_LIMIT),
        cost_estimate=pl.CostEstimate(
            flops=4 * rows * outs * 3 * (HW + 2 * WINDOW),
            bytes_accessed=4 * rows * positions + 4 * outs * positions + 36 * rows * outs,
            transcendentals=0,
        ),
        name="kernel_grad",
    )(place, x, other_x, own_cot, other_cot, after)


def forward_kernel(x_ref, w_ref, _, out_ref):
    step = pl.program_id(0)
    for group in range(3):

        @pl.when(step == group)
        def _(group=group):
            where = window(group)
            total = None
            for column, shift in enumerate(COLUMN_SHIFTS):
                term = lax.dot_general(
                    w_ref[column],
                    x_ref[:, where],
                    (((0,), (0,)), ((), ())),
                    preferred_element_type=jnp.float32,
                )
                if group == 1:
                    _, inside = column_mask(0, HW, shift)
                    term = moved(term, -shift)
                elif group == 0:
                    position, inside = column_mask(HW - WINDOW, WINDOW, shift)
                    inside = inside & (position >= HW - REACH)
                    term = moved(term, PAD - shift)
                else:
                    position, inside = column_mask(0, WINDOW, shift)
                    inside = inside & (position < REACH)
                    term = moved(term, -PAD - shift)
                term = jnp.where(inside, term, 0.0)
                total = term if total is None else total + term
            if group == 0:
                out_ref[:, : HW - WINDOW] = jnp.zeros((out_ref.shape[0], HW - WINDOW), jnp.float32)
                out_ref[:, HW - WINDOW :] = total
            elif group == 1:
                out_ref[...] += total
            else:
                out_ref[:, :WINDOW] += total


def forward(x, w, after):
    rows, positions = x.shape
    outs = w.shape[2]
    return pl.pallas_call(
        forward_kernel,
        out_shape=jax.ShapeDtypeStruct((outs, positions), jnp.float32),
        grid=(3,),
        in_specs=[
            pl.BlockSpec((rows, positions), lambda g: (0, 0), pipeline_mode=pl.Buffered(1)),
            pl.BlockSpec((3, rows, outs), lambda g: (g, 0, 0)),
            pl.BlockSpec(memory_space=pl.ANY),
        ],
        out_specs=pl.BlockSpec((outs, positions), lambda g: (0, 0)),
        compiler_params=pltpu.CompilerParams(vmem_limit_bytes=VMEM_LIMIT),
        cost_estimate=pl.CostEstimate(
            flops=2 * rows * outs * 3 * (HW + 2 * WINDOW),
            bytes_accessed=2 * rows * positions + 18 * rows * outs + 4 * outs * positions,
            transcendentals=0,
        ),
        name="forward",
    )(x, w, after)


def input_grad_kernel(cot_ref, w_ref, _, out_ref, middle, upper, lower):
    @pl.when(pl.program_id(0) == 0)
    def _():
        cot = cot_ref[...].astype(jnp.float32)
        for group, held in enumerate((upper, middle, lower)):
            for column, shift in enumerate(COLUMN_SHIFTS):
                held[column] = moved_cotangent(cot, group, shift)

    def products(group, held):
        total = None
        for column in range(3):
            term = jnp.dot(
                w_ref[3 * group + column], held[column], preferred_element_type=jnp.float32
            )
            total = term if total is None else total + term
        return total

    edge = HW - WINDOW
    centre = products(1, middle)
    out_ref[:, :WINDOW] = (centre[:, :WINDOW] + products(0, upper)).astype(jnp.bfloat16)
    out_ref[:, WINDOW:edge] = centre[:, WINDOW:edge].astype(jnp.bfloat16)
    out_ref[:, edge:] = (centre[:, edge:] + products(2, lower)).astype(jnp.bfloat16)


def input_gradient(cot, w, after):
    outs, positions = cot.shape
    rows = w.shape[1]
    block = min(rows, 256)
    return pl.pallas_call(
        input_grad_kernel,
        out_shape=jax.ShapeDtypeStruct((rows, positions), jnp.bfloat16),
        grid=(rows // block,),
        in_specs=[
            pl.BlockSpec((outs, positions), lambda g: (0, 0)),
            pl.BlockSpec((9, block, outs), lambda g: (0, g, 0)),
            pl.BlockSpec(memory_space=pl.ANY),
        ],
        out_specs=pl.BlockSpec((block, positions), lambda g: (g, 0)),
        scratch_shapes=[
            pltpu.VMEM((3, outs, HW), jnp.bfloat16),
            pltpu.VMEM((3, outs, WINDOW), jnp.bfloat16),
            pltpu.VMEM((3, outs, WINDOW), jnp.bfloat16),
        ],
        compiler_params=pltpu.CompilerParams(vmem_limit_bytes=VMEM_LIMIT),
        cost_estimate=pl.CostEstimate(
            flops=2 * rows * outs * 3 * (HW + 2 * WINDOW),
            bytes_accessed=2 * outs * positions + 18 * rows * outs + 2 * rows * positions,
            transcendentals=0,
        ),
        name="input_gradient",
    )(cot, w, after)


def common_exponent(values, bits):
    lowest = functools.reduce(
        jnp.minimum, [value[-1:].astype(jnp.float32) + bit for value, bit in values]
    )
    return lowest - bits


def scaled_sum(values, lowest):
    return sum(
        value.astype(jnp.float32) * jnp.exp2(lowest - value[-1:].astype(jnp.float32))
        for value, _ in values
    )


def later(value, *gates):
    for gate in gates:
        gate = gate[(0,) * (gate.ndim - 2)]
        value = jnp.where(gate.astype(jnp.float32) > -1e30, value, jnp.zeros_like(value))
    return value


def summed(values, bits, *gates):
    lowest = common_exponent(values, bits)
    total = later(scaled_sum(values, lowest), *gates).astype(jnp.float16)
    return lax.dynamic_update_slice(
        total, lowest.astype(jnp.float16), (total.shape[0] - 1, 0, 0)
    )


def token(value):
    return value[0].astype(jnp.float32)


def on_device(inputs, weight, cotangent):
    x = inputs[0]
    x_held = pltpu.with_memory_space_constraint(x, pltpu.HBM)
    own_cot = cotangent[0]
    w = jnp.transpose(weight, (1, 0, 2))
    taps, rows, outs = w.shape
    own_outs, positions = own_cot.shape
    samples = lax.axis_size("dp")
    chans = lax.axis_size("chan")
    depth = samples // 4
    place = lax.axis_index("dp")
    chan = lax.axis_index("chan")
    core, column, level = place % 2, (place // 2) % 2, place // 4
    core_rows = rows // 2
    core_tiles = core_rows // TILE
    chip_tiles = core_tiles // 2
    shard_tiles = chip_tiles // depth

    def to(value, distance):
        return lax.ppermute(value, "dp", [(i, i ^ distance) for i in range(samples)])

    def to_core(value):
        return to(value, 1)

    def to_column(value):
        return to(value, 2)

    def to_level(value, step):
        return to(value, 4 * step)

    if chans == 2:
        their_cot = lax.ppermute(own_cot, "chan", [(0, 1), (1, 0)])
        parts = (own_cot, their_cot)
        first = chan
    else:
        cot = lax.all_gather(own_cot, "chan", axis=0, tiled=True)
        parts = (cot[:LANES], cot[LANES:])
        first = 0
    other_x = to_core(lax.dynamic_slice_in_dim(x, (1 - core) * core_rows, core_rows, 0))
    where = jnp.stack([core, column * depth + level]).astype(jnp.int32)
    halves, exponents, sends, reduced, gathers = [], [], [], [], []
    bits_of_depth = [1 << shift for shift in range(depth.bit_length() - 1)]
    grad = jnp.zeros((taps, rows // TILE, 2, TILE, LANES), jnp.float16)
    after = own_cot
    for side in range(2):
        part = parts[side]
        if side == 0:
            held_part = pltpu.with_memory_space_constraint(part, pltpu.HBM)
        if side == 1:
            part = later(part, shards[0][-1:, :1, :1])
            their_cot = part
        shards = kernel_grad(
            where, depth, x_held, other_x, part if side else held_part, to_core(part), after
        )
        held = [None] * depth
        gates = ()
        for message in (1, 0):
            sent = later(shards[depth + message], *gates).astype(jnp.float16)
            came = to_column(sent)
            gates = (sent,)
            for slot in range(depth // 2 - 1, -1, -1):
                step = message * (depth // 2) + slot
                held[step] = [(shards[step], 0.0), (came[slot], 0.0)]
        after = sent[0, 0].astype(jnp.float32)
        bits = 1.0
        gates = (sends[-1],) if side else ()
        for bit in bits_of_depth:
            for step in range(depth - bit, 0, -2 * bit):
                pair = summed(held[step], bits, *gates)
                held[step ^ bit].append((to_level(pair, bit), bits))
                gates = (pair,)
                sends.append(pair)
                if side and step == depth - 1:
                    total = forward(x, w, token(pair))
                    gates += (total[:TILE, :LANES],)
            bits += 1.0
        reduced.append((held[0], bits))

    for side, (values, bits) in enumerate(reduced):
        lowest = common_exponent(values, bits)
        gates = (gathers[0][1],) if side else (sends[-1],)
        kept = later(scaled_sum(values, lowest)[:-1], *gates)
        shard = kept.astype(jnp.float16).reshape(taps, shard_tiles, 1, TILE, LANES)
        halves.append(shard)
        exponents.append(later(lowest, shard))
        near = [shard] + [None] * (depth - 1)
        for bit in bits_of_depth[::-1]:
            near[bit] = to_level(shard, bit)
        gathers.append((near, to_column(shard)))
        if side == 0:
            if chans == 2:
                cot = jnp.where(
                    chan == 0,
                    jnp.concatenate([own_cot, their_cot], 0),
                    jnp.concatenate([their_cot, own_cot], 0),
                )
            input_grad = input_gradient(cot, w, token(shard[0, 0]))

    for side, (near, own) in enumerate(gathers):
        for step in range(1, depth):
            if near[step] is None:
                low = step & -step
                source = near[step ^ low] if side else later(near[step ^ low], halves[1])
                near[step] = to_level(source, low)
        steps = list(range(depth))
        cuts = [steps[1:-1], steps[-1:]]
        here = [jnp.stack([near[step] for step in cut]) for cut in cuts]
        if side == 0:
            here[0] = later(here[0], halves[1])
        there = [to_column(values) for values in here]
        if side == 0:
            returned = there[1]
        here, there = [near[0][None]] + here, [own[None]] + there
        pieces = [(column, step, near[step]) for step in steps]
        arrivals = [(steps[0], own)] + [
            (step, values[slot])
            for cut, values in zip(cuts, there[1:])
            for slot, step in enumerate(cut)
        ]
        pieces += [(1 - column, step, value) for step, value in arrivals]
        if side == 0:
            messages = [(pieces, jnp.concatenate(here + there))]
        else:
            messages = [
                (pieces[:-1], jnp.concatenate(here + there[:-1])),
                (pieces[-1:], there[-1]),
            ]
        lane = first if side == 0 else 1 - first
        for listed, message in messages:
            if side == 1 and message is there[-1]:
                message = later(message, crossed)
            across = to_core(message)
            crossed = across if side == 0 else crossed
            for slot, (chip, step, piece) in reversed(list(enumerate(listed))):
                row = chip * chip_tiles + (level ^ step) * shard_tiles
                for base, value in ((core, piece), (1 - core, across[slot])):
                    grad = lax.dynamic_update_slice(
                        grad, value, (0, base * core_tiles + row, lane, 0, 0)
                    )
    exponents = [jnp.where(first == side, exponents[0], exponents[1]) for side in range(2)]
    exponent = jnp.concatenate(exponents, 0)
    other = to_core(later(exponent, returned))
    by_core = [jnp.where(core == side, exponent, other) for side in range(2)]
    factor = jnp.exp2(-jnp.stack(by_core)) * (1.0 / samples)
    grad = grad.reshape(taps, 2, core_tiles, 2, TILE, LANES).astype(jnp.float32)
    grad = (grad * factor[None, :, None]).reshape(taps, rows // TILE, 2, TILE, LANES)
    weight_grad = jnp.transpose(grad, (1, 3, 0, 2, 4)).reshape(rows, taps, outs)

    if chans == 2:
        mine = lax.dynamic_slice_in_dim(total, chan * own_outs, own_outs, 0)
        theirs = lax.dynamic_slice_in_dim(total, (1 - chan) * own_outs, own_outs, 0)
        theirs = jnp.where(token(halves[1][0, 0])[0, 0] > -1e30, theirs, 0.0)
        result = mine + lax.ppermute(theirs, "chan", [(0, 1), (1, 0)])
    else:
        result = lax.psum_scatter(total, "chan", scatter_dimension=0, tiled=True)
    result = result.astype(jnp.bfloat16)[None]
    return (result, input_grad[None], weight_grad)


def solution(mesh):
    placed = (P("dp", "chan", None), P("chan", None, None), P("dp", "chan", None))
    return jax.shard_map(
        on_device,
        mesh=mesh,
        in_specs=placed,
        out_specs=(P("dp", "chan", None), P("dp", "chan", None), P("chan", None, None)),
        check_vma=False,
    )
```
